32 devices in a mesh: dp: 8 (over z, y), seq: 4 (over x, core).
Axes of the slice: x: 2, y: 2, z: 4, core: 2. Of those that a mesh axis runs over, the one named last changes fastest.
Arguments:
- tokens: bfloat16 [96, 256, 768], P('dp', 'seq'), may hold values from -6 to 6
- masks: int32 [96, 256], P('dp', 'seq'), may hold values from 0 to 1, as said below
- cotangent: bfloat16 [96, 256, 768], P('dp', 'seq'), may hold values from -6 to 6
- w_qkv: bfloat16 [768, 2304], P('dp'), may hold values from -0.21875 to 0.21875
- w_out: bfloat16 [768, 768], P('dp'), may hold values from -0.875 to 0.875
- w_fc1: bfloat16 [768, 3072], P('dp'), may hold values from -0.21875 to 0.21875
- w_fc2: bfloat16 [3072, 768], P('dp'), may hold values from -0.109375 to 0.109375
- vectors: bfloat16 [768, 15], P('dp'), as said below
- master_qkv: float32 [768, 2304], P('dp'), may hold values from -0.21875 to 0.21875
- master_out: float32 [768, 768], P('dp'), may hold values from -0.875 to 0.875
- master_fc1: float32 [768, 3072], P('dp'), may hold values from -0.21875 to 0.21875
- master_fc2: float32 [3072, 768], P('dp'), may hold values from -0.109375 to 0.109375
- master_vectors: float32 [768, 15], P('dp')
- moment_qkv: float32 [768, 2304], P('dp'), may hold values from -160 to 160
- moment_out: float32 [768, 768], P('dp'), may hold values from -160 to 160
- moment_fc1: float32 [768, 3072], P('dp'), may hold values from -160 to 160
- moment_fc2: float32 [3072, 768], P('dp'), may hold values from -160 to 160
- moment_vectors: float32 [768, 15], P('dp'), may hold values from -512 to 512
- teacher_qkv: float32 [768, 2304], P('dp'), may hold values from -0.21875 to 0.21875
- teacher_out: float32 [768, 768], P('dp'), may hold values from -0.875 to 0.875
- teacher_fc1: float32 [768, 3072], P('dp'), may hold values from -0.21875 to 0.21875
- teacher_fc2: float32 [3072, 768], P('dp'), may hold values from -0.109375 to 0.109375
- teacher_vectors: float32 [768, 15], P('dp')
Outputs:
- output: bfloat16 [96, 256, 768], P('dp', 'seq')
- input_grad: float32 [96, 256, 768], P('dp', 'seq')
- grad_qkv: float32 [768, 2304], P('dp')
- grad_out: float32 [768, 768], P('dp')
- grad_fc1: float32 [768, 3072], P('dp')
- grad_fc2: float32 [3072, 768], P('dp')
- grad_vectors: float32 [768, 15], P('dp')
- new_qkv: float32 [768, 2304], P('dp')
- new_out: float32 [768, 768], P('dp')
- new_fc1: float32 [768, 3072], P('dp')
- new_fc2: float32 [3072, 768], P('dp')
- new_vectors: float32 [768, 15], P('dp')
- next_moment_qkv: float32 [768, 2304], P('dp')
- next_moment_out: float32 [768, 768], P('dp')
- next_moment_fc1: float32 [768, 3072], P('dp')
- next_moment_fc2: float32 [3072, 768], P('dp')
- next_moment_vectors: float32 [768, 15], P('dp')
- next_teacher_qkv: float32 [768, 2304], P('dp')
- next_teacher_out: float32 [768, 768], P('dp')
- next_teacher_fc1: float32 [768, 3072], P('dp')
- next_teacher_fc2: float32 [3072, 768], P('dp')
- next_teacher_vectors: float32 [768, 15], P('dp')
- copy_qkv: bfloat16 [768, 2304], P('dp')
- copy_out: bfloat16 [768, 768], P('dp')
- copy_fc1: bfloat16 [768, 3072], P('dp')
- copy_fc2: bfloat16 [3072, 768], P('dp')
- copy_vectors: bfloat16 [768, 15], P('dp')
The draws below stay inside these ranges and needn't reach their ends.
Inputs may be any that keep to these rules, and one draw needn't show every extreme that they name: `masks`: in each image a share of the 14 x 14 patches drawn between 40 and 80 percent is masked; the class row and padding slots are never masked. `vectors`: gains and layer scales (columns 0, 5, 6, 13) lie between 0.6 and 1.4.
All inputs are finite; a program needn't handle non-finite values.
Results may differ from the reference program's by a relative error of at most 0.018.
Values may be sent and summed in bfloat16 or wider, within the bound.
A program may use at most 256 MiB of HBM per device.

```python
import math
import jax
import jax.numpy as jnp
from jax import lax

D = 768
HEADS = 12
HEAD_DIM = 64
FF = 3072
NVEC = 15
GRID = 14
BAND = 4
SLOTS = 64
IMAGES = 96
SEQLEN = 256


def vector_law(key, salt):
    key = jax.random.fold_in(key, salt)
    first_key, second_key = jax.random.split(key)
    column = jnp.arange(NVEC)[None, :]
    gains = (column == 0) | (column == 5) | (column == 6) | (column == 13)
    token_column = column == 14
    spread = jnp.where(token_column, 1.0, 0.3)
    normal_part = jax.random.normal(first_key, (D, NVEC), jnp.float32) * spread
    gain_part = jax.random.uniform(second_key, (D, NVEC), jnp.float32, 0.6, 1.4)
    return jnp.where(gains, gain_part, normal_part)


def draw_vectors(key, part):
    return vector_law(key, 11).astype(jnp.bfloat16)


def draw_master_vectors(key, part):
    return vector_law(key, 12)


def draw_teacher_vectors(key, part):
    return vector_law(key, 13)


def draw_masks(key, part):
    patches = GRID * GRID

    def one_image(image_key):
        count_key, order_key = jax.random.split(image_key)
        chosen = jax.random.randint(count_key, (), (2 * patches + 4) // 5, 4 * patches // 5 + 1)
        order = jax.random.permutation(order_key, patches)
        ranking = jnp.argsort(order)
        position = jnp.arange(SEQLEN, dtype=jnp.int32)
        block_index = position // SLOTS
        inner_slot = position % SLOTS
        grid_row = BAND * block_index + inner_slot // GRID
        is_patch = (inner_slot < BAND * GRID) & (grid_row < GRID)
        patch_index = jnp.where(is_patch, grid_row * GRID + inner_slot % GRID, 0)
        return (is_patch & (ranking[patch_index] < chosen)).astype(jnp.int32)
    return jax.vmap(one_image)(jax.random.split(jax.random.fold_in(key, 21), IMAGES))


def level_of(own_key, shape, shards, low, high):
    factor_of = 1.0
    for axis_at, blocks in shards:
        draws = jax.random.uniform(jax.random.fold_in(jax.random.fold_in(own_key, 6), axis_at), (blocks,), jnp.float32, low / len(shards), high / len(shards))
        factor_of = factor_of * jnp.repeat(jnp.exp(draws), shape[axis_at] // blocks).reshape((-1,) + (1,) * (len(shape) - 1 - axis_at))
    return factor_of


def noise(key, extent, width, reach, cuts=(), held_as=jnp.bfloat16):
    loudness = level_of(key, extent, cuts, -0.22, 0.18) if cuts else 1.0
    drawn = jax.random.normal(key, extent, jnp.float32) * width * loudness
    return jnp.minimum(jnp.maximum(drawn, -reach), reach).astype(held_as)


def setup_inputs(seed: int = 0) -> dict:
    key_list = jax.random.split(jax.random.key(seed), 24)
    tokens = noise(key_list[0], (IMAGES, SEQLEN, D), 1.0, 6.0, ((0, 8), (1, 4)))
    masks = draw_masks(jax.random.fold_in(key_list[23], 71), 0)
    cotangent = noise(key_list[2], (IMAGES, SEQLEN, D), 1.0, 6.0, ((0, 8), (1, 4)))
    w_qkv = noise(key_list[3], (D, 3 * D), D ** -0.5, 0.21875, ((0, 8),))
    w_out = noise(key_list[4], (D, D), (D // 16) ** -0.5, 0.875, ((0, 8),))
    w_fc1 = noise(key_list[5], (D, FF), D ** -0.5, 0.21875, ((0, 8),))
    w_fc2 = noise(key_list[6], (FF, D), FF ** -0.5, 0.109375, ((0, 8),))
    vectors = draw_vectors(jax.random.fold_in(key_list[23], 71), 0)
    master_qkv = noise(key_list[8], (D, 3 * D), D ** -0.5, 0.21875, ((0, 8),), jnp.float32)
    master_out = noise(key_list[9], (D, D), (D // 16) ** -0.5, 0.875, ((0, 8),), jnp.float32)
    master_fc1 = noise(key_list[10], (D, FF), D ** -0.5, 0.21875, ((0, 8),), jnp.float32)
    master_fc2 = noise(key_list[11], (FF, D), FF ** -0.5, 0.109375, ((0, 8),), jnp.float32)
    master_vectors = draw_master_vectors(jax.random.fold_in(key_list[23], 71), 0)
    moment_qkv = noise(key_list[13], (D, 3 * D), (3 * IMAGES ** 0.5), 160.0, ((0, 8),), jnp.float32)
    moment_out = noise(key_list[14], (D, D), (3 * IMAGES ** 0.5), 160.0, ((0, 8),), jnp.float32)
    moment_fc1 = noise(key_list[15], (D, FF), (3 * IMAGES ** 0.5), 160.0, ((0, 8),), jnp.float32)
    moment_fc2 = noise(key_list[16], (FF, D), (3 * IMAGES ** 0.5), 160.0, ((0, 8),), jnp.float32)
    moment_vectors = noise(key_list[17], (D, NVEC), (10 * IMAGES ** 0.5), 512.0, ((0, 8),), jnp.float32)
    teacher_qkv = noise(key_list[18], (D, 3 * D), D ** -0.5, 0.21875, ((0, 8),), jnp.float32)
    teacher_out = noise(key_list[19], (D, D), (D // 16) ** -0.5, 0.875, ((0, 8),), jnp.float32)
    teacher_fc1 = noise(key_list[20], (D, FF), D ** -0.5, 0.21875, ((0, 8),), jnp.float32)
    teacher_fc2 = noise(key_list[21], (FF, D), FF ** -0.5, 0.109375, ((0, 8),), jnp.float32)
    teacher_vectors = draw_teacher_vectors(jax.random.fold_in(key_list[23], 71), 0)
    return dict(tokens=tokens, masks=masks, cotangent=cotangent, w_qkv=w_qkv, w_out=w_out, w_fc1=w_fc1, w_fc2=w_fc2, vectors=vectors, master_qkv=master_qkv, master_out=master_out, master_fc1=master_fc1, master_fc2=master_fc2, master_vectors=master_vectors, moment_qkv=moment_qkv, moment_out=moment_out, moment_fc1=moment_fc1, moment_fc2=moment_fc2, moment_vectors=moment_vectors, teacher_qkv=teacher_qkv, teacher_out=teacher_out, teacher_fc1=teacher_fc1, teacher_fc2=teacher_fc2, teacher_vectors=teacher_vectors)


@jax.custom_vjp
def low(v):
    return lax.optimization_barrier(v.astype(jnp.bfloat16)).astype(jnp.float32)

@jax.custom_vjp
def low_back(v):
    return v

def low_keep(v):
    return (low(v), None)

def low_pass(kept, grad):
    return (grad,)

def back_keep(v):
    return (v, None)

def back_low(kept, grad):
    return (low(grad),)
low.defvjp(low_keep, low_pass)
low_back.defvjp(back_keep, back_low)
highest = lax.Precision.HIGHEST
momentum_rate = 0.9
teacher_rate = 0.75
matrix_rate = 0.003
vector_rate = 0.03
matrix_decay = 0.05

def layer_norm(inputs, scale_row, shift_row):
    centre = lax.optimization_barrier(jnp.mean(inputs, -1, keepdims=True))
    centered = inputs - centre
    spread = lax.optimization_barrier(jnp.mean(centered * centered, -1, keepdims=True))
    return centered * lax.rsqrt(spread + 1e-06) * scale_row + shift_row

def exact_gelu(inputs):
    return jax.nn.gelu(inputs, approximate=False)

def live_slots():
    position = jnp.arange(SEQLEN, dtype=jnp.int32)
    block_index = position // SLOTS
    inner_slot = position % SLOTS
    grid_row = BAND * block_index + inner_slot // GRID
    is_patch = (inner_slot < BAND * GRID) & (grid_row < GRID)
    return is_patch | (inner_slot == BAND * GRID) & (block_index == 0)

def forward(weight_set, token_rows, mask_rows, live_mask):
    w_qkv, w_out, w_fc1, w_fc2, vector_params = weight_set
    group_size = token_rows.shape[0]
    masked = (mask_rows == 1)[..., None]
    start_rows = jnp.where(masked, vector_params[:, 14], token_rows)
    normed = low(layer_norm(start_rows, vector_params[:, 0], vector_params[:, 1]))
    bias_qkv = jnp.concatenate([vector_params[:, 2], jnp.zeros((D,), jnp.float32), vector_params[:, 3]])
    projected = low_back(low(jnp.einsum('gsd,de->gse', normed, w_qkv, precision=highest) + bias_qkv))
    head_shape = (group_size, SEQLEN, HEADS, HEAD_DIM)
    queries = projected[..., :D].reshape(head_shape)
    key_heads = projected[..., D:2 * D].reshape(head_shape)
    value_heads = projected[..., 2 * D:].reshape(head_shape)
    scores = jnp.einsum('gqhd,gkhd->ghqk', queries, key_heads, precision=highest) * HEAD_DIM ** (-0.5)
    scores = jnp.where(live_mask[None, None, None, :], scores, -1e+30)
    largest = lax.optimization_barrier(jnp.max(scores, -1, keepdims=True))
    raised = jnp.exp(scores - largest)
    probs = raised / lax.optimization_barrier(jnp.sum(raised, -1, keepdims=True))
    attended = jnp.einsum('ghqk,gkhd->gqhd', probs, value_heads, precision=highest).reshape(group_size, SEQLEN, D)
    attended = low_back(low(attended))
    branch = low_back(jnp.einsum('gsd,de->gse', attended, w_out, precision=highest)) + vector_params[:, 4]
    middle = start_rows + vector_params[:, 5] * branch
    second = low(layer_norm(middle, vector_params[:, 6], vector_params[:, 7]))
    fc1_bias = vector_params[:, 8:12].T.reshape(FF)
    hidden = low_back(jnp.einsum('gsd,de->gse', second, w_fc1, precision=highest)) + fc1_bias
    active = low(exact_gelu(hidden))
    mlp_out = low_back(jnp.einsum('gsf,fd->gsd', active, w_fc2, precision=highest)) + vector_params[:, 12]
    return (middle + vector_params[:, 13] * mlp_out) * live_mask[None, :, None].astype(jnp.float32)

def sgd_step(gradient, master, moment, teacher, step_rate, decay_rate):
    pulled = gradient + decay_rate * master
    moment_new = momentum_rate * moment + pulled
    weight_new = master - step_rate * (pulled + momentum_rate * moment_new)
    teacher_new = teacher_rate * teacher + (1.0 - teacher_rate) * weight_new
    return (weight_new, moment_new, teacher_new, weight_new.astype(jnp.bfloat16))

def reference(tokens, masks, cotangent, w_qkv, w_out, w_fc1, w_fc2, vectors, master_qkv, master_out, master_fc1, master_fc2, master_vectors, moment_qkv, moment_out, moment_fc1, moment_fc2, moment_vectors, teacher_qkv, teacher_out, teacher_fc1, teacher_fc2, teacher_vectors):
    weights = (w_qkv.astype(jnp.float32), w_out.astype(jnp.float32), w_fc1.astype(jnp.float32), w_fc2.astype(jnp.float32), vectors.astype(jnp.float32))
    live_mask = live_slots()
    group_size = 8 if IMAGES % 8 == 0 else 1
    steps_count = IMAGES // group_size
    token_groups = tokens.astype(jnp.float32).reshape(steps_count, group_size, SEQLEN, D)
    mask_groups = masks.reshape(steps_count, group_size, SEQLEN)
    seed_rows = cotangent.astype(jnp.float32) * (masks == 1).astype(jnp.float32)[..., None]
    seed_groups = seed_rows.reshape(steps_count, group_size, SEQLEN, D)

    def accumulate(running, group_data):
        token_rows, mask_rows, seed_part = group_data

        def apply_layer(weight_set, inputs):
            return forward(weight_set, inputs, mask_rows, live_mask)
        result, pull_back = jax.vjp(apply_layer, weights, token_rows)
        weight_grads, token_grad = pull_back(seed_part)
        running = tuple((left + right for left, right in zip(running, weight_grads)))
        return (running, (result.astype(jnp.bfloat16), token_grad))
    initial = tuple((jnp.zeros_like(weight) for weight in weights))
    grads, (results, token_grads) = lax.scan(accumulate, initial, (token_groups, mask_groups, seed_groups))
    output = results.reshape(IMAGES, SEQLEN, D)
    input_grad = token_grads.reshape(IMAGES, SEQLEN, D)
    big_rate = matrix_rate / math.sqrt(IMAGES)
    small_rate = vector_rate / math.sqrt(IMAGES)
    up_qkv = sgd_step(grads[0], master_qkv, moment_qkv, teacher_qkv, big_rate, matrix_decay)
    up_out = sgd_step(grads[1], master_out, moment_out, teacher_out, big_rate, matrix_decay)
    up_fc1 = sgd_step(grads[2], master_fc1, moment_fc1, teacher_fc1, big_rate, matrix_decay)
    up_fc2 = sgd_step(grads[3], master_fc2, moment_fc2, teacher_fc2, big_rate, matrix_decay)
    up_vec = sgd_step(grads[4], master_vectors, moment_vectors, teacher_vectors, small_rate, 0.0)
    return (output, input_grad, grads[0], grads[1], grads[2], grads[3], grads[4], up_qkv[0], up_out[0], up_fc1[0], up_fc2[0], up_vec[0], up_qkv[1], up_out[1], up_fc1[1], up_fc2[1], up_vec[1], up_qkv[2], up_out[2], up_fc1[2], up_fc2[2], up_vec[2], up_qkv[3], up_out[3], up_fc1[3], up_fc2[3], up_vec[3])
```

```python
import functools
import math
from typing import NamedTuple

import jax
import jax.numpy as jnp
from jax import lax
from jax.experimental import pallas as pl
from jax.experimental.pallas import tpu as pltpu
from jax.sharding import PartitionSpec as P

HEADS = 12
HEAD_DIM = 64
GRID = 14
BAND = 4
SLOTS = 64

momentum_rate = 0.9
teacher_rate = 0.75
matrix_rate = 0.003
vector_rate = 0.03
matrix_decay = 0.05

F32 = jnp.float32
BF16 = jnp.bfloat16
TILE = 32
NN = (((1,), (0,)), ((), ()))
NT = (((1,), (1,)), ((), ()))
TN = (((0,), (0,)), ((), ()))
QKV, OUT, FC1, FC2 = range(4)


def dot(a, b, form=NN):
    return lax.dot_general(a, b, form, preferred_element_type=F32)


def is_live(position):
    block = position // SLOTS
    inner = position % SLOTS
    patch = (inner < BAND * GRID) & (BAND * block + inner // GRID < GRID)
    return patch | (inner == BAND * GRID) & (block == 0)


def used_rows(seq_len):
    last = max(s for s in range(seq_len) if is_live(s))
    return min(seq_len, -(-(last + 1) // TILE) * TILE)


def normal(x):
    centre = jnp.mean(x, -1, keepdims=True)
    c = x - centre
    rstd = lax.rsqrt(jnp.mean(c * c, -1, keepdims=True) + 1e-6)
    return c * rstd, rstd


def layer(dims, r, emit, unit_of):
    images, rows, width, ff = dims
    total = images * rows
    tile = rows // 2 if rows % 32 == 0 else TILE
    per_image = rows // tile
    pairs = width // 128

    def vec(k):
        return r.vec[k : k + 1, :]

    def wide_mask(i, at):
        return jnp.concatenate([r.mask[i, pl.ds(at, tile), :].astype(F32)] * (width // 128), 1)

    def start_of(i, at, m):
        return jnp.where(m > 0.5, vec(14), r.tok[i, pl.ds(at, tile), :].astype(F32))

    def row_tiles(body, lo=0, hi=images):
        @pl.loop(lo * per_image, hi * per_image)
        def _(t):
            i = t // per_image
            at = pl.multiple_of((t % per_image) * tile, tile)
            body(i, at, pl.ds(pl.multiple_of(t * tile, tile), tile))

    def add_sum(k, x):
        r.gsum[k * 8 : (k + 1) * 8, :] += x.reshape(-1, 8, width).sum(0)

    r.gsum[...] = jnp.zeros_like(r.gsum)
    lane_row = lax.broadcasted_iota(jnp.int32, (rows, 128), 0)
    r.live[...] = jnp.where(is_live(lane_row), 1.0, 0.0).astype(F32)
    for ref in (r.out, r.ingrad):
        ref[:, rows:, :] = jnp.zeros((images, ref.shape[1] - rows, width), BF16)
    key_row = lax.broadcasted_iota(jnp.int32, (rows, rows), 0)
    r.dead[...] = jnp.where(is_live(key_row), 0.0, -1e30).astype(F32)

    yield

    def first(i, at, ds):
        m = wide_mask(i, at)
        xhat, _ = normal(start_of(i, at, m))
        r.normed[ds, :] = (xhat * vec(0) + vec(1)).astype(BF16)

    row_tiles(first)
    yield

    for i in range(images):
        ds = pl.ds(i * rows, rows)
        x = r.normed[ds, :]
        for b in range(3):
            for n in range(width // 256):
                c = b * width + n * 256
                y = dot(x, r.w_qkv[:, c : c + 256])
                if b == 0:
                    y = y + r.vec[2:3, n * 256 : (n + 1) * 256]
                if b == 2:
                    y = y + r.vec[3:4, n * 256 : (n + 1) * 256]
                y = y.astype(BF16)
                if b == 0:
                    y = y * BF16(HEAD_DIM**-0.5)
                r.proj[ds, c : c + 256] = y
        yield

    first_head = lax.broadcasted_iota(jnp.int32, (rows, 128), 1) < HEAD_DIM

    def stacked(x):
        zero = jnp.zeros_like(x)
        return jnp.concatenate([jnp.where(first_head, x, zero), jnp.where(first_head, zero, x)], 0)

    def pair_of(i, p, b):
        return (pl.ds(i * rows, rows), pl.ds(pl.multiple_of(b * width + p * 128, 128), 128))

    def forward_pair(p):
        for i in range(images):
            q2, k2, v2 = (r.proj[pair_of(i, p, b)] for b in range(3))
            scores = dot(stacked(k2), q2, NT)
            v_t = v2.T
            parts = []
            for h in range(2):
                s = scores[h * rows : (h + 1) * rows] + r.dead[...]
                e = jnp.exp(s - jnp.max(s, 0, keepdims=True))
                pr = (e * (1.0 / jnp.sum(e, 0, keepdims=True))).astype(BF16)
                r.probs[i * pairs + p, h * rows : (h + 1) * rows, :] = pr
                parts.append(dot(v_t[h * HEAD_DIM : (h + 1) * HEAD_DIM], pr))
            out = jnp.concatenate(parts, 0).T
            r.att[pl.ds(i * rows, rows), pl.ds(pl.multiple_of(p * 128, 128), 128)] = out.astype(BF16)

    for p in range(pairs):
        forward_pair(p)
        yield

    @pl.loop(0, images)
    def _(i):
        ds = pl.ds(pl.multiple_of(i * rows, TILE), rows)
        r.mid[ds, :] = dot(r.att[ds, :], r.w_out[...])

    yield

    def second(i, at, ds):
        m = wide_mask(i, at)
        branch = r.mid[ds, :] + vec(4)
        middle = start_of(i, at, m) + vec(5) * branch
        r.branch[ds, :] = branch.astype(BF16)
        r.mid[ds, :] = middle
        xhat, _ = normal(middle)
        r.sec[ds, :] = (xhat * vec(6) + vec(7)).astype(BF16)

    def seeded(i, at, ds):
        m = wide_mask(i, at)
        seed = r.cot[i, pl.ds(at, tile), :].astype(F32) * m
        r.gm[ds, :] = (seed * vec(13)).astype(BF16)
        add_sum(12, seed * vec(13))
        r.mlp[ds, :] = jnp.zeros((tile, width), F32)
        r.gs[ds, :] = jnp.zeros((tile, width), F32)

    row_tiles(second)
    yield
    row_tiles(seeded)
    yield

    for t in range(ff // width):
        u = unit_of(t)
        base = pl.multiple_of(u * width, width)
        for n in range(width // 256):
            cols = pl.ds(pl.multiple_of(base + n * 256, 256), 256)
            bias = r.vec[pl.ds(8 + u, 1), n * 256 : (n + 1) * 256]
            tot = jnp.zeros((8, 256), F32)
            for i in range(images):
                ds = pl.ds(i * rows, rows)
                h = dot(r.sec[ds, :], r.w_fc1[:, cols]) + bias
                ga = dot(r.gm[ds, :], r.w_fc2[cols, :], NT)
                phi = 0.5 * (1.0 + lax.erf(h * 0.5**0.5))
                r.act[ds, n * 256 : (n + 1) * 256] = (h * phi).astype(BF16)
                gh = ga * (phi + h * jnp.exp(-0.5 * h * h) * (2.0 * math.pi) ** -0.5)
                r.gh[ds, n * 256 : (n + 1) * 256] = gh.astype(BF16)
                tot = tot + gh.reshape(-1, 8, 256).sum(0)
            r.gsum[pl.ds(pl.multiple_of((8 + u) * 8, 8), 8), n * 256 : (n + 1) * 256] += tot
            yield
        for i in range(images):
            ds = pl.ds(i * rows, rows)
            r.mlp[ds, :] += dot(r.act[ds, :], r.w_fc2[pl.ds(base, width), :])
            r.gs[ds, :] += dot(r.gh[ds, :], r.w_fc1[:, pl.ds(base, width)], NT)
            yield
        emit(FC2, t, dot(r.act[...], r.gm[...], TN))
        yield
        emit(FC1, t, dot(r.sec[...], r.gh[...], TN))
        yield

    def middle_back(i, at, ds):
        m = wide_mask(i, at)
        seed = r.cot[i, pl.ds(at, tile), :].astype(F32) * m
        mlp = r.mlp[ds, :] + vec(12)
        middle = r.mid[ds, :]
        live = jnp.concatenate([r.live[pl.ds(at, tile), :]] * (width // 128), 1)
        r.out[i, pl.ds(at, tile), :] = ((middle + vec(13) * mlp) * live).astype(BF16)
        add_sum(13, seed * mlp)
        xhat, rstd = normal(middle)
        g = r.gs[ds, :]
        add_sum(6, g * xhat)
        add_sum(7, g)
        gx = g * vec(6)
        gmid = seed + rstd * (
            gx - jnp.mean(gx, -1, keepdims=True) - xhat * jnp.mean(gx * xhat, -1, keepdims=True)
        )
        r.gs[ds, :] = gmid
        gb = gmid * vec(5)
        add_sum(4, gb)
        add_sum(5, gmid * r.branch[ds, :].astype(F32))
        r.act[ds, :] = gb.astype(BF16)

    row_tiles(middle_back)
    yield

    @pl.loop(0, images)
    def _(i):
        ds = pl.ds(pl.multiple_of(i * rows, TILE), rows)
        r.gatt[ds, :] = dot(r.act[ds, :], r.w_out[...], NT).astype(BF16)

    yield
    emit(OUT, 0, dot(r.att[...], r.act[...], TN))

    yield

    def back_pair(p, which):
        for i in which:
            q2, k2, v2 = (r.proj[pair_of(i, p, b)] for b in range(3))
            go = r.gatt[pl.ds(i * rows, rows), pl.ds(pl.multiple_of(p * 128, 128), 128)]
            gp = dot(stacked(v2), go, NT)
            k_t = k2.T
            pr = r.probs[i * pairs + p]
            parts, gsc = [], []
            for h in range(2):
                prf = pr[h * rows : (h + 1) * rows].astype(F32)
                t = prf * gp[h * rows : (h + 1) * rows]
                s = (t - prf * jnp.sum(t, 0, keepdims=True)).astype(BF16)
                gsc.append(s)
                parts.append(dot(k_t[h * HEAD_DIM : (h + 1) * HEAD_DIM], s))
            gv = dot(pr, go)
            gv = jnp.where(first_head, gv[:rows], gv[rows:]).astype(BF16)
            gk = dot(jnp.concatenate(gsc, 0), q2)
            gk = jnp.where(first_head, gk[:rows], gk[rows:]).astype(BF16)
            gq = (jnp.concatenate(parts, 0).T * HEAD_DIM**-0.5).astype(BF16)
            r.proj[pair_of(i, p, 0)] = gq
            r.proj[pair_of(i, p, 1)] = gk
            r.proj[pair_of(i, p, 2)] = gv
            at = pl.ds(pl.multiple_of(p * 128, 128), 128)
            r.gsum[16:24, at] += gq.astype(F32).reshape(-1, 8, 128).sum(0)
            r.gsum[24:32, at] += gv.astype(F32).reshape(-1, 8, 128).sum(0)

    groups = width // 256

    def emit_group(g):
        cols = [slice(b * width + g * 256, b * width + (g + 1) * 256) for b in range(3)]
        emit(QKV, g, dot(r.normed[...], jnp.concatenate([r.proj[:, c] for c in cols], 1), TN))

    for g in range(groups - 1):
        for p in (2 * g, 2 * g + 1):
            back_pair(p, range(images))
            yield
        emit_group(g)
        yield

    def first_back(i, at, ds):
        m = wide_mask(i, at)
        xhat, rstd = normal(start_of(i, at, m))
        g = r.mlp[ds, :]
        add_sum(0, g * xhat)
        add_sum(1, g)
        gx = g * vec(0)
        gst = r.gs[ds, :] + rstd * (
            gx - jnp.mean(gx, -1, keepdims=True) - xhat * jnp.mean(gx * xhat, -1, keepdims=True)
        )
        add_sum(14, gst * m)
        r.ingrad[i, pl.ds(at, tile), :] = (gst * (1.0 - m)).astype(BF16)

    for i in range(images):
        back_pair(2 * groups - 2, (i,))
        back_pair(2 * groups - 1, (i,))
        yield
        if i == images - 1:
            emit_group(groups - 1)
            yield
        ds = pl.ds(i * rows, rows)
        r.mlp[ds, :] = dot(r.proj[ds, :], r.w_qkv[...], NT)
        yield
        row_tiles(first_back, i, i + 1)
        yield
    r.gvec[...] = r.gsum[...].reshape(16, 8, width).sum(1)
    yield


class Refs:
    def __init__(self, *groups):
        for group in groups:
            self.__dict__.update(group._asdict())


class Weights(NamedTuple):
    w_qkv: object
    w_out: object
    w_fc1: object
    w_fc2: object


class Rows(NamedTuple):
    tok: object
    mask: object
    cot: object
    vec: object
    out: object
    ingrad: object
    gvec: object


class Work(NamedTuple):
    gsum: object
    dead: object
    live: object
    normed: object
    proj: object
    probs: object
    att: object
    branch: object
    mid: object
    sec: object
    gm: object
    mlp: object
    gs: object
    act: object
    gh: object
    gatt: object


def plain_kernel(dims, tok, mask, cot, qkv, out_w, fc1, fc2, vec, out, ingrad, *refs):
    grads, gvec, work = refs[:4], refs[4], refs[5:]
    rows = Rows(tok, mask, cot, vec, out, ingrad, gvec)
    r = Refs(Weights(qkv, out_w, fc1, fc2), rows, Work(*work))
    width = dims[2]

    def emit(kind, u, value):
        value = value.astype(BF16)
        if kind == FC1:
            grads[FC1][:, pl.ds(pl.multiple_of(u * width, width), width)] = value
        elif kind == FC2:
            grads[FC2][pl.ds(pl.multiple_of(u * width, width), width), :] = value
        elif kind == OUT:
            grads[OUT][...] = value
        else:
            for b in range(3):
                c = b * width + u * 256
                grads[QKV][:, c : c + 256] = value[:, b * 256 : (b + 1) * 256]

    for _ in layer(dims, r, emit, lambda t: t):
        pass


def scratch(dims):
    images, rows, width, ff = dims
    total = images * rows
    low = lambda *s: pltpu.VMEM(s, BF16)
    full = lambda *s: pltpu.VMEM(s, F32)
    return Work(
        gsum=full(128, width),
        dead=full(rows, rows),
        live=full(rows, 128),
        normed=low(total, width),
        proj=low(total, 3 * width),
        probs=low(images * (width // 128), 2 * rows, rows),
        att=low(total, width),
        branch=low(total, width),
        mid=full(total, width),
        sec=low(total, width),
        gm=low(total, width),
        mlp=full(total, width),
        gs=full(total, width),
        act=low(total, width),
        gh=low(total, width),
        gatt=low(total, width),
    )


def plain_layer(tok, mask, cot, w_qkv, w_out, w_fc1, w_fc2, vec):
    images, seq_len, width = tok.shape
    dims = (images, used_rows(seq_len), width, w_fc1.shape[1])
    shape = jax.ShapeDtypeStruct
    return pl.pallas_call(
        functools.partial(plain_kernel, dims),
        out_shape=(
            shape(tok.shape, BF16),
            shape(tok.shape, BF16),
            shape(w_qkv.shape, BF16),
            shape(w_out.shape, BF16),
            shape(w_fc1.shape, BF16),
            shape(w_fc2.shape, BF16),
            shape((16, width), F32),
        ),
        in_specs=[pl.BlockSpec(memory_space=pltpu.VMEM)] * 8,
        out_specs=[pl.BlockSpec(memory_space=pltpu.VMEM)] * 7,
        scratch_shapes=list(scratch(dims)),
        compiler_params=pltpu.CompilerParams(
            vmem_limit_bytes=63 << 20
        ),
        name="layer",
    )(tok, mask, cot, w_qkv, w_out, w_fc1, w_fc2, vec)


NZ = 4
PARTS = 12
MESH = pl.DeviceIdType.MESH


class Sems:
    count = 0

    def take(self, count, each=1):
        at = self.count
        self.count += count * each
        return at


def make_sems():
    s = Sems()
    s.tok, s.mask = s.take(3), s.take(3)
    s.cot, s.out, s.ingrad = s.take(9), s.take(9), s.take(9)
    s.vec_z, s.vec_y = s.take(3), s.take(1)
    s.wz, s.wy, s.wx, s.wc = (s.take(4, n) for n in (4, 4, 8, 8))
    s.c, s.r1, s.r2 = (s.take(PARTS + 1) for _ in range(3))
    s.zr1, s.zr2 = s.take(9, 3), s.take(3)
    s.gx, s.gc = s.take(7), s.take(4)
    s.vs, s.vy, s.vz, s.vb = s.take(3), s.take(1), s.take(3), s.take(3)
    return s


SEMS = make_sems()
LOCAL = 90


SCHEDULE = (
    (6, 0), (5, 0, 3), (5, 0, 1), (0, 0), (10,), (2, 0, 0), (1, 0, 3), (5, 0, 2), (11,), (1, 0, 1),
    (5, 1, 3), (6, 1), (2, 0, 3), (9,), (0, 1), (3, 0, 0, 1), (2, 0, 1), (3, 0, 3, 0), (2, 1, 0),
    (3, 0, 1, 0), (3, 0, 3, 1), (1, 0, 2), (5, 1, 1), (6, 2), (3, 0, 1, 1), (3, 1, 0, 1), (1, 1, 3),
    (5, 1, 2), (7, 0), (3, 0, 2, 0), (1, 1, 1), (5, 2, 3), (3, 1, 3, 0), (2, 0, 2), (1, 1, 2),
    (5, 2, 1), (3, 1, 1, 0), (3, 0, 2, 1), (3, 1, 2, 0), (4, 0, 0, 1), (4, 0, 3, 0), (4, 0, 3, 1),
    (4, 0, 1, 0), (4, 0, 1, 1), (4, 0, 2, 0), (4, 0, 2, 1), (26, 0), (0, 2), (0, 3), (2, 2, 0),
    (1, 2, 3), (5, 2, 2), (6, 3), (7, 1), (0, 4), (2, 1, 3), (0, 5), (2, 1, 1), (0, 6), (2, 1, 2),
    (3, 2, 0, 1), (0, 7), (1, 2, 1), (5, 3, 3), (7, 2), (0, 8), (3, 2, 3, 0), (0, 9), (0, 10),
    (2, 2, 3), (3, 1, 3, 1), (3, 1, 1, 1), (3, 1, 2, 1), (4, 1, 0, 1), (4, 1, 3, 0), (4, 1, 3, 1),
    (4, 1, 1, 0), (4, 1, 1, 1), (4, 1, 2, 0), (4, 1, 2, 1), (26, 1), (0, 11), (0, 12), (3, 2, 1, 0),
    (2, 3, 0), (1, 2, 2), (5, 3, 1), (8,), (0, 13), (3, 2, 3, 1), (2, 2, 1), (1, 3, 3), (5, 3, 2),
    (3, 3, 0, 1), (3, 2, 2, 0), (2, 2, 2), (3, 2, 1, 1), (1, 3, 1), (3, 3, 3, 0), (3, 2, 2, 1),
    (4, 2, 0, 1), (4, 2, 3, 0), (4, 2, 3, 1), (4, 2, 1, 0), (4, 2, 1, 1), (4, 2, 2, 0),
    (4, 2, 2, 1), (4, 3, 0, 1), (26, 2), (26, 3), (0, 14), (2, 3, 3), (3, 3, 1, 0), (0, 15),
    (0, 16), (0, 17), (0, 18), (0, 19), (0, 20), (3, 3, 3, 1), (2, 3, 1), (0, 21), (1, 3, 2),
    (12, 0), (4, 3, 3, 0), (4, 3, 3, 1), (0, 22), (3, 3, 1, 1), (0, 23), (0, 24), (12, 1),
    (3, 3, 2, 0), (0, 25), (0, 26), (0, 27), (0, 28), (2, 3, 2), (0, 29), (4, 3, 1, 0),
    (4, 3, 1, 1), (0, 30), (0, 31), (13, 0), (12, 2), (0, 32), (12, 3), (3, 3, 2, 1), (0, 33),
    (13, 1), (0, 34), (0, 35), (0, 36), (14, 0), (0, 37), (4, 3, 2, 0), (4, 3, 2, 1), (0, 38),
    (0, 39), (12, 4), (13, 2), (0, 40), (12, 5), (0, 41), (0, 42), (13, 3), (0, 43), (0, 44),
    (0, 45), (14, 2), (0, 46), (18, 0), (18, 1), (18, 2), (13, 4), (12, 6), (12, 7), (0, 47),
    (0, 48), (25, 25), (13, 5), (0, 49), (14, 4), (12, 8), (0, 50), (0, 51), (0, 52), (0, 53),
    (13, 7), (12, 9), (13, 8), (13, 6), (0, 54), (25, 25), (0, 55), (15, 2, 0), (0, 56), (12, 10),
    (13, 9), (0, 57), (19, 0), (0, 58), (0, 59), (0, 60), (19, 1), (14, 6), (15, 1, 0), (0, 61),
    (0, 62), (16, 2, 0), (0, 63), (0, 64), (0, 65), (20,), (19, 2), (12, 11), (13, 10), (12, 12),
    (17, 2), (15, 0, 0), (13, 11), (15, 3, 0), (16, 1, 0), (21,), (13, 12), (17, 1), (22,),
    (15, 0, 1), (16, 0, 0), (15, 0, 2), (16, 3, 0), (17, 3), (16, 0, 1), (16, 0, 2), (15, 0, 3),
    (23,), (16, 0, 3), (24,), (17, 0),
)

OFFSET = (0, 1, 3, 2)


class More(NamedTuple):
    vecs: object
    U: object
    RC: object
    R1: object
    R2: object
    ZR1: object
    ZR2: object
    XS: object
    XR: object
    gv0: object
    gv1: object
    gv2: object
    gv3: object
    gv4: object
    ss: object
    rs: object
    ls: object


def linked_kernel(dims, tokens, wide, cotangent, *refs):
    w_in, in_vec, o_out, o_ingrad, g_outs, gvec_out = (
        *(refs[:4], refs[4], refs[5]),
        *(refs[6], refs[7:11], refs[11]),
    )
    refs = refs[12:]
    w, rows, g_held = refs[:4], Rows(*refs[4:11]), refs[11:15]
    r = Refs(Weights(*w), rows, Work(*refs[15:31]), More(*refs[31:]))
    images, rows, width, ff = dims
    d, s = lax.axis_index("dp"), lax.axis_index("seq")
    z, y, x, c = d // 2, d % 2, s // 2, s % 2
    slots = tokens.shape[1]
    here = (d, s)
    to_c, to_x, to_y = (d, x * 2 + 1 - c), (d, (1 - x) * 2 + c), (z * 2 + 1 - y, s)

    def to_z(k):
        return (lax.rem(z + k, NZ) * 2 + y, s)

    def to_s(k):
        return (d, lax.rem(s + k, 4))

    def back(k):
        return lax.rem(z + NZ - k, NZ)

    pending = []

    def copy(sem, src, dst, dev):
        return pltpu.make_async_remote_copy(
            src, dst, r.ss.at[sem], r.rs.at[sem], device_id=dev, device_id_type=MESH
        )

    def send(sem, src, dst, dev, keep=True):
        op = copy(sem, src, dst, dev)
        op.start()
        if keep:
            pending.append(op)
        return op

    def got(sem, dst):
        copy(sem, dst, dst, to_c).wait_recv()

    local_ops = {}

    def local(name, src, dst):
        k = len(local_ops)
        op = pltpu.make_async_copy(src, dst, r.ls.at[k])
        op.start()
        local_ops[name] = op

    barrier = pltpu.get_barrier_semaphore()
    peers = [to_y] + [to_s(k) for k in (1, 2, 3)] + [to_z(k) for k in (1, 2, 3)]
    for dev in peers:
        pl.semaphore_signal(barrier, inc=1, device_id=dev, device_id_type=MESH)
    pl.semaphore_wait(barrier, len(peers))

    def band(t):
        return pl.ds(pl.multiple_of(t * slots, 64), slots)

    def scatter(sem, src, dst, lo=0, hi=images):
        for k in (2, 1, 3):
            t = lax.rem(s + k, 4)
            rows_out = src.at[pl.ds(t * images + lo, hi - lo)]
            send(sem + k - 1, rows_out, dst.at[lo:hi, band(s)], to_s(k))
        local((sem, 0), src.at[pl.ds(s * images + lo, hi - lo)], dst.at[lo:hi, band(s)])

    def scattered(sem, dst, lo=0, hi=images):
        for k in (2, 1, 3):
            got(sem + k - 1, dst.at[lo:hi, band(lax.rem(s + 4 - k, 4))])
        local_ops[sem, 0].wait()

    def block(a, zz, yy):
        return (zz * 2 + yy) * w_in[a].shape[0]

    def cut(ref, a, base, kind, mine=True):
        n, m = w_in[a].shape
        half = n // 2
        if kind == 2:
            at = base + (c if mine else 1 - c) * half
            return ref.at[pl.ds(pl.multiple_of(at, 16), half)]
        at, xx = base + c * half, x if mine else 1 - x
        if a == FC2:
            q = half // 4
            if kind == 0:
                return ref.at[pl.ds(pl.multiple_of(at + x * q, 16), half - q)]
            return ref.at[pl.ds(pl.multiple_of(at + xx * (half - q), 16), q)]
        q = m // 4 if a == FC1 else m // 6
        rs = pl.ds(pl.multiple_of(at, 16), half)
        if kind == 0:
            return ref.at[rs, pl.ds(pl.multiple_of(x * q, 128), m - q)]
        return ref.at[rs, pl.ds(pl.multiple_of(xx * (m - q), 128), q)]

    def piece(a, zz, yy, kind, mine=True):
        return cut(w[a], a, block(a, zz, yy), kind, mine)

    def own_piece(a):
        return cut(w_in[a], a, 0, 0)

    def w_own(a):
        n = w_in[a].shape[0]
        local(
            (a,),
            w_in[a],
            w[a].at[pl.ds(pl.multiple_of(block(a, z, y), 16), n)],
        )

    def w_y0(a):
        send(SEMS.wy + 4 * a, own_piece(a), piece(a, z, y, 0), to_y)

    def w_z(a, k):
        send(SEMS.wz + 4 * a + k - 1, own_piece(a), piece(a, z, y, 0), to_z(k))

    def w_share(a, k, other):
        p = piece(a, back(k), 1 - y if other else y, 1)
        send(SEMS.wx + 8 * a + 4 * other + k, p, p, to_x)

    def w_zr(a, k):
        p = piece(a, back(k), y, 0)
        got(SEMS.wz + 4 * a + k - 1, p)
        send(SEMS.wy + 4 * a + k, p, p, to_y)
        w_share(a, k, 0)

    def w_yr(a, k):
        got(SEMS.wy + 4 * a + k, piece(a, back(k), 1 - y, 0))
        w_share(a, k, 1)

    def w_xr(a, k, other):
        yy = 1 - y if other else y
        got(SEMS.wx + 8 * a + 4 * other + k, piece(a, back(k), yy, 1, False))
        p = piece(a, back(k), yy, 2)
        send(SEMS.wc + 8 * a + 4 * other + k, p, p, to_c)

    def w_cr(a, k, other):
        yy = 1 - y if other else y
        got(SEMS.wc + 8 * a + 4 * other + k, piece(a, back(k), yy, 2, False))

    BLOCKS = [(0, 1), (3, 0), (3, 1), (1, 0), (1, 1), (2, 0), (2, 1)]

    def unit_of(t):
        return lax.rem(z + OFFSET[t], NZ)

    def part_of(kind, t):
        return (9 + t, 8, 2 * t + 1, 2 * t)[kind]

    def x_first(q):
        return q in (0, 2, 4, 6)

    def halves(q):
        return (min(q, 11), *((0, 2) if q < 11 else (q - 11, q - 10)))

    step, half, third = width // 16, width // 2, width // 4
    sent = {}

    def emit(kind, t, value):
        q = part_of(kind, t)
        slot = q % 4
        value = value.astype(BF16)
        for cc in range(2):
            for yy in range(2):
                if kind == FC2:
                    pieces = [(yy * half + cc * third, 0, third)]
                else:
                    pieces = [(((zz * 2 + yy) * 2 + cc) * step, zz * step, step) for zz in range(4)]
                for src, dst, size in pieces:
                    for xx in range(2):
                        v = value[src : src + size, xx * half : (xx + 1) * half]
                        r.U[slot, cc, yy, xx, dst : dst + size, :] = v
        for part in (q,) if q < 11 else (11, 12):
            _, lo, hi = halves(part)
            src, dst = r.U.at[slot, 1 - c, :, lo:hi], r.RC.at[slot, :, lo:hi]
            sent[0, part] = send(SEMS.c + part, src, dst, to_c, False)

    def g_1(part):
        q, lo, hi = halves(part)
        slot = q % 4
        got(SEMS.c + part, r.RC.at[slot, :, lo:hi])

        def add(side):
            if x_first(q):

                @pl.loop(0, 2)
                def _(k):
                    r.U[slot, c, k, side] = r.U[slot, c, k, side] + r.RC[slot, k, side]

            else:

                @pl.loop(lo, hi)
                def _(k):
                    r.U[slot, c, side, k] = r.U[slot, c, side, k] + r.RC[slot, side, k]

        if x_first(q):
            add(1 - x)
            op = send(SEMS.r1 + part, r.U.at[slot, c, :, 1 - x], r.R1.at[q], to_x, False)
            add(x)
        else:
            add(1 - y)
            src = r.U.at[slot, c, 1 - y, lo:hi]
            op = send(SEMS.r1 + part, src, r.R1.at[q, lo:hi], to_y, False)
            add(y)
        sent[1, part] = op

    def z_slot(q):
        return unit_of(q // 2) if q < 8 else q - 4

    def zr_sem(part, k):
        j = 8 if part == 12 else z_slot(part)
        return SEMS.zr1 + 3 * j + k - 1

    def g_2(part):
        q, lo, hi = halves(part)
        got(SEMS.r1 + part, r.R1.at[q, lo:hi])
        sent[0, part].wait_send()

        @pl.loop(lo, hi)
        def _(k):
            if x_first(q):
                r.R1[q, k] = r.R1[q, k] + r.U[q % 4, c, k, x]
            else:
                r.R1[q, k] = r.R1[q, k] + r.U[q % 4, c, y, k]

        sent[1, part].wait_send()
        if x_first(q):
            send(SEMS.r2 + q, r.R1.at[q, 1 - y], r.R2.at[q // 2], to_y)
            return
        for k in (2, 1, 3):
            zz = lax.rem(z + k, NZ)
            src = r.R1.at[q, lo:hi, pl.ds(pl.multiple_of(zz * step, 16), step)]
            send(zr_sem(part, k), src, r.ZR1.at[z_slot(q), k - 1, lo:hi], to_z(k))

    def g_3(q):
        t = q // 2
        got(SEMS.r2 + q, r.R2.at[t])
        r.R2[t] = r.R2[t] + r.R1[q, y]
        k = OFFSET[t]
        if k:
            send(SEMS.zr2 + k - 1, r.R2.at[t], r.ZR2.at[k - 1], to_z(k))

    def g_4(kind, i):
        if kind == FC2:
            for k in (1, 2, 3):
                got(SEMS.zr2 + k - 1, r.ZR2.at[k - 1])
            total = r.R2[0].astype(F32)
            for k in range(3):
                total = total + r.ZR2[k].astype(F32)
            g = g_held[FC2]
            g[c, x] = total.astype(BF16).reshape(4, step, half)
            send(SEMS.gx, g.at[c, x], g.at[c, x], to_x)
            return
        for part in {FC1: (1, 3, 5, 7), OUT: (8,), QKV: (9 + i,)}[kind]:
            q, lo, hi = halves(part)
            j = z_slot(q)
            for k in (1, 2, 3):
                got(zr_sem(part, k), r.ZR1.at[j, k - 1, lo:hi])
            rs = pl.ds(pl.multiple_of(z * step, 16), step)
            total = r.R1[q, lo:hi, rs].astype(F32)
            for k in range(3):
                total = total + r.ZR1[j, k, lo:hi].astype(F32)
            r.XS[j, lo:hi] = total.astype(BF16)
        sem, at = x_span(kind, i)
        send(sem, r.XS.at[at], r.XR.at[at], to_x)

    def x_span(kind, i):
        if kind == FC1:
            return SEMS.gx + 1, (slice(0, 4),)
        q, lo, hi = halves(8 if kind == OUT else 9 + i)
        return SEMS.gx + (2 if kind == OUT else 3 + i), (q - 4, slice(lo, hi))

    def g_5(kind, i):
        g = g_held[kind]
        if kind == FC2:
            got(SEMS.gx, g.at[c, 1 - x])
        else:
            sem, at = x_span(kind, i)
            got(sem, r.XR.at[at])
            units = range(4) if kind == FC1 else (at[0],)
            for n, j in enumerate(units):
                sides = (0, 1) if kind == FC1 else range(at[1].start, at[1].stop)
                for xx in sides:
                    g[c, xx, min(i, 2) + n] = r.XS[j, xx] + r.XR[j, xx]
        if kind != QKV or i == 3:
            send(SEMS.gc + kind, g.at[c], g.at[c], to_c)

    def g_6(kind):
        g = g_held[kind]
        got(SEMS.gc + kind, g.at[1 - c])
        o = g_outs[kind]
        for cc in range(2):
            rs = slice(cc * step, (cc + 1) * step)
            for xx in range(2):
                if kind == FC2:
                    for i in range(4):
                        at = (cc * 4 + i) * step
                        dst = o.at[at : at + step, xx * half : (xx + 1) * half]
                        local((kind, cc, xx, i), g.at[cc, xx, i], dst)
                elif kind == QKV:
                    cuts = ((0, 256, 0, 0), (256, half, 1, 0))
                    if xx:
                        cuts = ((0, 128, 1, 128), (128, half, 2, 0))
                    for i in range(3):
                        for b0, b1, at, off in cuts:
                            col = at * width + i * 256 + off
                            dst = o.at[rs, col : col + b1 - b0]
                            local((kind, cc, xx, i, at), g.at[cc, xx, i, :, b0:b1], dst)
                else:
                    for i in range(4 if kind == FC1 else 1):
                        col = i * width + xx * half
                        local((kind, cc, xx, i), g.at[cc, xx, i], o.at[rs, col : col + half])

    def v_part(p):
        return slice(p // 2 * 8, p // 2 * 8 + 8), slice(p % 2 * half, (p % 2 + 1) * half)

    def v_1():
        for p in range(4):
            r.gv0[p] = r.gvec[v_part(p)]
        r.gv1[s] = r.gv0[s]
        for k in (2, 1, 3):
            send(SEMS.vs + k - 1, r.gv0.at[lax.rem(s + k, 4)], r.gv1.at[s], to_s(k))

    def v_2():
        for k in (2, 1, 3):
            got(SEMS.vs + k - 1, r.gv1.at[lax.rem(s + 4 - k, 4)])
        r.gv2[0] = r.gv1[0] + r.gv1[1] + r.gv1[2] + r.gv1[3]
        send(SEMS.vy, r.gv2.at[0], r.gv2.at[1], to_y)

    def v_3():
        got(SEMS.vy, r.gv2.at[1])
        r.gv3[z] = r.gv2[0] + r.gv2[1]
        for k in (2, 1, 3):
            send(SEMS.vz + k - 1, r.gv3.at[z], r.gv3.at[z], to_z(k))

    def v_4():
        for k in (2, 1, 3):
            got(SEMS.vz + k - 1, r.gv3.at[back(k)])
        r.gv4[s] = (r.gv3[0] + r.gv3[1]) + (r.gv3[2] + r.gv3[3])
        for k in (2, 1, 3):
            send(SEMS.vb + k - 1, r.gv4.at[s], r.gv4.at[s], to_s(k))

    def v_5():
        for k in (2, 1, 3):
            got(SEMS.vb + k - 1, r.gv4.at[lax.rem(s + 4 - k, 4)])
        for p in range(4):
            gvec_out[v_part(p)] = r.gv4[p]

    def give_back(sem, src, dst, lo, hi):
        n = hi - lo
        for k in (2, 1, 3):
            t = lax.rem(s + k, 4)
            send(
                sem + k - 1,
                src.at[lo:hi, pl.ds(pl.multiple_of(t * slots, 64), slots)],
                dst.at[pl.ds(s * images + lo, n)],
                to_s(k),
            )
        local(
            (sem, lo, 0),
            src.at[lo:hi, pl.ds(pl.multiple_of(s * slots, 64), slots)],
            dst.at[pl.ds(s * images + lo, n)],
        )

    def given_back(sem, dst, lo, hi):
        for k in (2, 1, 3):
            t = lax.rem(s + 4 - k, 4)
            got(sem + k - 1, dst.at[pl.ds(t * images + lo, hi - lo)])

    def vectors_in():
        total = jnp.zeros((16, width), F32)
        n = width // (2 * NZ)
        lane = lax.broadcasted_iota(jnp.int32, (128, width), 0)
        col = lax.broadcasted_iota(jnp.int32, (128, width), 1)
        for k in range(2 * NZ):
            pick = jnp.where((col == lane + k * n) & (lane < n), 1.0, 0.0).astype(BF16)
            total = total + dot(r.vecs[k % 2, k // 2].astype(BF16), pick)
        r.vec[...] = total

    def vec_z():
        for j in (1, 2, 3):
            got(SEMS.vec_z + j - 1, r.vecs.at[y, back(j)])
        send(SEMS.vec_y, r.vecs.at[y], r.vecs.at[y], to_y)

    def vec_y():
        got(SEMS.vec_y, r.vecs.at[1 - y])
        vectors_in()

    def tokens_in():
        scattered(SEMS.mask, r.mask)
        scattered(SEMS.tok, r.tok)

    def cot_out(i):
        scatter(SEMS.cot + 3 * i, cotangent, r.cot, i, i + 1)

    def cot_in():
        for i in range(images):
            scattered(SEMS.cot + 3 * i, r.cot, i, i + 1)

    def out_back(i):
        give_back(SEMS.out + 3 * i, r.out, o_out, i, i + 1)

    def ingrad_back(i):
        give_back(SEMS.ingrad + 3 * i, r.ingrad, o_ingrad, i, i + 1)

    def drain(keep):
        count = max(0, len(pending) - keep)
        for op in pending[:count]:
            op.wait_send()
        del pending[:count]

    r.vecs[y, z] = in_vec[...]
    for k in (1, 2, 3):
        send(SEMS.vec_z + k - 1, in_vec, r.vecs.at[y, z], to_z(k))
    scatter(SEMS.mask, wide, r.mask)
    scatter(SEMS.tok, tokens, r.tok)
    piece_done = layer(dims, r, emit, unit_of)

    def go(k):
        next(piece_done)

    table = (go, w_zr, w_yr, w_xr, w_cr, w_z, w_y0, cot_out, cot_in, tokens_in, vec_z, vec_y)
    table += (g_1, g_2, g_3, g_4, g_5, g_6, out_back, ingrad_back)
    table += (v_1, v_2, v_3, v_4, v_5, drain, lambda a: local_ops[a,].wait())
    first = True
    for op, *at in SCHEDULE:
        table[op](*at)
        if first:
            for a in (QKV, OUT, FC1, FC2):
                w_own(a)
            first = False
    for _ in piece_done:
        pass
    for i in range(images):
        given_back(SEMS.out + 3 * i, o_out, i, i + 1)
        given_back(SEMS.ingrad + 3 * i, o_ingrad, i, i + 1)
    drain(0)
    for key, op in local_ops.items():
        if len(key) > 2:
            op.wait()


def linked_layer(tokens, wide, cotangent, weights):
    count, slots, width = tokens.shape
    w_qkv, w_out, w_fc1, w_fc2, vectors = weights
    images, seq_len = count // 4, slots * 4
    dims = (images, used_rows(seq_len), width, w_fc1.shape[1])
    n, k = vectors.shape
    vec = jnp.zeros((16, 128), F32).at[:k, :n].set(vectors.astype(F32).T)
    shape = jax.ShapeDtypeStruct
    low = lambda *s: pltpu.VMEM(s, BF16)
    full = lambda *s: pltpu.VMEM(s, F32)
    step, half = width // 16, width // 2
    hbm = pl.BlockSpec(memory_space=pl.ANY)
    vmem = pl.BlockSpec(memory_space=pltpu.VMEM)
    held = [low(w.shape[0] * 2 * NZ, w.shape[1]) for w in weights[:4]]
    held += [low(images, seq_len, w) for w in (width, 128, width)]
    held += [full(16, width)] + [low(images, seq_len, width)] * 2 + [full(16, width)]
    held += [low(2, 2, u, step, half) for u in (3, 1, 4, 4)]
    more = [
        full(2, NZ, 16, 128),
        low(4, 2, 2, 2, width // 4, half),
        low(4, 2, 2, width // 4, half),
        low(PARTS, 2, width // 4, half),
        low(4, width // 4, half),
        low(8, 3, 2, step, half),
        low(3, width // 4, half),
        low(8, 2, step, half),
        low(8, 2, step, half),
        full(4, 8, half),
        full(4, 8, half),
        full(2, 8, half),
        full(4, 8, half),
        full(4, 8, half),
    ]
    more += [pltpu.SemaphoreType.DMA((SEMS.count,))] * 2 + [pltpu.SemaphoreType.DMA((LOCAL,))]
    return pl.pallas_call(
        functools.partial(linked_kernel, dims),
        out_shape=(
            shape(tokens.shape, BF16),
            shape(tokens.shape, BF16),
            *(shape(w.shape, BF16) for w in weights[:4]),
            shape((16, width), F32),
        ),
        in_specs=[hbm] * 7 + [vmem],
        out_specs=[hbm] * 6 + [vmem],
        scratch_shapes=held + list(scratch(dims)) + more,
        compiler_params=pltpu.CompilerParams(
            collective_id=0,
            has_side_effects=True,
            vmem_limit_bytes=63 << 20,
        ),
        name="layer",
    )(tokens, wide, cotangent, w_qkv, w_out, w_fc1, w_fc2, vec)


def sgd_step(gradient, master, moment, teacher, step_rate, decay_rate):
    pulled = gradient + decay_rate * master
    moment_new = momentum_rate * moment + pulled
    weight_new = master - step_rate * (pulled + momentum_rate * moment_new)
    teacher_new = teacher_rate * teacher + (1.0 - teacher_rate) * weight_new
    return (weight_new, moment_new, teacher_new, weight_new.astype(BF16))


def on_device(tokens, masks, cotangent, *rest):
    weights, masters, moments, teachers = rest[:5], rest[5:10], rest[10:15], rest[15:20]
    images, slots, width = tokens.shape
    step = (weights, masters, moments, teachers)
    wide = jnp.broadcast_to((masks == 1).astype(BF16)[..., None], (images, slots, 128))
    if (lax.axis_size("dp"), lax.axis_size("seq")) == (2 * NZ, 4):
        out, ingrad, *sums, gvec = linked_layer(tokens, wide, cotangent, weights)
        return finish(out, ingrad, sums, gvec, *step)
    full = [lax.all_gather(w, "dp", axis=0, tiled=True) for w in weights]
    vec = jnp.zeros((16, width), F32).at[: full[4].shape[1]].set(full[4].astype(F32).T)
    tok, mask, cot = (
        lax.all_to_all(v, "seq", 0, 1, tiled=True) for v in (tokens, wide, cotangent)
    )
    out, ingrad, *grads, gvec = plain_layer(tok, mask, cot, *full[:4], vec)
    out, ingrad = (lax.all_to_all(v, "seq", 1, 0, tiled=True) for v in (out, ingrad))
    sums = [lax.psum_scatter(g, "dp", scatter_dimension=0, tiled=True) for g in grads]
    sums = [lax.psum(g, "seq") for g in sums]
    gvec = lax.psum(gvec, ("dp", "seq"))
    return finish(out, ingrad, sums, gvec, *step)


def update_kernel(steps, *refs):
    ins, outs = refs[:22], refs[22:]
    for k in range(5):
        g = ins[k][...].astype(F32)
        got = sgd_step(g, *(ins[5 * j + k][...] for j in (1, 2, 3)), *steps[k])
        for ref, v in zip((outs[k], *(outs[5 * j + k] for j in (1, 2, 3, 4))), (g, *got)):
            ref[...] = v
    outs[25][...] = ins[20][...]
    outs[26][...] = ins[21][...].astype(F32)


def finish(out, ingrad, sums, gvec, weights, masters, moments, teachers):
    images, slots, width = out.shape
    part = width // lax.axis_size("dp")
    own = lax.dynamic_slice(gvec, (0, lax.axis_index("dp") * part), (16, part))
    own = own[: weights[4].shape[1]]
    image_total = images * lax.axis_size("dp")
    big = (matrix_rate / math.sqrt(image_total), matrix_decay)
    small = (vector_rate / math.sqrt(image_total), 0.0)
    steps = (big, big, big, big, small)
    if part % 16 or images % (part // 16):
        sums = [g.astype(F32) for g in (*sums, own.T)]
        old = zip(sums, masters, moments, teachers, steps)
        ups = [sgd_step(*v, *rates) for *v, rates in old]
        return (out, ingrad.astype(F32), *sums, *(u[j] for j in range(4) for u in ups))
    count = part // 16

    def spec(a):
        if a.ndim == 2 and a.shape[0] < part:
            return pl.BlockSpec(a.shape, lambda i: (0, 0))
        rest = (0,) * (a.ndim - 1)
        return pl.BlockSpec((a.shape[0] // count, *a.shape[1:]), lambda i: (i, *rest))

    flip = lambda group: (*group[:4], group[4].T)
    args = [*sums, own, *flip(masters), *flip(moments), *flip(teachers), out, ingrad]
    shape = jax.ShapeDtypeStruct
    outs = [shape(m.shape, F32) for _ in range(4) for m in flip(masters)]
    outs += [shape(m.shape, BF16) for m in flip(masters)]
    outs += [shape(out.shape, BF16), shape(out.shape, F32)]
    res = pl.pallas_call(
        functools.partial(update_kernel, steps),
        grid=(count,),
        out_shape=outs,
        in_specs=[spec(a) for a in args],
        out_specs=[spec(a) for a in outs],
        compiler_params=pltpu.CompilerParams(vmem_limit_bytes=60 << 20),
        name="update",
    )(*args)
    res = [v.T if k % 5 == 4 and k < 25 else v for k, v in enumerate(res)]
    return (res[25], res[26], *res[:25])


def solution(mesh):
    band = P("dp", "seq", None)
    rows = P("dp", None)
    return jax.shard_map(
        on_device,
        mesh=mesh,
        in_specs=(band, P("dp", "seq"), band) + (rows,) * 20,
        out_specs=(band, band) + (rows,) * 25,
        check_vma=False,
    )
```

```python
import functools
import math
from typing import NamedTuple

import jax
import jax.numpy as jnp
from jax import lax
from jax.experimental import pallas as pl
from jax.experimental.pallas import tpu as pltpu
from jax.sharding import PartitionSpec as P

HEADS = 12
HEAD_DIM = 64
GRID = 14
BAND = 4
SLOTS = 64

momentum_rate = 0.9
teacher_rate = 0.75
matrix_rate = 0.003
vector_rate = 0.03
matrix_decay = 0.05

F32 = jnp.float32
BF16 = jnp.bfloat16
TILE = 32
NN = (((1,), (0,)), ((), ()))
NT = (((1,), (1,)), ((), ()))
TN = (((0,), (0,)), ((), ()))
QKV, OUT, FC1, FC2 = range(4)


def dot(a, b, form=NN):
    return lax.dot_general(a, b, form, preferred_element_type=F32)


def is_live(position):
    block = position // SLOTS
    inner = position % SLOTS
    patch = (inner < BAND * GRID) & (BAND * block + inner // GRID < GRID)
    return patch | (inner == BAND * GRID) & (block == 0)


def used_rows(seq_len):
    last = max(s for s in range(seq_len) if is_live(s))
    return min(seq_len, -(-(last + 1) // TILE) * TILE)


def normal(x):
    centre = jnp.mean(x, -1, keepdims=True)
    c = x - centre
    rstd = lax.rsqrt(jnp.mean(c * c, -1, keepdims=True) + 1e-6)
    return c * rstd, rstd


def layer(dims, r, emit, unit_of):
    images, rows, width, ff = dims
    total = images * rows
    tile = rows // 2 if rows % 32 == 0 else TILE
    per_image = rows // tile
    pairs = width // 128

    def vec(k):
        return r.vec[k : k + 1, :]

    def wide_mask(i, at):
        return jnp.concatenate([r.mask[i, pl.ds(at, tile), :].astype(F32)] * (width // 128), 1)

    def start_of(i, at, m):
        return jnp.where(m > 0.5, vec(14), r.tok[i, pl.ds(at, tile), :].astype(F32))

    def row_tiles(body, lo=0, hi=images):
        @pl.loop(lo * per_image, hi * per_image)
        def _(t):
            i = t // per_image
            at = pl.multiple_of((t % per_image) * tile, tile)
            body(i, at, pl.ds(pl.multiple_of(t * tile, tile), tile))

    def add_sum(k, x):
        r.gsum[k * 8 : (k + 1) * 8, :] += x.reshape(-1, 8, width).sum(0)

    r.gsum[...] = jnp.zeros_like(r.gsum)
    lane_row = lax.broadcasted_iota(jnp.int32, (rows, 128), 0)
    r.live[...] = jnp.where(is_live(lane_row), 1.0, 0.0).astype(F32)
    for ref in (r.out, r.ingrad):
        ref[:, rows:, :] = jnp.zeros((images, ref.shape[1] - rows, width), BF16)
    key_row = lax.broadcasted_iota(jnp.int32, (rows, rows), 0)
    r.dead[...] = jnp.where(is_live(key_row), 0.0, -1e30).astype(F32)

    yield

    def first(i, at, ds):
        m = wide_mask(i, at)
        xhat, _ = normal(start_of(i, at, m))
        r.normed[ds, :] = (xhat * vec(0) + vec(1)).astype(BF16)

    row_tiles(first)
    yield

    for i in range(images):
        ds = pl.ds(i * rows, rows)
        x = r.normed[ds, :]
        for b in range(3):
            for n in range(width // 256):
                c = b * width + n * 256
                y = dot(x, r.w_qkv[:, c : c + 256])
                if b == 0:
                    y = y + r.vec[2:3, n * 256 : (n + 1) * 256]
                if b == 2:
                    y = y + r.vec[3:4, n * 256 : (n + 1) * 256]
                y = y.astype(BF16)
                if b == 0:
                    y = y * BF16(HEAD_DIM**-0.5)
                r.proj[ds, c : c + 256] = y
        yield

    first_head = lax.broadcasted_iota(jnp.int32, (rows, 128), 1) < HEAD_DIM

    def stacked(x):
        zero = jnp.zeros_like(x)
        return jnp.concatenate([jnp.where(first_head, x, zero), jnp.where(first_head, zero, x)], 0)

    def pair_of(i, p, b):
        return (pl.ds(i * rows, rows), pl.ds(pl.multiple_of(b * width + p * 128, 128), 128))

    def forward_pair(p):
        for i in range(images):
            q2, k2, v2 = (r.proj[pair_of(i, p, b)] for b in range(3))
            scores = dot(stacked(k2), q2, NT)
            v_t = v2.T
            parts = []
            for h in range(2):
                s = scores[h * rows : (h + 1) * rows] + r.dead[...]
                e = jnp.exp(s - jnp.max(s, 0, keepdims=True))
                pr = (e * (1.0 / jnp.sum(e, 0, keepdims=True))).astype(BF16)
                r.probs[i * pairs + p, h * rows : (h + 1) * rows, :] = pr
                parts.append(dot(v_t[h * HEAD_DIM : (h + 1) * HEAD_DIM], pr))
            out = jnp.concatenate(parts, 0).T
            r.att[pl.ds(i * rows, rows), pl.ds(pl.multiple_of(p * 128, 128), 128)] = out.astype(BF16)

    for p in range(pairs):
        forward_pair(p)
        yield

    @pl.loop(0, images)
    def _(i):
        ds = pl.ds(pl.multiple_of(i * rows, TILE), rows)
        r.mid[ds, :] = dot(r.att[ds, :], r.w_out[...])

    yield

    def second(i, at, ds):
        m = wide_mask(i, at)
        branch = r.mid[ds, :] + vec(4)
        middle = start_of(i, at, m) + vec(5) * branch
        r.branch[ds, :] = branch.astype(BF16)
        r.mid[ds, :] = middle
        xhat, _ = normal(middle)
        r.sec[ds, :] = (xhat * vec(6) + vec(7)).astype(BF16)

    def seeded(i, at, ds):
        m = wide_mask(i, at)
        seed = r.cot[i, pl.ds(at, tile), :].astype(F32) * m
        r.gm[ds, :] = (seed * vec(13)).astype(BF16)
        add_sum(12, seed * vec(13))
        r.mlp[ds, :] = jnp.zeros((tile, width), F32)
        r.gs[ds, :] = jnp.zeros((tile, width), F32)

    row_tiles(second)
    yield
    row_tiles(seeded)
    yield

    for t in range(ff // width):
        u = unit_of(t)
        base = pl.multiple_of(u * width, width)
        for n in range(width // 256):
            cols = pl.ds(pl.multiple_of(base + n * 256, 256), 256)
            bias = r.vec[pl.ds(8 + u, 1), n * 256 : (n + 1) * 256]
            tot = jnp.zeros((8, 256), F32)
            for i in range(images):
                ds = pl.ds(i * rows, rows)
                h = dot(r.sec[ds, :], r.w_fc1[:, cols]) + bias
                ga = dot(r.gm[ds, :], r.w_fc2[cols, :], NT)
                phi = 0.5 * (1.0 + lax.erf(h * 0.5**0.5))
                r.act[ds, n * 256 : (n + 1) * 256] = (h * phi).astype(BF16)
                gh = ga * (phi + h * jnp.exp(-0.5 * h * h) * (2.0 * math.pi) ** -0.5)
                r.gh[ds, n * 256 : (n + 1) * 256] = gh.astype(BF16)
                tot = tot + gh.reshape(-1, 8, 256).sum(0)
            r.gsum[pl.ds(pl.multiple_of((8 + u) * 8, 8), 8), n * 256 : (n + 1) * 256] += tot
            yield
        emit(FC1, t, dot(r.sec[...], r.gh[...], TN))
        yield
        emit(FC2, t, dot(r.act[...], r.gm[...], TN))
        yield
        for i in range(images):
            ds = pl.ds(i * rows, rows)
            r.mlp[ds, :] += dot(r.act[ds, :], r.w_fc2[pl.ds(base, width), :])
            r.gs[ds, :] += dot(r.gh[ds, :], r.w_fc1[:, pl.ds(base, width)], NT)
            yield

    def middle_back(i, at, ds):
        m = wide_mask(i, at)
        seed = r.cot[i, pl.ds(at, tile), :].astype(F32) * m
        mlp = r.mlp[ds, :] + vec(12)
        middle = r.mid[ds, :]
        live = jnp.concatenate([r.live[pl.ds(at, tile), :]] * (width // 128), 1)
        r.out[i, pl.ds(at, tile), :] = ((middle + vec(13) * mlp) * live).astype(BF16)
        add_sum(13, seed * mlp)
        xhat, rstd = normal(middle)
        g = r.gs[ds, :]
        add_sum(6, g * xhat)
        add_sum(7, g)
        gx = g * vec(6)
        gmid = seed + rstd * (
            gx - jnp.mean(gx, -1, keepdims=True) - xhat * jnp.mean(gx * xhat, -1, keepdims=True)
        )
        r.gs[ds, :] = gmid
        gb = gmid * vec(5)
        add_sum(4, gb)
        add_sum(5, gmid * r.branch[ds, :].astype(F32))
        r.act[ds, :] = gb.astype(BF16)

    row_tiles(middle_back)
    yield

    @pl.loop(0, images)
    def _(i):
        ds = pl.ds(pl.multiple_of(i * rows, TILE), rows)
        r.gatt[ds, :] = dot(r.act[ds, :], r.w_out[...], NT).astype(BF16)

    yield
    emit(OUT, 0, dot(r.att[...], r.act[...], TN))

    yield

    def back_pair(p):
        for i in range(images):
            q2, k2, v2 = (r.proj[pair_of(i, p, b)] for b in range(3))
            go = r.gatt[pl.ds(i * rows, rows), pl.ds(pl.multiple_of(p * 128, 128), 128)]
            gp = dot(stacked(v2), go, NT)
            k_t = k2.T
            pr = r.probs[i * pairs + p]
            parts, gsc = [], []
            for h in range(2):
                prf = pr[h * rows : (h + 1) * rows].astype(F32)
                t = prf * gp[h * rows : (h + 1) * rows]
                s = (t - prf * jnp.sum(t, 0, keepdims=True)).astype(BF16)
                gsc.append(s)
                parts.append(dot(k_t[h * HEAD_DIM : (h + 1) * HEAD_DIM], s))
            gv = dot(pr, go)
            gv = jnp.where(first_head, gv[:rows], gv[rows:]).astype(BF16)
            gk = dot(jnp.concatenate(gsc, 0), q2)
            gk = jnp.where(first_head, gk[:rows], gk[rows:]).astype(BF16)
            gq = (jnp.concatenate(parts, 0).T * HEAD_DIM**-0.5).astype(BF16)
            r.proj[pair_of(i, p, 0)] = gq
            r.proj[pair_of(i, p, 1)] = gk
            r.proj[pair_of(i, p, 2)] = gv
            at = pl.ds(pl.multiple_of(p * 128, 128), 128)
            r.gsum[16:24, at] += gq.astype(F32).reshape(-1, 8, 128).sum(0)
            r.gsum[24:32, at] += gv.astype(F32).reshape(-1, 8, 128).sum(0)

    groups = width // 256

    def emit_group(g):
        cols = [slice(b * width + g * 256, b * width + (g + 1) * 256) for b in range(3)]
        emit(QKV, g, dot(r.normed[...], jnp.concatenate([r.proj[:, c] for c in cols], 1), TN))

    for g in range(groups):
        for p in (2 * g, 2 * g + 1):
            back_pair(p)
            yield
        emit_group(g)
        yield

    def first_back(i, at, ds):
        m = wide_mask(i, at)
        xhat, rstd = normal(start_of(i, at, m))
        g = r.mlp[ds, :]
        add_sum(0, g * xhat)
        add_sum(1, g)
        gx = g * vec(0)
        gst = r.gs[ds, :] + rstd * (
            gx - jnp.mean(gx, -1, keepdims=True) - xhat * jnp.mean(gx * xhat, -1, keepdims=True)
        )
        add_sum(14, gst * m)
        r.ingrad[i, pl.ds(at, tile), :] = (gst * (1.0 - m)).astype(BF16)

    for i in range(images):
        ds = pl.ds(i * rows, rows)
        r.mlp[ds, :] = dot(r.proj[ds, :], r.w_qkv[...], NT)
        yield
        row_tiles(first_back, i, i + 1)
        yield
    r.gvec[...] = r.gsum[...].reshape(16, 8, width).sum(1)
    yield


class Refs:
    def __init__(self, *groups):
        for group in groups:
            self.__dict__.update(group._asdict())


class Weights(NamedTuple):
    w_qkv: object
    w_out: object
    w_fc1: object
    w_fc2: object


class Rows(NamedTuple):
    tok: object
    mask: object
    cot: object
    vec: object
    out: object
    ingrad: object
    gvec: object


class Work(NamedTuple):
    gsum: object
    dead: object
    live: object
    normed: object
    proj: object
    probs: object
    att: object
    branch: object
    mid: object
    sec: object
    gm: object
    mlp: object
    gs: object
    act: object
    gh: object
    gatt: object


def plain_kernel(dims, tok, mask, cot, qkv, out_w, fc1, fc2, vec, out, ingrad, *refs):
    grads, gvec, work = refs[:4], refs[4], refs[5:]
    rows = Rows(tok, mask, cot, vec, out, ingrad, gvec)
    r = Refs(Weights(qkv, out_w, fc1, fc2), rows, Work(*work))
    width = dims[2]

    def emit(kind, u, value):
        value = value.astype(BF16)
        if kind == FC1:
            grads[FC1][:, pl.ds(pl.multiple_of(u * width, width), width)] = value
        elif kind == FC2:
            grads[FC2][pl.ds(pl.multiple_of(u * width, width), width), :] = value
        elif kind == OUT:
            grads[OUT][...] = value
        else:
            for b in range(3):
                c = b * width + u * 256
                grads[QKV][:, c : c + 256] = value[:, b * 256 : (b + 1) * 256]

    for _ in layer(dims, r, emit, lambda t: t):
        pass


def scratch(dims):
    images, rows, width, ff = dims
    total = images * rows
    low = lambda *s: pltpu.VMEM(s, BF16)
    full = lambda *s: pltpu.VMEM(s, F32)
    return Work(
        gsum=full(128, width),
        dead=full(rows, rows),
        live=full(rows, 128),
        normed=low(total, width),
        proj=low(total, 3 * width),
        probs=low(images * (width // 128), 2 * rows, rows),
        att=low(total, width),
        branch=low(total, width),
        mid=full(total, width),
        sec=low(total, width),
        gm=low(total, width),
        mlp=full(total, width),
        gs=full(total, width),
        act=low(total, width),
        gh=low(total, width),
        gatt=low(total, width),
    )


def plain_layer(tok, mask, cot, w_qkv, w_out, w_fc1, w_fc2, vec):
    images, seq_len, width = tok.shape
    dims = (images, used_rows(seq_len), width, w_fc1.shape[1])
    shape = jax.ShapeDtypeStruct
    return pl.pallas_call(
        functools.partial(plain_kernel, dims),
        out_shape=(
            shape(tok.shape, BF16),
            shape(tok.shape, BF16),
            shape(w_qkv.shape, BF16),
            shape(w_out.shape, BF16),
            shape(w_fc1.shape, BF16),
            shape(w_fc2.shape, BF16),
            shape((16, width), F32),
        ),
        in_specs=[pl.BlockSpec(memory_space=pltpu.VMEM)] * 8,
        out_specs=[pl.BlockSpec(memory_space=pltpu.VMEM)] * 7,
        scratch_shapes=list(scratch(dims)),
        compiler_params=pltpu.CompilerParams(
            vmem_limit_bytes=63 << 20
        ),
        name="layer",
    )(tok, mask, cot, w_qkv, w_out, w_fc1, w_fc2, vec)


NZ = 4
PARTS = 12
MESH = pl.DeviceIdType.MESH


class Sems:
    sends = recvs = locals = 0

    def send(self, count=1):
        self.sends += count
        return self.sends - count

    def recv(self, count=1):
        self.recvs += count
        return self.recvs - count

    def both(self, count=1):
        return self.send(), self.recv(count)

    def local(self, count=1):
        self.locals += count
        return self.locals - count


def make_sems():
    s = Sems()
    s.tok, s.mask, s.cot, s.out, s.ingrad = (s.both() for _ in range(5))
    s.vec_z, s.vec_y = s.both(), s.both()
    s.sz, s.sy, s.sx, s.sc = (s.send(4) for _ in range(4))
    s.wz, s.wy, s.wx, s.wc = s.recv(16), s.recv(16), s.recv(32), s.recv(16)
    s.c, s.r1 = (s.send(5), s.recv(5)), (s.send(5), s.recv(PARTS + 1))
    s.r2, s.zr2 = s.both(4), s.both()
    s.za, s.zc, s.zd = s.both(8), s.recv(8), s.both(2)
    s.gx, s.gx_fc2 = s.both(7), s.send()
    s.gc = s.send(4), s.recv(4)
    s.vs, s.vy, s.vz, s.vb = (s.both() for _ in range(4))
    s.l_tok, s.l_mask, s.l_cot, s.l_out, s.l_ingrad = (s.local() for _ in range(5))
    s.l_w, s.l_g = s.local(4), s.local(4)
    return s


SEMS = make_sems()


SCHEDULE = (
    (0, 0), (10,), (11,), (2, 0, 0), (27, 0, 2), (1, 0, 1), (6, 1), (27, 0, 3), (1, 0, 2), (5, 1),
    (6, 2), (2, 0, 1), (2, 1, 0), (27, 1, 2), (9,), (0, 1), (1, 0, 3), (5, 2), (3, 0, 0, 1),
    (27, 1, 3), (3, 0, 1, 0), (1, 1, 1), (2, 0, 2), (3, 0, 2, 0), (3, 0, 1, 1), (1, 1, 2),
    (3, 1, 0, 1), (3, 0, 3, 0), (3, 1, 1, 0), (3, 0, 2, 1), (3, 1, 2, 0), (2, 2, 0), (27, 2, 2),
    (1, 2, 1), (1, 1, 3), (3, 2, 0, 1), (7, 0), (2, 0, 3), (3, 2, 1, 0), (3, 1, 3, 0), (2, 1, 1),
    (27, 2, 3), (2, 1, 2), (1, 2, 2), (3, 0, 3, 1), (3, 1, 1, 1), (7, 1), (3, 1, 2, 1), (4, 0, 0),
    (25, 0), (0, 2), (2, 2, 1), (3, 2, 2, 0), (1, 2, 3), (5, 3), (6, 3), (0, 3), (2, 1, 3), (0, 4),
    (0, 5), (0, 6), (0, 7), (7, 2), (2, 2, 2), (3, 2, 1, 1), (0, 8), (27, 3, 2), (1, 3, 1),
    (3, 2, 3, 0), (3, 1, 3, 1), (0, 9), (0, 10), (2, 2, 3), (4, 1, 0), (25, 1), (0, 11), (27, 3, 3),
    (0, 12), (8,), (0, 13), (3, 2, 2, 1), (1, 3, 2), (2, 3, 0), (3, 3, 1, 0), (3, 2, 3, 1),
    (3, 3, 2, 0), (1, 3, 3), (2, 3, 1), (3, 3, 0, 1), (4, 2, 0), (4, 3, 0), (25, 2), (25, 3),
    (0, 14), (3, 3, 3, 0), (0, 15), (0, 16), (3, 3, 1, 1), (0, 17), (2, 3, 2), (0, 18), (0, 19),
    (0, 20), (12, 1), (3, 3, 2, 1), (0, 21), (2, 3, 3), (12, 0), (4, 3, 1), (0, 22), (0, 23),
    (0, 24), (0, 25), (3, 3, 3, 1), (0, 26), (0, 27), (0, 28), (12, 3), (13, 1), (0, 29), (4, 3, 2),
    (0, 30), (12, 2), (0, 31), (0, 32), (0, 33), (13, 0), (0, 34), (0, 35), (12, 5), (0, 36),
    (0, 37), (12, 4), (4, 3, 3), (0, 38), (13, 2), (0, 39), (0, 40), (13, 3), (26, 3), (0, 41),
    (14, 0), (0, 42), (0, 43), (0, 44), (12, 7), (26, 1), (0, 45), (12, 6), (13, 5), (0, 46),
    (13, 4), (0, 47), (14, 2), (0, 48), (26, 5), (0, 49), (18, 0), (0, 50), (13, 6), (12, 8),
    (0, 51), (13, 7), (0, 52), (18, 1), (0, 53), (14, 4), (12, 9), (0, 54), (26, 7), (0, 55),
    (18, 2), (14, 6), (0, 56), (12, 10), (0, 57), (0, 58), (0, 59), (19, 0), (0, 60), (12, 11),
    (12, 12), (13, 8), (15, 2, 0), (0, 61), (19, 1), (0, 62), (0, 63), (0, 64), (20,), (19, 2),
    (15, 3, 0), (13, 9), (26, 8), (16, 2, 0), (26, 9), (13, 10), (15, 1, 0), (15, 0, 0), (13, 11),
    (21,), (26, 10), (13, 12), (22,), (15, 0, 2), (15, 0, 1), (16, 3, 0), (16, 1, 0), (15, 0, 3),
    (16, 0, 0), (23,), (16, 0, 2), (16, 0, 1), (16, 0, 3), (24,),
)


class More(NamedTuple):
    vecs: object
    U: object
    RC: object
    R1: object
    R2: object
    ZA: object
    ZB: object
    ZC: object
    ZD: object
    ZR2: object
    XS: object
    XR: object
    gv0: object
    gv1: object
    gv2: object
    gv3: object
    gv4: object
    ss: object
    rs: object
    ls: object
    wide: object


def linked_kernel(dims, tokens, masks, cotangent, *refs):
    w_in, in_vec, o_out, o_ingrad, g_outs, gvec_out = (
        *(refs[:4], refs[4], refs[5]),
        *(refs[6], refs[7:11], refs[11]),
    )
    refs = refs[12:]
    w, rows, g_held = refs[:4], Rows(*refs[4:11]), refs[11:15]
    r = Refs(Weights(*w), rows, Work(*refs[15:31]), More(*refs[31:]))
    images, rows, width, ff = dims
    d, s = lax.axis_index("dp"), lax.axis_index("seq")
    z, y, x, c = d // 2, d % 2, s // 2, s % 2
    slots = tokens.shape[1]
    upper = z // 2
    mate, inner, outer = z + 1 - 2 * (z % 2), (z + 1) // 2 % 2 == 1, (z + 1) // 2 % 2 == 0
    far = (z, mate, 2 - upper, 3 - 3 * upper)
    to_c, to_x, to_y = (d, x * 2 + 1 - c), (d, (1 - x) * 2 + c), (z * 2 + 1 - y, s)

    def to_z(k):
        return (lax.rem(z + k, NZ) * 2 + y, s)

    def to_s(k):
        return (d, lax.rem(s + k, 4))

    def at_z(zz):
        return (zz * 2 + y, s)

    def copy(pair, src, dst, dev):
        return pltpu.make_async_remote_copy(
            src, dst, r.ss.at[pair[0]], r.rs.at[pair[1]], device_id=dev, device_id_type=MESH
        )

    def send(pair, src, dst, dev):
        copy(pair, src, dst, dev).start()

    def got(pair, dst):
        copy((0, pair[1]), dst, dst, to_c).wait_recv()

    def left(sem, src):
        copy((sem, 0), src, src, to_c).wait_send()

    def local(sem, src, dst):
        pltpu.make_async_copy(src, dst, r.ls.at[sem]).start()

    def settled(sem, dst):
        pltpu.make_async_copy(dst, dst, r.ls.at[sem]).wait()

    barrier = pltpu.get_barrier_semaphore()
    peers = [to_y] + [to_s(k) for k in (1, 2, 3)] + [to_z(k) for k in (1, 2, 3)]
    for dev in peers:
        pl.semaphore_signal(barrier, inc=1, device_id=dev, device_id_type=MESH)
    pl.semaphore_wait(barrier, len(peers))

    def band(t):
        return pl.ds(pl.multiple_of(t * slots, 64), slots)

    def scatter(pair, sem, src, dst, lo=0, hi=images):
        for k in (2, 1, 3):
            t = lax.rem(s + k, 4)
            rows_out = src.at[pl.ds(t * images + lo, hi - lo)]
            send(pair, rows_out, dst.at[lo:hi, band(s)], to_s(k))
        local(sem, src.at[pl.ds(s * images + lo, hi - lo)], dst.at[lo:hi, band(s)])

    def give_back(pair, sem, src, dst, i):
        at = pl.ds(s * images + i, 1)
        for k in (2, 1, 3):
            send(pair, src.at[i : i + 1, band(lax.rem(s + k, 4))], dst.at[at], to_s(k))
        local(sem, src.at[i : i + 1, band(s)], dst.at[at])

    def block(a, zz, yy):
        return (zz * 2 + yy) * w_in[a].shape[0]

    def cut(ref, a, base, kind, mine=True):
        n, m = w_in[a].shape
        half = n // 2
        if kind == 2:
            at = base + (c if mine else 1 - c) * half
            return ref.at[pl.ds(pl.multiple_of(at, 16), half)]
        at, xx = base + c * half, x if mine else 1 - x
        if a == FC2:
            q = half // 4
            if kind == 0:
                return ref.at[pl.ds(pl.multiple_of(at + x * q, 16), half - q)]
            return ref.at[pl.ds(pl.multiple_of(at + xx * (half - q), 16), q)]
        q = m // 4 if a == FC1 else m // 6
        rs = pl.ds(pl.multiple_of(at, 16), half)
        if kind == 0:
            return ref.at[rs, pl.ds(pl.multiple_of(x * q, 128), m - q)]
        return ref.at[rs, pl.ds(pl.multiple_of(xx * (m - q), 128), q)]

    def piece(a, zz, yy, kind, mine=True):
        return cut(w[a], a, block(a, zz, yy), kind, mine)

    def own_piece(a):
        return cut(w_in[a], a, 0, 0)

    def w_own(a):
        n = w_in[a].shape[0]
        at = pl.ds(pl.multiple_of(block(a, z, y), 16), n)
        local(SEMS.l_w + a, w_in[a], w[a].at[at])

    def w_y0(a):
        send((SEMS.sy + a, SEMS.wy + 4 * a), own_piece(a), piece(a, z, y, 0), to_y)

    def w_z(a):
        pair = (SEMS.sz + a, SEMS.wz + 4 * a + 1)
        send(pair, own_piece(a), piece(a, z, y, 0), at_z(mate))
        pair = (SEMS.sz + a, SEMS.wz + 4 * a + jnp.where(inner, 2, 3))
        send(pair, own_piece(a), piece(a, z, y, 0), at_z(far[2]))

    def w_share(a, k, other):
        p = piece(a, far[k], 1 - y if other else y, 1)
        send((SEMS.sx + a, SEMS.wx + 8 * a + 4 * other + k), p, p, to_x)

    def w_zr(a, k):
        p = piece(a, far[k], y, 0)
        if k == 1:
            got((0, SEMS.wz + 4 * a + k), p)
        else:
            pl.when(outer)(lambda: got((0, SEMS.wz + 4 * a + k), p))
        send((SEMS.sy + a, SEMS.wy + 4 * a + k), p, p, to_y)
        w_share(a, k, 0)

    def w_on(a, k):
        p = piece(a, far[k], y, 0)

        @pl.when(inner)
        def _():
            got((0, SEMS.wz + 4 * a + k), p)
            send((SEMS.sz + a, SEMS.wz + 4 * a + k), p, p, at_z(mate))

    def w_yr(a, k):
        got((0, SEMS.wy + 4 * a + k), piece(a, far[k], 1 - y, 0))
        w_share(a, k, 1)

    def w_xr(a, k, other):
        yy = 1 - y if other else y
        got((0, SEMS.wx + 8 * a + 4 * other + k), piece(a, far[k], yy, 1, False))
        p = piece(a, far[k], yy, 2)
        send((SEMS.sc + a, SEMS.wc + 4 * a + (k if a == FC2 else 0)), p, p, to_c)

    def w_cr(a, k):
        n = w_in[a].shape[0]
        n = (n if k else n // 2) if a == FC2 else 7 * n // 2
        got((0, SEMS.wc + 4 * a + k), w[a].at[0:n])

    def w_left(a):
        n, m = w_in[a].shape
        half = n // 2
        q = half // 4 if a == FC2 else m // 4 if a == FC1 else m // 6

        def share(count, far_end):
            if a == FC2:
                return w[a].at[0 : count * (q if far_end else half - q)]
            return w[a].at[0 : count * half, 0 : q if far_end else m - q]

        pl.when(outer)(lambda: left(SEMS.sz + a, share(2, False)))
        pl.when(inner)(lambda: left(SEMS.sz + a, share(4, False)))
        left(SEMS.sy + a, share(4, False))
        left(SEMS.sx + a, share(7, True))
        left(SEMS.sc + a, w[a].at[0 : 7 * half])

    def unit_of(t):
        return far[t]

    def part_of(kind, t):
        return (9 + t, 8, 2 * t + 1, 2 * t)[kind]

    def x_first(q):
        return q in (2, 4, 6)

    def halves(q):
        return (min(q, 11), *((0, 2) if q < 11 else (q - 11, q - 10)))

    step, half, third = width // 16, width // 2, width // 4

    def c_sem(part):
        return 4 if part == 12 else part % 4

    def emit(kind, t, value):
        q = part_of(kind, t)
        slot = q % 4
        value = value.astype(BF16)
        for cc in range(2):
            for yy in range(2):
                if kind == FC2:
                    pieces = [(yy * half + cc * third, 0, third)]
                else:
                    pieces = [(((zz * 2 + yy) * 2 + cc) * step, zz * step, step) for zz in range(4)]
                for src, dst, size in pieces:
                    for xx in range(2):
                        v = value[src : src + size, xx * half : (xx + 1) * half]
                        r.U[slot, cc, yy, xx, dst : dst + size, :] = v
        for part in (q,) if q < 11 else (11, 12):
            _, lo, hi = halves(part)
            src, dst = r.U.at[slot, 1 - c, :, lo:hi], r.RC.at[slot, :, lo:hi]
            send((SEMS.c[0] + c_sem(part), SEMS.c[1] + c_sem(part)), src, dst, to_c)

    def g_1(part):
        q, lo, hi = halves(part)
        slot = q % 4
        got((0, SEMS.c[1] + c_sem(part)), r.RC.at[slot, :, lo:hi])

        def add(side):
            if x_first(q):

                @pl.loop(0, 2)
                def _(k):
                    r.U[slot, c, k, side] = r.U[slot, c, k, side] + r.RC[slot, k, side]

            else:

                @pl.loop(lo, hi)
                def _(k):
                    r.U[slot, c, side, k] = r.U[slot, c, side, k] + r.RC[slot, side, k]

        pair = (SEMS.r1[0] + c_sem(part), SEMS.r1[1] + part)
        if x_first(q):
            add(1 - x)
            send(pair, r.U.at[slot, c, :, 1 - x], r.R1.at[q], to_x)
            add(x)
        else:
            add(1 - y)
            send(pair, r.U.at[slot, c, 1 - y, lo:hi], r.R1.at[q, lo:hi], to_y)
            add(y)

    def z_slot(q):
        return unit_of(q // 2) if q < 8 else q - 4

    def steps(at, count=1):
        return pl.ds(pl.multiple_of(at * step, 16), count * step)

    def g_2(part):
        q, lo, hi = halves(part)
        got((0, SEMS.r1[1] + part), r.R1.at[q, lo:hi])
        left(SEMS.c[0] + c_sem(part), r.RC.at[q % 4, :, lo:hi])

        @pl.loop(lo, hi)
        def _(k):
            if x_first(q):
                r.R1[q, k] = r.R1[q, k] + r.U[q % 4, c, k, x]
            else:
                r.R1[q, k] = r.R1[q, k] + r.U[q % 4, c, y, k]

        left(SEMS.r1[0] + c_sem(part), r.R1.at[q, lo:hi])
        if q in (0, 2, 4, 6):
            side, dev = (1 - y, to_y) if x_first(q) else (1 - x, to_x)
            send((SEMS.r2[0], SEMS.r2[1] + q // 2), r.R1.at[q, side], r.R2.at[q // 2], dev)
            return
        if part > 10:
            for k in (2, 1, 3):
                src = r.R1.at[q, lo, steps(lax.rem(z + k, NZ))]
                send((SEMS.zd[0], SEMS.zd[1] + lo), src, r.ZD.at[lo, k - 1], to_z(k))
            return
        j = z_slot(q)
        pair = (SEMS.za[0], SEMS.za[1] + j)

        @pl.when(outer)
        def _():
            src = r.R1.at[q, lo:hi, steps(1 - upper, 3)]
            send(pair, src, r.ZA.at[j, lo:hi], at_z(mate))

        @pl.when(inner)
        def _():
            send(pair, r.R1.at[q, lo:hi, steps(mate)], r.ZB.at[j, lo:hi], at_z(mate))

    def g_7(part):
        q, lo, hi = halves(part)
        j = z_slot(q)

        @pl.when(inner)
        def _():
            got((0, SEMS.za[1] + j), r.ZA.at[j, lo:hi])
            across = steps(1 - upper, 2)
            own = r.R1[q, lo:hi, steps(2 - 2 * upper, 2)]
            r.ZA[j, lo:hi, across] = r.ZA[j, lo:hi, across] + own
            for i in range(2):
                src = r.ZA.at[j, lo:hi, steps(1 - upper + i)]
                pair = (SEMS.za[0], SEMS.zc + j)
                send(pair, src, r.ZC.at[j, lo:hi], at_z(2 - 2 * upper + i))

    def g_3(q):
        t = q // 2
        got((0, SEMS.r2[1] + t), r.R2.at[t])
        r.R2[t] = r.R2[t] + r.R1[q, y if x_first(q) else x]
        if t:
            u = unit_of(t)
            k = lax.rem(u + NZ - z, NZ)
            send(SEMS.zr2, r.R2.at[t], r.ZR2.at[k - 1], at_z(u))

    def g_4(kind, i):
        if kind == FC2:
            got(SEMS.zr2, r.ZR2)
            total = r.R2[0].astype(F32)
            for k in range(3):
                total = total + r.ZR2[k].astype(F32)
            g = g_held[FC2]
            g[c, x, 0] = total.astype(BF16)
            send((SEMS.gx_fc2, SEMS.gx[1]), g.at[c, x], g.at[c, x], to_x)
            return
        for part in {FC1: (1, 3, 5, 7), OUT: (8,), QKV: (9 + i,)}[kind]:
            q, lo, hi = halves(part)
            j = z_slot(q)
            if part > 10:
                got((0, SEMS.zd[1] + lo), r.ZD.at[lo])
                total = r.R1[q, lo, steps(z)].astype(F32)
                for k in range(3):
                    total = total + r.ZD[lo, k].astype(F32)
                r.XS[j, lo] = total.astype(BF16)
                continue
            got((0, SEMS.zc + j), r.ZC.at[j, lo:hi])

            def put(near, at):
                total = r.R1[q, lo:hi, steps(z)].astype(F32) + near[j, lo:hi, at].astype(F32)
                r.XS[j, lo:hi] = (total + r.ZC[j, lo:hi].astype(F32)).astype(BF16)

            @pl.when(outer)
            def _():
                got((0, SEMS.za[1] + j), r.ZB.at[j, lo:hi])
                put(r.ZB, slice(None))

            @pl.when(inner)
            def _():
                put(r.ZA, steps(2 * upper))

        sem, at = x_span(kind, i)
        send((SEMS.gx[0], sem), r.XS.at[at], r.XR.at[at], to_x)

    def x_span(kind, i):
        if kind == FC1:
            return SEMS.gx[1] + 1, (slice(0, 4),)
        q, lo, hi = halves(8 if kind == OUT else 9 + i)
        return SEMS.gx[1] + (2 if kind == OUT else 3 + i), (q - 4, slice(lo, hi))

    def g_5(kind, i):
        g = g_held[kind]
        if kind == FC2:
            got(SEMS.gx, g.at[c, 1 - x])
        else:
            sem, at = x_span(kind, i)
            got((0, sem), r.XR.at[at])
            units = range(4) if kind == FC1 else (at[0],)
            for n, j in enumerate(units):
                sides = (0, 1) if kind == FC1 else range(at[1].start, at[1].stop)
                for xx in sides:
                    g[c, xx, min(i, 2) + n] = r.XS[j, xx] + r.XR[j, xx]
        if kind != QKV or i == 3:
            mine = g_outs[kind].at[c]
            send((SEMS.gc[0] + kind, SEMS.gc[1] + kind), g.at[c], mine, to_c)
            local(SEMS.l_g + kind, g.at[c], mine)

    def v_part(p):
        return slice(p // 2 * 8, p // 2 * 8 + 8), slice(p % 2 * half, (p % 2 + 1) * half)

    def v_1():
        for p in range(4):
            r.gv0[p] = r.gvec[v_part(p)]
        r.gv1[s] = r.gv0[s]
        for k in (2, 1, 3):
            send(SEMS.vs, r.gv0.at[lax.rem(s + k, 4)], r.gv1.at[s], to_s(k))

    def v_2():
        got(SEMS.vs, r.gv1.at[0:3])
        r.gv2[0] = r.gv1[0] + r.gv1[1] + r.gv1[2] + r.gv1[3]
        send(SEMS.vy, r.gv2.at[0], r.gv2.at[1], to_y)

    def v_3():
        got(SEMS.vy, r.gv2.at[1])
        r.gv3[z] = r.gv2[0] + r.gv2[1]
        for k in (2, 1, 3):
            send(SEMS.vz, r.gv3.at[z], r.gv3.at[z], to_z(k))

    def v_4():
        got(SEMS.vz, r.gv3.at[0:3])
        r.gv4[s] = (r.gv3[0] + r.gv3[1]) + (r.gv3[2] + r.gv3[3])
        for k in (2, 1, 3):
            send(SEMS.vb, r.gv4.at[s], r.gv4.at[s], to_s(k))

    def v_5():
        got(SEMS.vb, r.gv4.at[0:3])
        n = width // (2 * NZ)
        row = lax.broadcasted_iota(jnp.int32, (half, 128), 0)
        lane = lax.broadcasted_iota(jnp.int32, (half, 128), 1)
        for top in range(2):
            total = jnp.zeros((8, 128), F32)
            for side in range(2):
                pick = jnp.where((row + side * half == lane + d * n) & (lane < n), 1.0, 0.0)
                part = lax.dot(
                    r.gv4[2 * top + side],
                    pick.astype(F32),
                    precision=lax.Precision.HIGHEST,
                    preferred_element_type=F32,
                )
                total = total + part
            gvec_out[top * 8 : top * 8 + 8, :] = total

    def vectors_in():
        total = jnp.zeros((16, width), F32)
        n = width // (2 * NZ)
        lane = lax.broadcasted_iota(jnp.int32, (128, width), 0)
        col = lax.broadcasted_iota(jnp.int32, (128, width), 1)
        for k in range(2 * NZ):
            pick = jnp.where((col == lane + k * n) & (lane < n), 1.0, 0.0).astype(BF16)
            total = total + dot(r.vecs[k % 2, k // 2].astype(BF16), pick)
        r.vec[...] = total

    def vec_z():
        got(SEMS.vec_z, r.vecs.at[y, 0:3])
        send(SEMS.vec_y, r.vecs.at[y], r.vecs.at[y], to_y)

    def vec_y():
        got(SEMS.vec_y, r.vecs.at[1 - y])
        vectors_in()

    three = slice(0, 3 * slots)

    def tokens_in():
        got(SEMS.mask, r.mask.at[:, three])
        settled(SEMS.l_mask, r.mask.at[:, 0:slots])
        got(SEMS.tok, r.tok.at[:, three])
        settled(SEMS.l_tok, r.tok.at[:, 0:slots])

    def cot_out(i):
        scatter(SEMS.cot, SEMS.l_cot, cotangent, r.cot, i, i + 1)

    def cot_in():
        got(SEMS.cot, r.cot.at[:, three])
        settled(SEMS.l_cot, r.cot.at[:, 0:slots])

    def out_back(i):
        give_back(SEMS.out, SEMS.l_out, r.out, o_out, i)

    def ingrad_back(i):
        give_back(SEMS.ingrad, SEMS.l_ingrad, r.ingrad, o_ingrad, i)

    def own_in(a):
        settled(SEMS.l_w + a, w[a].at[0 : w_in[a].shape[0]])

    own = r.vecs.at[y, z]
    own[...] = jnp.zeros((16, 128), F32)
    own[0 : in_vec.shape[0], 0 : in_vec.shape[1]] = in_vec[...].astype(F32)
    for k in (1, 2, 3):
        send(SEMS.vec_z, own, own, to_z(k))
    marks = jnp.where(masks[...] == 1, 1.0, 0.0).astype(F32).T
    for i in range(masks.shape[0]):
        r.wide[i] = jnp.broadcast_to(marks[:, i : i + 1], (slots, 128)).astype(BF16)
    scatter(SEMS.tok, SEMS.l_tok, tokens, r.tok)
    scatter(SEMS.mask, SEMS.l_mask, r.wide, r.mask)
    w_y0(QKV)
    w_z(QKV)
    for a in (QKV, OUT, FC1, FC2):
        w_own(a)
    piece_done = layer(dims, r, emit, unit_of)

    def go(k):
        next(piece_done)

    table = (go, w_zr, w_yr, w_xr, w_cr, w_z, w_y0, cot_out, cot_in, tokens_in, vec_z, vec_y)
    table += (g_1, g_2, g_3, g_4, g_5, None, out_back, ingrad_back)
    table += (v_1, v_2, v_3, v_4, v_5, own_in, g_7, w_on)
    for op, *at in SCHEDULE:
        table[op](*at)
    for _ in piece_done:
        pass
    bands = (SEMS.out, SEMS.l_out, o_out), (SEMS.ingrad, SEMS.l_ingrad, o_ingrad)
    for pair, sem, dst in bands:
        got(pair, dst.at[0 : 3 * images])
        settled(sem, dst.at[0:images])
    sent = [(SEMS.tok, r.tok), (SEMS.mask, r.mask), (SEMS.cot, r.cot)]
    sent = [(pair, ref.at[:, three]) for pair, ref in sent]
    sent += [(pair, dst.at[0 : 3 * images]) for pair, _, dst in bands]
    sent += [(SEMS.vec_z, r.vecs.at[0, 0:3]), (SEMS.vec_y, r.vecs.at[0])]
    sent += [(SEMS.r2, r.R2), (SEMS.za, r.ZA.at[0:7]), (SEMS.zd, r.ZD), (SEMS.zr2, r.ZR2), (SEMS.gx, r.XS)]
    sent += [((SEMS.gx_fc2,), g_held[FC2].at[c, x])]
    sent += [((SEMS.gc[0] + a,), g_held[a].at[c]) for a in range(4)]
    sent += [(SEMS.vs, r.gv0.at[0:3]), (SEMS.vy, r.gv2.at[0])]
    sent += [(SEMS.vz, r.gv3.at[0:3]), (SEMS.vb, r.gv4.at[0:3])]
    for pair, src in sent:
        left(pair[0], src)
    for a in range(4):
        w_left(a)
        settled(SEMS.l_g + a, g_outs[a].at[c])
        got((0, SEMS.gc[1] + a), g_outs[a].at[1 - c])


def linked_layer(tokens, masks, cotangent, weights):
    count, slots, width = tokens.shape
    images, seq_len = count // 4, slots * 4
    dims = (images, used_rows(seq_len), width, weights[2].shape[1])
    shape = jax.ShapeDtypeStruct
    low = lambda *s: pltpu.VMEM(s, BF16)
    full = lambda *s: pltpu.VMEM(s, F32)
    sems = lambda n: pltpu.SemaphoreType.DMA((n,))
    step, half, third = width // 16, width // 2, width // 4
    hbm = pl.BlockSpec(memory_space=pl.ANY)
    vmem = pl.BlockSpec(memory_space=pltpu.VMEM)
    sums = [(2, 2, 3, step, half), (2, 2, 1, step, half), (2, 2, 4, step, half)]
    sums += [(2, 2, 1, third, half)]
    held = [low(w.shape[0] * 2 * NZ, w.shape[1]) for w in weights[:4]]
    held += [low(images, seq_len, w) for w in (width, 128, width)]
    held += [full(16, width)] + [low(images, seq_len, width)] * 2 + [full(16, width)]
    held += [low(*v) for v in sums]
    more = More(
        vecs=full(2, NZ, 16, 128),
        U=low(4, 2, 2, 2, third, half),
        RC=low(4, 2, 2, third, half),
        R1=low(PARTS, 2, third, half),
        R2=low(4, third, half),
        ZA=low(8, 2, 3 * step, half),
        ZB=low(8, 2, step, half),
        ZC=low(8, 2, step, half),
        ZD=low(2, 3, step, half),
        ZR2=low(3, third, half),
        XS=low(8, 2, step, half),
        XR=low(8, 2, step, half),
        gv0=full(4, 8, half),
        gv1=full(4, 8, half),
        gv2=full(2, 8, half),
        gv3=full(4, 8, half),
        gv4=full(4, 8, half),
        ss=sems(SEMS.sends),
        rs=sems(SEMS.recvs),
        ls=sems(SEMS.locals),
        wide=low(count, slots, 128),
    )
    return pl.pallas_call(
        functools.partial(linked_kernel, dims),
        out_shape=(
            shape(tokens.shape, BF16),
            shape(tokens.shape, BF16),
            *(shape(v, BF16) for v in sums),
            shape((16, 128), F32),
        ),
        in_specs=[hbm, vmem] + [hbm] * 5 + [vmem],
        out_specs=[hbm] * 6 + [vmem],
        scratch_shapes=held + list(scratch(dims)) + list(more),
        compiler_params=pltpu.CompilerParams(
            collective_id=0,
            has_side_effects=True,
            vmem_limit_bytes=63 << 20,
        ),
        name="layer",
    )(tokens, masks, cotangent, *weights[:4], weights[4].T)


def sgd_step(gradient, master, moment, teacher, step_rate, decay_rate):
    pulled = gradient + decay_rate * master
    moment_new = momentum_rate * moment + pulled
    weight_new = master - step_rate * (pulled + momentum_rate * moment_new)
    teacher_new = teacher_rate * teacher + (1.0 - teacher_rate) * weight_new
    return (weight_new, moment_new, teacher_new, weight_new.astype(BF16))


def on_device(tokens, masks, cotangent, *rest):
    weights, masters, moments, teachers = rest[:5], rest[5:10], rest[10:15], rest[15:20]
    images, slots, width = tokens.shape
    step = (weights, masters, moments, teachers)
    if (lax.axis_size("dp"), lax.axis_size("seq")) == (2 * NZ, 4):
        out, ingrad, *sums, gvec = linked_layer(tokens, masks, cotangent, weights)
        return finish(out, ingrad, sums, gvec, *step)
    wide = jnp.broadcast_to((masks == 1).astype(BF16)[..., None], (images, slots, 128))
    full = [lax.all_gather(w, "dp", axis=0, tiled=True) for w in weights]
    vec = jnp.zeros((16, width), F32).at[: full[4].shape[1]].set(full[4].astype(F32).T)
    tok, mask, cot = (
        lax.all_to_all(v, "seq", 0, 1, tiled=True) for v in (tokens, wide, cotangent)
    )
    out, ingrad, *grads, gvec = plain_layer(tok, mask, cot, *full[:4], vec)
    out, ingrad = (lax.all_to_all(v, "seq", 1, 0, tiled=True) for v in (out, ingrad))
    sums = [lax.psum_scatter(g, "dp", scatter_dimension=0, tiled=True) for g in grads]
    sums = [lax.psum(g, "seq") for g in sums]
    gvec = lax.psum(gvec, ("dp", "seq"))
    part = width // lax.axis_size("dp")
    own = lax.dynamic_slice(gvec, (0, lax.axis_index("dp") * part), (16, part))
    return finish(out, ingrad, sums, own, *step)


def whole(kind, ref):
    if len(ref.shape) == 2:
        return ref[...].astype(F32)
    units, half = ref.shape[2], ref.shape[4]
    if kind != QKV:
        pieces = [ref[0, xx, u] for u in range(units) for xx in range(2)]
    else:
        at, cut = range(units), half * 2 // 3
        pieces = [ref[0, 0, u, :, 0:cut] for u in at]
        for u in at:
            pieces += [ref[0, 0, u, :, cut:half], ref[0, 1, u, :, 0 : half - cut]]
        pieces += [ref[0, 1, u, :, half - cut : half] for u in at]
    return jnp.concatenate(pieces, 1).astype(F32)


def update_kernel(steps, *refs):
    ins, outs = refs[:22], refs[22:]
    for k in range(5):
        n, m = ins[5 + k].shape
        g = whole(k, ins[k])[:n, :m]
        got = sgd_step(g, *(ins[5 * j + k][...] for j in (1, 2, 3)), *steps[k])
        for ref, v in zip((outs[k], *(outs[5 * j + k] for j in (1, 2, 3, 4))), (g, *got)):
            ref[...] = v
    outs[25][...] = ins[20][...]
    outs[26][...] = ins[21][...].astype(F32)


def finish(out, ingrad, sums, own, weights, masters, moments, teachers):
    images, slots, width = out.shape
    part = width // lax.axis_size("dp")
    image_total = images * lax.axis_size("dp")
    big = (matrix_rate / math.sqrt(image_total), matrix_decay)
    small = (vector_rate / math.sqrt(image_total), 0.0)
    steps = (big, big, big, big, small)
    count = part // 16
    if part % 32 or images % count:
        sums = [g.astype(F32) for g in (*sums, own[: weights[4].shape[1]].T)]
        old = zip(sums, masters, moments, teachers, steps)
        ups = [sgd_step(*v, *rates) for *v, rates in old]
        return (out, ingrad.astype(F32), *sums, *(u[j] for j in range(4) for u in ups))

    def spec(a):
        if a.ndim == 5:
            block = (1, 2, a.shape[2], a.shape[3] * 2 // count, a.shape[4])
            return pl.BlockSpec(block, lambda i: (i // (count // 2), 0, 0, i % (count // 2), 0))
        if a.ndim == 2 and a.shape[0] < part:
            return pl.BlockSpec(a.shape, lambda i: (0, 0))
        rest = (0,) * (a.ndim - 1)
        return pl.BlockSpec((a.shape[0] // count, *a.shape[1:]), lambda i: (i, *rest))

    flip = lambda group: (*group[:4], group[4].T)
    args = [*sums, own, *flip(masters), *flip(moments), *flip(teachers), out, ingrad]
    shape = jax.ShapeDtypeStruct
    outs = [shape(m.shape, F32) for _ in range(4) for m in flip(masters)]
    outs += [shape(m.shape, BF16) for m in flip(masters)]
    outs += [shape(out.shape, BF16), shape(out.shape, F32)]
    res = pl.pallas_call(
        functools.partial(update_kernel, steps),
        grid=(count,),
        out_shape=outs,
        in_specs=[spec(a) for a in args],
        out_specs=[spec(a) for a in outs],
        compiler_params=pltpu.CompilerParams(vmem_limit_bytes=60 << 20),
        name="update",
    )(*args)
    res = [v.T if k % 5 == 4 and k < 25 else v for k, v in enumerate(res)]
    return (res[25], res[26], *res[:25])


def solution(mesh):
    band = P("dp", "seq", None)
    rows = P("dp", None)
    return jax.shard_map(
        on_device,
        mesh=mesh,
        in_specs=(band, P("dp", "seq"), band) + (rows,) * 20,
        out_specs=(band, band) + (rows,) * 25,
        check_vma=False,
    )
```

```python
import functools
import math
from typing import NamedTuple

import jax
import jax.numpy as jnp
from jax import lax
from jax.experimental import pallas as pl
from jax.experimental.pallas import tpu as pltpu
from jax.sharding import PartitionSpec as P

HEADS = 12
HEAD_DIM = 64
GRID = 14
BAND = 4
SLOTS = 64

momentum_rate = 0.9
teacher_rate = 0.75
matrix_rate = 0.003
vector_rate = 0.03
matrix_decay = 0.05

F32 = jnp.float32
BF16 = jnp.bfloat16
TILE = 32
NN = (((1,), (0,)), ((), ()))
NT = (((1,), (1,)), ((), ()))
TN = (((0,), (0,)), ((), ()))
QKV, OUT, FC1, FC2 = range(4)


def dot(a, b, form=NN):
    return lax.dot_general(a, b, form, preferred_element_type=F32)


def is_live(position):
    block = position // SLOTS
    inner = position % SLOTS
    patch = (inner < BAND * GRID) & (BAND * block + inner // GRID < GRID)
    return patch | (inner == BAND * GRID) & (block == 0)


def used_rows(seq_len):
    last = max(s for s in range(seq_len) if is_live(s))
    return min(seq_len, -(-(last + 1) // TILE) * TILE)


def normal(x):
    centre = jnp.mean(x, -1, keepdims=True)
    c = x - centre
    rstd = lax.rsqrt(jnp.mean(c * c, -1, keepdims=True) + 1e-6)
    return c * rstd, rstd


def layer(dims, r, emit, unit_of):
    images, rows, width, ff = dims
    total = images * rows
    tile = rows // 2 if rows % 32 == 0 else TILE
    per_image = rows // tile
    pairs = width // 128

    def vec(k):
        return r.vec[k : k + 1, :]

    def wide_mask(i, at):
        return jnp.concatenate([r.mask[i, pl.ds(at, tile), :].astype(F32)] * (width // 128), 1)

    def start_of(i, at, m):
        return jnp.where(m > 0.5, vec(14), r.tok[i, pl.ds(at, tile), :].astype(F32))

    def row_tiles(body, lo=0, hi=images):
        @pl.loop(lo * per_image, hi * per_image)
        def _(t):
            i = t // per_image
            at = pl.multiple_of((t % per_image) * tile, tile)
            body(i, at, pl.ds(pl.multiple_of(t * tile, tile), tile))

    def add_sum(k, x):
        r.gsum[k * 8 : (k + 1) * 8, :] += x.reshape(-1, 8, width).sum(0)

    r.gsum[...] = jnp.zeros_like(r.gsum)
    lane_row = lax.broadcasted_iota(jnp.int32, (rows, 128), 0)
    r.live[...] = jnp.where(is_live(lane_row), 1.0, 0.0).astype(F32)
    for ref in (r.out, r.ingrad):
        ref[:, rows:, :] = jnp.zeros((images, ref.shape[1] - rows, width), BF16)
    key_row = lax.broadcasted_iota(jnp.int32, (rows, rows), 0)
    r.dead[...] = jnp.where(is_live(key_row), 0.0, -1e30).astype(F32)

    yield

    def first(i, at, ds):
        m = wide_mask(i, at)
        xhat, _ = normal(start_of(i, at, m))
        r.normed[ds, :] = (xhat * vec(0) + vec(1)).astype(BF16)

    row_tiles(first)
    yield

    for i in range(images):
        ds = pl.ds(i * rows, rows)
        x = r.normed[ds, :]
        for b in range(3):
            for n in range(width // 256):
                c = b * width + n * 256
                y = dot(x, r.w_qkv[:, c : c + 256])
                if b == 0:
                    y = y + r.vec[2:3, n * 256 : (n + 1) * 256]
                if b == 2:
                    y = y + r.vec[3:4, n * 256 : (n + 1) * 256]
                y = y.astype(BF16)
                if b == 0:
                    y = y * BF16(HEAD_DIM**-0.5)
                r.proj[ds, c : c + 256] = y
        yield

    first_head = lax.broadcasted_iota(jnp.int32, (rows, 128), 1) < HEAD_DIM

    def stacked(x):
        zero = jnp.zeros_like(x)
        return jnp.concatenate([jnp.where(first_head, x, zero), jnp.where(first_head, zero, x)], 0)

    def pair_of(i, p, b):
        return (pl.ds(i * rows, rows), pl.ds(pl.multiple_of(b * width + p * 128, 128), 128))

    def forward_pair(p):
        for i in range(images):
            q2, k2, v2 = (r.proj[pair_of(i, p, b)] for b in range(3))
            scores = dot(stacked(k2), q2, NT)
            v_t = v2.T
            parts = []
            for h in range(2):
                s = scores[h * rows : (h + 1) * rows] + r.dead[...]
                e = jnp.exp(s - jnp.max(s, 0, keepdims=True))
                pr = (e * (1.0 / jnp.sum(e, 0, keepdims=True))).astype(BF16)
                r.probs[i * pairs + p, h * rows : (h + 1) * rows, :] = pr
                parts.append(dot(v_t[h * HEAD_DIM : (h + 1) * HEAD_DIM], pr))
            out = jnp.concatenate(parts, 0).T
            r.att[pl.ds(i * rows, rows), pl.ds(pl.multiple_of(p * 128, 128), 128)] = out.astype(BF16)

    for p in range(pairs):
        forward_pair(p)
        yield

    @pl.loop(0, images)
    def _(i):
        ds = pl.ds(pl.multiple_of(i * rows, TILE), rows)
        r.mid[ds, :] = dot(r.att[ds, :], r.w_out[...])

    yield

    def second(i, at, ds):
        m = wide_mask(i, at)
        branch = r.mid[ds, :] + vec(4)
        middle = start_of(i, at, m) + vec(5) * branch
        r.branch[ds, :] = branch.astype(BF16)
        r.mid[ds, :] = middle
        xhat, _ = normal(middle)
        r.sec[ds, :] = (xhat * vec(6) + vec(7)).astype(BF16)

    def seeded(i, at, ds):
        m = wide_mask(i, at)
        seed = r.cot[i, pl.ds(at, tile), :].astype(F32) * m
        r.gm[ds, :] = (seed * vec(13)).astype(BF16)
        add_sum(12, seed * vec(13))
        r.mlp[ds, :] = jnp.zeros((tile, width), F32)
        r.gs[ds, :] = jnp.zeros((tile, width), F32)

    row_tiles(second)
    yield
    row_tiles(seeded)
    yield

    for t in range(ff // width):
        u = unit_of(t)
        base = pl.multiple_of(u * width, width)
        for n in range(width // 256):
            cols = pl.ds(pl.multiple_of(base + n * 256, 256), 256)
            bias = r.vec[pl.ds(8 + u, 1), n * 256 : (n + 1) * 256]
            tot = jnp.zeros((8, 256), F32)
            for i in range(images):
                ds = pl.ds(i * rows, rows)
                h = dot(r.sec[ds, :], r.w_fc1[:, cols]) + bias
                ga = dot(r.gm[ds, :], r.w_fc2[cols, :], NT)
                phi = 0.5 * (1.0 + lax.erf(h * 0.5**0.5))
                r.act[ds, n * 256 : (n + 1) * 256] = (h * phi).astype(BF16)
                gh = ga * (phi + h * jnp.exp(-0.5 * h * h) * (2.0 * math.pi) ** -0.5)
                r.gh[ds, n * 256 : (n + 1) * 256] = gh.astype(BF16)
                tot = tot + gh.reshape(-1, 8, 256).sum(0)
            r.gsum[pl.ds(pl.multiple_of((8 + u) * 8, 8), 8), n * 256 : (n + 1) * 256] += tot
            yield
        emit(FC1, t, dot(r.sec[...], r.gh[...], TN))
        yield
        emit(FC2, t, dot(r.act[...], r.gm[...], TN))
        yield
        for i in range(images):
            ds = pl.ds(i * rows, rows)
            r.mlp[ds, :] += dot(r.act[ds, :], r.w_fc2[pl.ds(base, width), :])
            r.gs[ds, :] += dot(r.gh[ds, :], r.w_fc1[:, pl.ds(base, width)], NT)
            yield

    def middle_back(i, at, ds):
        m = wide_mask(i, at)
        seed = r.cot[i, pl.ds(at, tile), :].astype(F32) * m
        mlp = r.mlp[ds, :] + vec(12)
        middle = r.mid[ds, :]
        live = jnp.concatenate([r.live[pl.ds(at, tile), :]] * (width // 128), 1)
        r.out[i, pl.ds(at, tile), :] = ((middle + vec(13) * mlp) * live).astype(BF16)
        add_sum(13, seed * mlp)
        xhat, rstd = normal(middle)
        g = r.gs[ds, :]
        add_sum(6, g * xhat)
        add_sum(7, g)
        gx = g * vec(6)
        gmid = seed + rstd * (
            gx - jnp.mean(gx, -1, keepdims=True) - xhat * jnp.mean(gx * xhat, -1, keepdims=True)
        )
        r.gs[ds, :] = gmid
        gb = gmid * vec(5)
        add_sum(4, gb)
        add_sum(5, gmid * r.branch[ds, :].astype(F32))
        r.act[ds, :] = gb.astype(BF16)

    row_tiles(middle_back)
    yield

    @pl.loop(0, images)
    def _(i):
        ds = pl.ds(pl.multiple_of(i * rows, TILE), rows)
        r.gatt[ds, :] = dot(r.act[ds, :], r.w_out[...], NT).astype(BF16)

    yield
    emit(OUT, 0, dot(r.att[...], r.act[...], TN))

    yield

    def back_pair(p):
        for i in range(images):
            q2, k2, v2 = (r.proj[pair_of(i, p, b)] for b in range(3))
            go = r.gatt[pl.ds(i * rows, rows), pl.ds(pl.multiple_of(p * 128, 128), 128)]
            gp = dot(stacked(v2), go, NT)
            k_t = k2.T
            pr = r.probs[i * pairs + p]
            parts, gsc = [], []
            for h in range(2):
                prf = pr[h * rows : (h + 1) * rows].astype(F32)
                t = prf * gp[h * rows : (h + 1) * rows]
                s = (t - prf * jnp.sum(t, 0, keepdims=True)).astype(BF16)
                gsc.append(s)
                parts.append(dot(k_t[h * HEAD_DIM : (h + 1) * HEAD_DIM], s))
            gv = dot(pr, go)
            gv = jnp.where(first_head, gv[:rows], gv[rows:]).astype(BF16)
            gk = dot(jnp.concatenate(gsc, 0), q2)
            gk = jnp.where(first_head, gk[:rows], gk[rows:]).astype(BF16)
            gq = (jnp.concatenate(parts, 0).T * HEAD_DIM**-0.5).astype(BF16)
            r.proj[pair_of(i, p, 0)] = gq
            r.proj[pair_of(i, p, 1)] = gk
            r.proj[pair_of(i, p, 2)] = gv
            at = pl.ds(pl.multiple_of(p * 128, 128), 128)
            r.gsum[16:24, at] += gq.astype(F32).reshape(-1, 8, 128).sum(0)
            r.gsum[24:32, at] += gv.astype(F32).reshape(-1, 8, 128).sum(0)

    groups = width // 256

    def emit_group(g):
        cols = [slice(b * width + g * 256, b * width + (g + 1) * 256) for b in range(3)]
        emit(QKV, g, dot(r.normed[...], jnp.concatenate([r.proj[:, c] for c in cols], 1), TN))

    for g in range(groups):
        for p in (2 * g, 2 * g + 1):
            back_pair(p)
            yield
        emit_group(g)
        yield

    def first_back(i, at, ds):
        m = wide_mask(i, at)
        xhat, rstd = normal(start_of(i, at, m))
        g = r.mlp[ds, :]
        add_sum(0, g * xhat)
        add_sum(1, g)
        gx = g * vec(0)
        gst = r.gs[ds, :] + rstd * (
            gx - jnp.mean(gx, -1, keepdims=True) - xhat * jnp.mean(gx * xhat, -1, keepdims=True)
        )
        add_sum(14, gst * m)
        r.ingrad[i, pl.ds(at, tile), :] = (gst * (1.0 - m)).astype(BF16)

    for i in range(images):
        ds = pl.ds(i * rows, rows)
        r.mlp[ds, :] = dot(r.proj[ds, :], r.w_qkv[...], NT)
        yield
        row_tiles(first_back, i, i + 1)
        yield
    r.gvec[...] = r.gsum[...].reshape(16, 8, width).sum(1)
    yield


class Refs:
    def __init__(self, *groups):
        for group in groups:
            self.__dict__.update(group._asdict())


class Weights(NamedTuple):
    w_qkv: object
    w_out: object
    w_fc1: object
    w_fc2: object


class Rows(NamedTuple):
    tok: object
    mask: object
    cot: object
    vec: object
    out: object
    ingrad: object
    gvec: object


class Work(NamedTuple):
    gsum: object
    dead: object
    live: object
    normed: object
    proj: object
    probs: object
    att: object
    branch: object
    mid: object
    sec: object
    gm: object
    mlp: object
    gs: object
    act: object
    gh: object
    gatt: object


def plain_kernel(dims, tok, mask, cot, qkv, out_w, fc1, fc2, vec, out, ingrad, *refs):
    grads, gvec, work = refs[:4], refs[4], refs[5:]
    rows = Rows(tok, mask, cot, vec, out, ingrad, gvec)
    r = Refs(Weights(qkv, out_w, fc1, fc2), rows, Work(*work))
    width = dims[2]

    def emit(kind, u, value):
        value = value.astype(BF16)
        if kind == FC1:
            grads[FC1][:, pl.ds(pl.multiple_of(u * width, width), width)] = value
        elif kind == FC2:
            grads[FC2][pl.ds(pl.multiple_of(u * width, width), width), :] = value
        elif kind == OUT:
            grads[OUT][...] = value
        else:
            for b in range(3):
                c = b * width + u * 256
                grads[QKV][:, c : c + 256] = value[:, b * 256 : (b + 1) * 256]

    for _ in layer(dims, r, emit, lambda t: t):
        pass


def scratch(dims):
    images, rows, width, ff = dims
    total = images * rows
    low = lambda *s: pltpu.VMEM(s, BF16)
    full = lambda *s: pltpu.VMEM(s, F32)
    return Work(
        gsum=full(128, width),
        dead=full(rows, rows),
        live=full(rows, 128),
        normed=low(total, width),
        proj=low(total, 3 * width),
        probs=low(images * (width // 128), 2 * rows, rows),
        att=low(total, width),
        branch=low(total, width),
        mid=full(total, width),
        sec=low(total, width),
        gm=low(total, width),
        mlp=full(total, width),
        gs=full(total, width),
        act=low(total, width),
        gh=low(total, width),
        gatt=low(total, width),
    )


def plain_layer(tok, mask, cot, w_qkv, w_out, w_fc1, w_fc2, vec):
    images, seq_len, width = tok.shape
    dims = (images, used_rows(seq_len), width, w_fc1.shape[1])
    shape = jax.ShapeDtypeStruct
    return pl.pallas_call(
        functools.partial(plain_kernel, dims),
        out_shape=(
            shape(tok.shape, BF16),
            shape(tok.shape, BF16),
            shape(w_qkv.shape, BF16),
            shape(w_out.shape, BF16),
            shape(w_fc1.shape, BF16),
            shape(w_fc2.shape, BF16),
            shape((16, width), F32),
        ),
        in_specs=[pl.BlockSpec(memory_space=pltpu.VMEM)] * 8,
        out_specs=[pl.BlockSpec(memory_space=pltpu.VMEM)] * 7,
        scratch_shapes=list(scratch(dims)),
        compiler_params=pltpu.CompilerParams(
            vmem_limit_bytes=63 << 20
        ),
        name="layer",
    )(tok, mask, cot, w_qkv, w_out, w_fc1, w_fc2, vec)


NZ = 4
PARTS = 12
MESH = pl.DeviceIdType.MESH


class Sems:
    sends = recvs = locals = 0

    def send(self, count=1):
        self.sends += count
        return self.sends - count

    def recv(self, count=1):
        self.recvs += count
        return self.recvs - count

    def both(self, count=1):
        return self.send(), self.recv(count)

    def local(self, count=1):
        self.locals += count
        return self.locals - count


def make_sems():
    s = Sems()
    s.tok, s.mask, s.cot, s.out, s.ingrad = (s.both() for _ in range(5))
    s.vec_z, s.vec_y = s.both(), s.both()
    s.sz, s.sy, s.sx, s.sc = (s.send(4) for _ in range(4))
    s.wz, s.wy, s.wx, s.wc = s.recv(16), s.recv(16), s.recv(32), s.recv(16)
    s.c, s.r1 = (s.send(5), s.recv(5)), (s.send(5), s.recv(PARTS + 1))
    s.r2, s.zr2 = s.both(4), s.both()
    s.za, s.zc, s.zd = s.both(8), s.recv(8), s.both(2)
    s.gx, s.gx_fc2 = s.both(7), s.send()
    s.gc = s.send(4), s.recv(4)
    s.vs, s.vy, s.vz, s.vb = (s.both() for _ in range(4))
    s.l_tok, s.l_cot, s.l_out, s.l_ingrad = (s.local() for _ in range(4))
    s.l_w, s.l_g = s.local(4), s.local(4)
    return s


SEMS = make_sems()


SCHEDULE = (
    (0, 0), (10,), (11,), (2, 0, 0), (27, 0, 2), (1, 0, 1), (6, 1), (27, 0, 3), (1, 0, 2), (5, 1),
    (6, 2), (2, 0, 1), (2, 1, 0), (27, 1, 2), (9,), (0, 1), (1, 0, 3), (5, 2), (3, 0, 0, 1),
    (27, 1, 3), (3, 0, 1, 0), (1, 1, 1), (2, 0, 2), (3, 0, 2, 0), (3, 0, 1, 1), (1, 1, 2),
    (3, 1, 0, 1), (3, 0, 3, 0), (3, 1, 1, 0), (3, 0, 2, 1), (3, 1, 2, 0), (2, 2, 0), (27, 2, 2),
    (1, 2, 1), (6, 3), (1, 1, 3), (3, 2, 0, 1), (7, 0), (2, 0, 3), (3, 2, 1, 0), (3, 1, 3, 0),
    (2, 1, 1), (27, 2, 3), (2, 1, 2), (1, 2, 2), (3, 0, 3, 1), (3, 1, 1, 1), (7, 1), (3, 1, 2, 1),
    (4, 0, 0), (25, 0), (0, 2), (2, 2, 1), (3, 2, 2, 0), (1, 2, 3), (5, 3), (0, 3), (0, 4), (0, 5),
    (0, 6), (2, 3, 0), (0, 7), (2, 1, 3), (3, 2, 1, 1), (0, 8), (7, 2), (27, 3, 2), (1, 3, 1),
    (3, 2, 3, 0), (0, 9), (0, 10), (3, 3, 0, 1), (3, 1, 3, 1), (2, 2, 2), (27, 3, 3), (4, 1, 0),
    (25, 1), (0, 11), (0, 12), (1, 3, 2), (8,), (0, 13), (2, 2, 3), (3, 3, 1, 0), (3, 2, 2, 1),
    (3, 3, 2, 0), (1, 3, 3), (2, 3, 1), (3, 2, 3, 1), (4, 2, 0), (4, 3, 0), (25, 2), (25, 3),
    (0, 14), (3, 3, 3, 0), (0, 15), (0, 16), (3, 3, 1, 1), (0, 17), (2, 3, 2), (0, 18), (0, 19),
    (0, 20), (12, 1), (3, 3, 2, 1), (0, 21), (2, 3, 3), (12, 0), (4, 3, 1), (0, 22), (0, 23),
    (0, 24), (0, 25), (3, 3, 3, 1), (0, 26), (0, 27), (0, 28), (12, 3), (13, 1), (0, 29), (4, 3, 2),
    (0, 30), (12, 2), (0, 31), (0, 32), (0, 33), (13, 0), (0, 34), (0, 35), (12, 5), (0, 36),
    (0, 37), (12, 4), (4, 3, 3), (0, 38), (13, 2), (0, 39), (0, 40), (13, 3), (26, 3), (0, 41),
    (14, 0), (0, 42), (0, 43), (0, 44), (12, 7), (26, 1), (0, 45), (12, 6), (13, 5), (0, 46),
    (13, 4), (0, 47), (14, 2), (0, 48), (26, 5), (0, 49), (18, 0), (0, 50), (13, 6), (12, 8),
    (0, 51), (13, 7), (0, 52), (18, 1), (0, 53), (14, 4), (12, 9), (0, 54), (26, 7), (0, 55),
    (18, 2), (14, 6), (0, 56), (12, 10), (0, 57), (0, 58), (0, 59), (19, 0), (0, 60), (12, 11),
    (12, 12), (13, 8), (15, 2, 0), (0, 61), (19, 1), (0, 62), (0, 63), (0, 64), (20,), (19, 2),
    (15, 3, 0), (13, 9), (26, 8), (16, 2, 0), (26, 9), (13, 10), (15, 1, 0), (15, 0, 0), (13, 11),
    (21,), (26, 10), (13, 12), (22,), (15, 0, 2), (15, 0, 1), (16, 3, 0), (16, 1, 0), (15, 0, 3),
    (16, 0, 0), (23,), (16, 0, 2), (16, 0, 1), (16, 0, 3), (24,),
)


class More(NamedTuple):
    vecs: object
    U: object
    RC: object
    R1: object
    R2: object
    ZA: object
    ZB: object
    ZC: object
    ZD: object
    ZR2: object
    XS: object
    XR: object
    gv0: object
    gv1: object
    gv2: object
    gv3: object
    gv4: object
    ss: object
    rs: object
    ls: object
    mk: object
    mr: object


def linked_kernel(dims, tokens, masks, cotangent, *refs):
    w_in, in_vec, o_out, o_ingrad, g_outs, gvec_out = (
        *(refs[:4], refs[4], refs[5]),
        *(refs[6], refs[7:11], refs[11]),
    )
    refs = refs[12:]
    w, rows, g_held = refs[:4], Rows(*refs[4:11]), refs[11:15]
    r = Refs(Weights(*w), rows, Work(*refs[15:31]), More(*refs[31:]))
    images, rows, width, ff = dims
    d, s = lax.axis_index("dp"), lax.axis_index("seq")
    z, y, x, c = d // 2, d % 2, s // 2, s % 2
    slots = tokens.shape[1]
    upper = z // 2
    mate, inner, outer = z + 1 - 2 * (z % 2), (z + 1) // 2 % 2 == 1, (z + 1) // 2 % 2 == 0
    far = (z, mate, 2 - upper, 3 - 3 * upper)
    to_c, to_x, to_y = (d, x * 2 + 1 - c), (d, (1 - x) * 2 + c), (z * 2 + 1 - y, s)

    def to_z(k):
        return (lax.rem(z + k, NZ) * 2 + y, s)

    def to_s(k):
        return (d, lax.rem(s + k, 4))

    def at_z(zz):
        return (zz * 2 + y, s)

    def copy(pair, src, dst, dev):
        return pltpu.make_async_remote_copy(
            src, dst, r.ss.at[pair[0]], r.rs.at[pair[1]], device_id=dev, device_id_type=MESH
        )

    def send(pair, src, dst, dev):
        copy(pair, src, dst, dev).start()

    def got(pair, dst):
        copy((0, pair[1]), dst, dst, to_c).wait_recv()

    def left(sem, src):
        copy((sem, 0), src, src, to_c).wait_send()

    def local(sem, src, dst):
        pltpu.make_async_copy(src, dst, r.ls.at[sem]).start()

    def settled(sem, dst):
        pltpu.make_async_copy(dst, dst, r.ls.at[sem]).wait()

    barrier = pltpu.get_barrier_semaphore()
    peers = [to_y] + [to_s(k) for k in (1, 2, 3)] + [to_z(k) for k in (1, 2, 3)]
    for dev in peers:
        pl.semaphore_signal(barrier, inc=1, device_id=dev, device_id_type=MESH)
    pl.semaphore_wait(barrier, len(peers))

    def band(t):
        return pl.ds(pl.multiple_of(t * slots, 64), slots)

    def scatter(pair, sem, src, dst, lo=0, hi=images):
        for k in (2, 1, 3):
            t = lax.rem(s + k, 4)
            rows_out = src.at[pl.ds(t * images + lo, hi - lo)]
            send(pair, rows_out, dst.at[lo:hi, band(s)], to_s(k))
        local(sem, src.at[pl.ds(s * images + lo, hi - lo)], dst.at[lo:hi, band(s)])

    def give_back(pair, sem, src, dst, i):
        at = pl.ds(s * images + i, 1)
        for k in (2, 1, 3):
            send(pair, src.at[i : i + 1, band(lax.rem(s + k, 4))], dst.at[at], to_s(k))
        local(sem, src.at[i : i + 1, band(s)], dst.at[at])

    def block(a, zz, yy):
        return (zz * 2 + yy) * w_in[a].shape[0]

    def cut(ref, a, base, kind, mine=True):
        n, m = w_in[a].shape
        half = n // 2
        if kind == 2:
            at = base + (c if mine else 1 - c) * half
            return ref.at[pl.ds(pl.multiple_of(at, 16), half)]
        at, xx = base + c * half, x if mine else 1 - x
        if a == FC2:
            q = half // 4
            if kind == 0:
                return ref.at[pl.ds(pl.multiple_of(at + x * q, 16), half - q)]
            return ref.at[pl.ds(pl.multiple_of(at + xx * (half - q), 16), q)]
        q = m // 4 if a == FC1 else m // 6
        rs = pl.ds(pl.multiple_of(at, 16), half)
        if kind == 0:
            return ref.at[rs, pl.ds(pl.multiple_of(x * q, 128), m - q)]
        return ref.at[rs, pl.ds(pl.multiple_of(xx * (m - q), 128), q)]

    def piece(a, zz, yy, kind, mine=True):
        return cut(w[a], a, block(a, zz, yy), kind, mine)

    def own_piece(a):
        return cut(w_in[a], a, 0, 0)

    def w_own(a):
        n = w_in[a].shape[0]
        at = pl.ds(pl.multiple_of(block(a, z, y), 16), n)
        local(SEMS.l_w + a, w_in[a], w[a].at[at])

    def w_y0(a):
        send((SEMS.sy + a, SEMS.wy + 4 * a), own_piece(a), piece(a, z, y, 0), to_y)

    def w_z(a):
        pair = (SEMS.sz + a, SEMS.wz + 4 * a + 1)
        send(pair, own_piece(a), piece(a, z, y, 0), at_z(mate))
        pair = (SEMS.sz + a, SEMS.wz + 4 * a + jnp.where(inner, 2, 3))
        send(pair, own_piece(a), piece(a, z, y, 0), at_z(far[2]))

    def w_share(a, k, other):
        p = piece(a, far[k], 1 - y if other else y, 1)
        send((SEMS.sx + a, SEMS.wx + 8 * a + 4 * other + k), p, p, to_x)

    def w_zr(a, k):
        p = piece(a, far[k], y, 0)
        if k == 1:
            got((0, SEMS.wz + 4 * a + k), p)
        else:
            pl.when(outer)(lambda: got((0, SEMS.wz + 4 * a + k), p))
        send((SEMS.sy + a, SEMS.wy + 4 * a + k), p, p, to_y)
        w_share(a, k, 0)

    def w_on(a, k):
        p = piece(a, far[k], y, 0)

        @pl.when(inner)
        def _():
            got((0, SEMS.wz + 4 * a + k), p)
            send((SEMS.sz + a, SEMS.wz + 4 * a + k), p, p, at_z(mate))

    def w_yr(a, k):
        got((0, SEMS.wy + 4 * a + k), piece(a, far[k], 1 - y, 0))
        w_share(a, k, 1)

    def w_xr(a, k, other):
        yy = 1 - y if other else y
        got((0, SEMS.wx + 8 * a + 4 * other + k), piece(a, far[k], yy, 1, False))
        p = piece(a, far[k], yy, 2)
        send((SEMS.sc + a, SEMS.wc + 4 * a + (k if a == FC2 else 0)), p, p, to_c)

    def w_cr(a, k):
        n = w_in[a].shape[0]
        n = (n if k else n // 2) if a == FC2 else 7 * n // 2
        got((0, SEMS.wc + 4 * a + k), w[a].at[0:n])

    def w_left(a):
        n, m = w_in[a].shape
        half = n // 2
        q = half // 4 if a == FC2 else m // 4 if a == FC1 else m // 6

        def share(count, far_end):
            if a == FC2:
                return w[a].at[0 : count * (q if far_end else half - q)]
            return w[a].at[0 : count * half, 0 : q if far_end else m - q]

        pl.when(outer)(lambda: left(SEMS.sz + a, share(2, False)))
        pl.when(inner)(lambda: left(SEMS.sz + a, share(4, False)))
        left(SEMS.sy + a, share(4, False))
        left(SEMS.sx + a, share(7, True))
        left(SEMS.sc + a, w[a].at[0 : 7 * half])

    def unit_of(t):
        return far[t]

    def part_of(kind, t):
        return (9 + t, 8, 2 * t + 1, 2 * t)[kind]

    def x_first(q):
        return q in (2, 4, 6)

    def halves(q):
        return (min(q, 11), *((0, 2) if q < 11 else (q - 11, q - 10)))

    step, half, third = width // 16, width // 2, width // 4

    def c_sem(part):
        return 4 if part == 12 else part % 4

    def emit(kind, t, value):
        q = part_of(kind, t)
        slot = q % 4
        value = value.astype(BF16)
        for cc in range(2):
            for yy in range(2):
                if kind == FC2:
                    pieces = [(yy * half + cc * third, 0, third)]
                else:
                    pieces = [(((zz * 2 + yy) * 2 + cc) * step, zz * step, step) for zz in range(4)]
                for src, dst, size in pieces:
                    for xx in range(2):
                        v = value[src : src + size, xx * half : (xx + 1) * half]
                        r.U[slot, cc, yy, xx, dst : dst + size, :] = v
        for part in (q,) if q < 11 else (11, 12):
            _, lo, hi = halves(part)
            src, dst = r.U.at[slot, 1 - c, :, lo:hi], r.RC.at[slot, :, lo:hi]
            send((SEMS.c[0] + c_sem(part), SEMS.c[1] + c_sem(part)), src, dst, to_c)

    def g_1(part):
        q, lo, hi = halves(part)
        slot = q % 4
        got((0, SEMS.c[1] + c_sem(part)), r.RC.at[slot, :, lo:hi])

        def add(side):
            if x_first(q):

                @pl.loop(0, 2)
                def _(k):
                    r.U[slot, c, k, side] = r.U[slot, c, k, side] + r.RC[slot, k, side]

            else:

                @pl.loop(lo, hi)
                def _(k):
                    r.U[slot, c, side, k] = r.U[slot, c, side, k] + r.RC[slot, side, k]

        pair = (SEMS.r1[0] + c_sem(part), SEMS.r1[1] + part)
        if x_first(q):
            add(1 - x)
            send(pair, r.U.at[slot, c, :, 1 - x], r.R1.at[q], to_x)
            add(x)
        else:
            add(1 - y)
            send(pair, r.U.at[slot, c, 1 - y, lo:hi], r.R1.at[q, lo:hi], to_y)
            add(y)

    def z_slot(q):
        return unit_of(q // 2) if q < 8 else q - 4

    def steps(at, count=1):
        return pl.ds(pl.multiple_of(at * step, 16), count * step)

    def g_2(part):
        q, lo, hi = halves(part)
        got((0, SEMS.r1[1] + part), r.R1.at[q, lo:hi])
        left(SEMS.c[0] + c_sem(part), r.RC.at[q % 4, :, lo:hi])

        @pl.loop(lo, hi)
        def _(k):
            if x_first(q):
                r.R1[q, k] = r.R1[q, k] + r.U[q % 4, c, k, x]
            else:
                r.R1[q, k] = r.R1[q, k] + r.U[q % 4, c, y, k]

        left(SEMS.r1[0] + c_sem(part), r.R1.at[q, lo:hi])
        if q in (0, 2, 4, 6):
            side, dev = (1 - y, to_y) if x_first(q) else (1 - x, to_x)
            send((SEMS.r2[0], SEMS.r2[1] + q // 2), r.R1.at[q, side], r.R2.at[q // 2], dev)
            return
        if part > 10:
            for k in (2, 1, 3):
                src = r.R1.at[q, lo, steps(lax.rem(z + k, NZ))]
                send((SEMS.zd[0], SEMS.zd[1] + lo), src, r.ZD.at[lo, k - 1], to_z(k))
            return
        j = z_slot(q)
        pair = (SEMS.za[0], SEMS.za[1] + j)

        @pl.when(outer)
        def _():
            src = r.R1.at[q, lo:hi, steps(1 - upper, 3)]
            send(pair, src, r.ZA.at[j, lo:hi], at_z(mate))

        @pl.when(inner)
        def _():
            send(pair, r.R1.at[q, lo:hi, steps(mate)], r.ZB.at[j, lo:hi], at_z(mate))

    def g_7(part):
        q, lo, hi = halves(part)
        j = z_slot(q)

        @pl.when(inner)
        def _():
            got((0, SEMS.za[1] + j), r.ZA.at[j, lo:hi])
            across = steps(1 - upper, 2)
            own = r.R1[q, lo:hi, steps(2 - 2 * upper, 2)]
            r.ZA[j, lo:hi, across] = r.ZA[j, lo:hi, across] + own
            for i in range(2):
                src = r.ZA.at[j, lo:hi, steps(1 - upper + i)]
                pair = (SEMS.za[0], SEMS.zc + j)
                send(pair, src, r.ZC.at[j, lo:hi], at_z(2 - 2 * upper + i))

    def g_3(q):
        t = q // 2
        got((0, SEMS.r2[1] + t), r.R2.at[t])
        r.R2[t] = r.R2[t] + r.R1[q, y if x_first(q) else x]
        if t:
            u = unit_of(t)
            k = lax.rem(u + NZ - z, NZ)
            send(SEMS.zr2, r.R2.at[t], r.ZR2.at[k - 1], at_z(u))

    def g_4(kind, i):
        if kind == FC2:
            got(SEMS.zr2, r.ZR2)
            total = r.R2[0].astype(F32)
            for k in range(3):
                total = total + r.ZR2[k].astype(F32)
            g = g_held[FC2]
            g[c, x, 0] = total.astype(BF16)
            send((SEMS.gx_fc2, SEMS.gx[1]), g.at[c, x], g.at[c, x], to_x)
            return
        for part in {FC1: (1, 3, 5, 7), OUT: (8,), QKV: (9 + i,)}[kind]:
            q, lo, hi = halves(part)
            j = z_slot(q)
            if part > 10:
                got((0, SEMS.zd[1] + lo), r.ZD.at[lo])
                total = r.R1[q, lo, steps(z)].astype(F32)
                for k in range(3):
                    total = total + r.ZD[lo, k].astype(F32)
                r.XS[j, lo] = total.astype(BF16)
                continue
            got((0, SEMS.zc + j), r.ZC.at[j, lo:hi])

            def put(near, at):
                total = r.R1[q, lo:hi, steps(z)].astype(F32) + near[j, lo:hi, at].astype(F32)
                r.XS[j, lo:hi] = (total + r.ZC[j, lo:hi].astype(F32)).astype(BF16)

            @pl.when(outer)
            def _():
                got((0, SEMS.za[1] + j), r.ZB.at[j, lo:hi])
                put(r.ZB, slice(None))

            @pl.when(inner)
            def _():
                put(r.ZA, steps(2 * upper))

        sem, at = x_span(kind, i)
        send((SEMS.gx[0], sem), r.XS.at[at], r.XR.at[at], to_x)

    def x_span(kind, i):
        if kind == FC1:
            return SEMS.gx[1] + 1, (slice(0, 4),)
        q, lo, hi = halves(8 if kind == OUT else 9 + i)
        return SEMS.gx[1] + (2 if kind == OUT else 3 + i), (q - 4, slice(lo, hi))

    def g_5(kind, i):
        g = g_held[kind]
        if kind == FC2:
            got(SEMS.gx, g.at[c, 1 - x])
        else:
            sem, at = x_span(kind, i)
            got((0, sem), r.XR.at[at])
            units = range(4) if kind == FC1 else (at[0],)
            for n, j in enumerate(units):
                sides = (0, 1) if kind == FC1 else range(at[1].start, at[1].stop)
                for xx in sides:
                    g[c, xx, min(i, 2) + n] = r.XS[j, xx] + r.XR[j, xx]
        if kind != QKV or i == 3:
            mine = g_outs[kind].at[c]
            send((SEMS.gc[0] + kind, SEMS.gc[1] + kind), g.at[c], mine, to_c)
            local(SEMS.l_g + kind, g.at[c], mine)

    def v_part(p):
        return slice(p // 2 * 8, p // 2 * 8 + 8), slice(p % 2 * half, (p % 2 + 1) * half)

    def v_1():
        for p in range(4):
            r.gv0[p] = r.gvec[v_part(p)]
        r.gv1[s] = r.gv0[s]
        for k in (2, 1, 3):
            send(SEMS.vs, r.gv0.at[lax.rem(s + k, 4)], r.gv1.at[s], to_s(k))

    def v_2():
        got(SEMS.vs, r.gv1.at[0:3])
        r.gv2[0] = r.gv1[0] + r.gv1[1] + r.gv1[2] + r.gv1[3]
        send(SEMS.vy, r.gv2.at[0], r.gv2.at[1], to_y)

    def v_3():
        got(SEMS.vy, r.gv2.at[1])
        r.gv3[z] = r.gv2[0] + r.gv2[1]
        for k in (2, 1, 3):
            send(SEMS.vz, r.gv3.at[z], r.gv3.at[z], to_z(k))

    def v_4():
        got(SEMS.vz, r.gv3.at[0:3])
        r.gv4[s] = (r.gv3[0] + r.gv3[1]) + (r.gv3[2] + r.gv3[3])
        for k in (2, 1, 3):
            send(SEMS.vb, r.gv4.at[s], r.gv4.at[s], to_s(k))

    def v_5():
        got(SEMS.vb, r.gv4.at[0:3])
        n = width // (2 * NZ)
        row = lax.broadcasted_iota(jnp.int32, (half, 128), 0)
        lane = lax.broadcasted_iota(jnp.int32, (half, 128), 1)
        for top in range(2):
            total = jnp.zeros((8, 128), F32)
            for side in range(2):
                pick = jnp.where((row + side * half == lane + d * n) & (lane < n), 1.0, 0.0)
                part = lax.dot(
                    r.gv4[2 * top + side],
                    pick.astype(F32),
                    precision=lax.Precision.HIGHEST,
                    preferred_element_type=F32,
                )
                total = total + part
            gvec_out[top * 8 : top * 8 + 8, :] = total

    def vectors_in():
        total = jnp.zeros((16, width), F32)
        n = width // (2 * NZ)
        lane = lax.broadcasted_iota(jnp.int32, (128, width), 0)
        col = lax.broadcasted_iota(jnp.int32, (128, width), 1)
        for k in range(2 * NZ):
            pick = jnp.where((col == lane + k * n) & (lane < n), 1.0, 0.0).astype(BF16)
            total = total + dot(r.vecs[k % 2, k // 2].astype(BF16), pick)
        r.vec[...] = total

    def vec_z():
        got(SEMS.vec_z, r.vecs.at[y, 0:3])
        send(SEMS.vec_y, r.vecs.at[y], r.vecs.at[y], to_y)

    def vec_y():
        got(SEMS.vec_y, r.vecs.at[1 - y])
        vectors_in()

    three = slice(0, 3 * slots)

    def tokens_in():
        got(SEMS.mask, r.mr.at[0:3])
        for b in range(4):
            column = r.mr[b].T[0:slots]
            for i in range(images):
                wide = jnp.broadcast_to(column[:, i : i + 1], (slots, 128)).astype(BF16)
                r.mask[i, b * slots : (b + 1) * slots, :] = wide
        got(SEMS.tok, r.tok.at[:, three])
        settled(SEMS.l_tok, r.tok.at[:, 0:slots])

    def cot_out(i):
        scatter(SEMS.cot, SEMS.l_cot, cotangent, r.cot, i, i + 1)

    def cot_in():
        got(SEMS.cot, r.cot.at[:, three])
        settled(SEMS.l_cot, r.cot.at[:, 0:slots])

    def out_back(i):
        give_back(SEMS.out, SEMS.l_out, r.out, o_out, i)

    def ingrad_back(i):
        give_back(SEMS.ingrad, SEMS.l_ingrad, r.ingrad, o_ingrad, i)

    def own_in(a):
        settled(SEMS.l_w + a, w[a].at[0 : w_in[a].shape[0]])

    own = r.vecs.at[y, z]
    own[...] = jnp.zeros((16, 128), F32)
    own[0 : in_vec.shape[0], 0 : in_vec.shape[1]] = in_vec[...].astype(F32)
    for k in (1, 2, 3):
        send(SEMS.vec_z, own, own, to_z(k))
    marks = jnp.where(masks[...] == 1, 1.0, 0.0).astype(F32)
    r.mk[...] = jnp.zeros(r.mk.shape, F32)
    for t in range(4):
        r.mk[t, 0:images, 0:slots] = marks[t * images : (t + 1) * images]
    r.mr[s] = r.mk[s]
    for k in (2, 1, 3):
        send(SEMS.mask, r.mk.at[lax.rem(s + k, 4)], r.mr.at[s], to_s(k))
    scatter(SEMS.tok, SEMS.l_tok, tokens, r.tok)
    w_y0(QKV)
    w_z(QKV)
    for a in (QKV, OUT, FC1, FC2):
        w_own(a)
    piece_done = layer(dims, r, emit, unit_of)

    def go(k):
        next(piece_done)

    table = (go, w_zr, w_yr, w_xr, w_cr, w_z, w_y0, cot_out, cot_in, tokens_in, vec_z, vec_y)
    table += (g_1, g_2, g_3, g_4, g_5, None, out_back, ingrad_back)
    table += (v_1, v_2, v_3, v_4, v_5, own_in, g_7, w_on)
    for op, *at in SCHEDULE:
        table[op](*at)
    for _ in piece_done:
        pass
    bands = (SEMS.out, SEMS.l_out, o_out), (SEMS.ingrad, SEMS.l_ingrad, o_ingrad)
    for pair, sem, dst in bands:
        got(pair, dst.at[0 : 3 * images])
        settled(sem, dst.at[0:images])
    sent = [(SEMS.tok, r.tok), (SEMS.cot, r.cot)]
    sent = [(pair, ref.at[:, three]) for pair, ref in sent] + [(SEMS.mask, r.mk.at[0:3])]
    sent += [(pair, dst.at[0 : 3 * images]) for pair, _, dst in bands]
    sent += [(SEMS.vec_z, r.vecs.at[0, 0:3]), (SEMS.vec_y, r.vecs.at[0])]
    sent += [(SEMS.r2, r.R2), (SEMS.za, r.ZA.at[0:7]), (SEMS.zd, r.ZD), (SEMS.zr2, r.ZR2), (SEMS.gx, r.XS)]
    sent += [((SEMS.gx_fc2,), g_held[FC2].at[c, x])]
    sent += [((SEMS.gc[0] + a,), g_held[a].at[c]) for a in range(4)]
    sent += [(SEMS.vs, r.gv0.at[0:3]), (SEMS.vy, r.gv2.at[0])]
    sent += [(SEMS.vz, r.gv3.at[0:3]), (SEMS.vb, r.gv4.at[0:3])]
    for pair, src in sent:
        left(pair[0], src)
    for a in range(4):
        w_left(a)
        settled(SEMS.l_g + a, g_outs[a].at[c])
        got((0, SEMS.gc[1] + a), g_outs[a].at[1 - c])


def linked_layer(tokens, masks, cotangent, weights):
    count, slots, width = tokens.shape
    images, seq_len = count // 4, slots * 4
    dims = (images, used_rows(seq_len), width, weights[2].shape[1])
    shape = jax.ShapeDtypeStruct
    low = lambda *s: pltpu.VMEM(s, BF16)
    full = lambda *s: pltpu.VMEM(s, F32)
    sems = lambda n: pltpu.SemaphoreType.DMA((n,))
    step, half, third = width // 16, width // 2, width // 4
    hbm = pl.BlockSpec(memory_space=pl.ANY)
    vmem = pl.BlockSpec(memory_space=pltpu.VMEM)
    sums = [(2, 2, 3, step, half), (2, 2, 1, step, half), (2, 2, 4, step, half)]
    sums += [(2, 2, 1, third, half)]
    held = [low(w.shape[0] * 2 * NZ, w.shape[1]) for w in weights[:4]]
    held += [low(images, seq_len, w) for w in (width, 128, width)]
    held += [full(16, width)] + [low(images, seq_len, width)] * 2 + [full(16, width)]
    held += [low(*v) for v in sums]
    more = More(
        vecs=full(2, NZ, 16, 128),
        U=low(4, 2, 2, 2, third, half),
        RC=low(4, 2, 2, third, half),
        R1=low(PARTS, 2, third, half),
        R2=low(4, third, half),
        ZA=low(8, 2, 3 * step, half),
        ZB=low(8, 2, step, half),
        ZC=low(8, 2, step, half),
        ZD=low(2, 3, step, half),
        ZR2=low(3, third, half),
        XS=low(8, 2, step, half),
        XR=low(8, 2, step, half),
        gv0=full(4, 8, half),
        gv1=full(4, 8, half),
        gv2=full(2, 8, half),
        gv3=full(4, 8, half),
        gv4=full(4, 8, half),
        ss=sems(SEMS.sends),
        rs=sems(SEMS.recvs),
        ls=sems(SEMS.locals),
        mk=full(4, 8, 128),
        mr=full(4, 8, 128),
    )
    return pl.pallas_call(
        functools.partial(linked_kernel, dims),
        out_shape=(
            shape(tokens.shape, BF16),
            shape(tokens.shape, BF16),
            *(shape(v, BF16) for v in sums),
            shape((16, 128), F32),
        ),
        in_specs=[hbm, vmem] + [hbm] * 5 + [vmem],
        out_specs=[hbm] * 6 + [vmem],
        scratch_shapes=held + list(scratch(dims)) + list(more),
        compiler_params=pltpu.CompilerParams(
            collective_id=0,
            has_side_effects=True,
            vmem_limit_bytes=63 << 20,
        ),
        name="layer",
    )(tokens, masks, cotangent, *weights[:4], weights[4].T)


def sgd_step(gradient, master, moment, teacher, step_rate, decay_rate):
    pulled = gradient + decay_rate * master
    moment_new = momentum_rate * moment + pulled
    weight_new = master - step_rate * (pulled + momentum_rate * moment_new)
    teacher_new = teacher_rate * teacher + (1.0 - teacher_rate) * weight_new
    return (weight_new, moment_new, teacher_new, weight_new.astype(BF16))


def on_device(tokens, masks, cotangent, *rest):
    weights, masters, moments, teachers = rest[:5], rest[5:10], rest[10:15], rest[15:20]
    images, slots, width = tokens.shape
    step = (weights, masters, moments, teachers)
    if (lax.axis_size("dp"), lax.axis_size("seq")) == (2 * NZ, 4):
        out, ingrad, *sums, gvec = linked_layer(tokens, masks, cotangent, weights)
        return finish(out, ingrad, sums, gvec, *step)
    wide = jnp.broadcast_to((masks == 1).astype(BF16)[..., None], (images, slots, 128))
    full = [lax.all_gather(w, "dp", axis=0, tiled=True) for w in weights]
    vec = jnp.zeros((16, width), F32).at[: full[4].shape[1]].set(full[4].astype(F32).T)
    tok, mask, cot = (
        lax.all_to_all(v, "seq", 0, 1, tiled=True) for v in (tokens, wide, cotangent)
    )
    out, ingrad, *grads, gvec = plain_layer(tok, mask, cot, *full[:4], vec)
    out, ingrad = (lax.all_to_all(v, "seq", 1, 0, tiled=True) for v in (out, ingrad))
    sums = [lax.psum_scatter(g, "dp", scatter_dimension=0, tiled=True) for g in grads]
    sums = [lax.psum(g, "seq") for g in sums]
    gvec = lax.psum(gvec, ("dp", "seq"))
    part = width // lax.axis_size("dp")
    own = lax.dynamic_slice(gvec, (0, lax.axis_index("dp") * part), (16, part))
    return finish(out, ingrad, sums, own, *step)


def whole(kind, ref):
    if len(ref.shape) == 2:
        return ref[...].astype(F32)
    units, half = ref.shape[2], ref.shape[4]
    if kind != QKV:
        pieces = [ref[0, xx, u] for u in range(units) for xx in range(2)]
    else:
        at, cut = range(units), half * 2 // 3
        pieces = [ref[0, 0, u, :, 0:cut] for u in at]
        for u in at:
            pieces += [ref[0, 0, u, :, cut:half], ref[0, 1, u, :, 0 : half - cut]]
        pieces += [ref[0, 1, u, :, half - cut : half] for u in at]
    return jnp.concatenate(pieces, 1).astype(F32)


def update_kernel(steps, *refs):
    ins, outs = refs[:22], refs[22:]
    for k in range(5):
        n, m = ins[5 + k].shape
        g = whole(k, ins[k])[:n, :m]
        got = sgd_step(g, *(ins[5 * j + k][...] for j in (1, 2, 3)), *steps[k])
        for ref, v in zip((outs[k], *(outs[5 * j + k] for j in (1, 2, 3, 4))), (g, *got)):
            ref[...] = v
    outs[25][...] = ins[20][...]
    outs[26][...] = ins[21][...].astype(F32)


def finish(out, ingrad, sums, own, weights, masters, moments, teachers):
    images, slots, width = out.shape
    part = width // lax.axis_size("dp")
    image_total = images * lax.axis_size("dp")
    big = (matrix_rate / math.sqrt(image_total), matrix_decay)
    small = (vector_rate / math.sqrt(image_total), 0.0)
    steps = (big, big, big, big, small)
    count = 2
    if part % (16 * count) or images % count:
        sums = [g.astype(F32) for g in (*sums, own[: weights[4].shape[1]].T)]
        old = zip(sums, masters, moments, teachers, steps)
        ups = [sgd_step(*v, *rates) for *v, rates in old]
        return (out, ingrad.astype(F32), *sums, *(u[j] for j in range(4) for u in ups))

    def spec(a):
        if a.ndim == 5:
            block = (1, 2, a.shape[2], a.shape[3] * 2 // count, a.shape[4])
            return pl.BlockSpec(block, lambda i: (i // (count // 2), 0, 0, i % (count // 2), 0))
        if a.ndim == 2 and a.shape[0] < part:
            return pl.BlockSpec(a.shape, lambda i: (0, 0))
        rest = (0,) * (a.ndim - 1)
        return pl.BlockSpec((a.shape[0] // count, *a.shape[1:]), lambda i: (i, *rest))

    flip = lambda group: (*group[:4], group[4].T)
    args = [*sums, own, *flip(masters), *flip(moments), *flip(teachers), out, ingrad]
    shape = jax.ShapeDtypeStruct
    outs = [shape(m.shape, F32) for _ in range(4) for m in flip(masters)]
    outs += [shape(m.shape, BF16) for m in flip(masters)]
    outs += [shape(out.shape, BF16), shape(out.shape, F32)]
    res = pl.pallas_call(
        functools.partial(update_kernel, steps),
        grid=(count,),
        out_shape=outs,
        in_specs=[spec(a) for a in args],
        out_specs=[spec(a) for a in outs],
        compiler_params=pltpu.CompilerParams(vmem_limit_bytes=60 << 20),
        name="update",
    )(*args)
    res = [v.T if k % 5 == 4 and k < 25 else v for k, v in enumerate(res)]
    return (res[25], res[26], *res[:25])


def solution(mesh):
    band = P("dp", "seq", None)
    rows = P("dp", None)
    return jax.shard_map(
        on_device,
        mesh=mesh,
        in_specs=(band, P("dp", "seq"), band) + (rows,) * 20,
        out_specs=(band, band) + (rows,) * 25,
        check_vma=False,
    )
```

```python
import functools
import math
from typing import NamedTuple

import jax
import jax.numpy as jnp
from jax import lax
from jax.experimental import pallas as pl
from jax.experimental.pallas import tpu as pltpu
from jax.sharding import PartitionSpec as P

HEADS = 12
HEAD_DIM = 64
GRID = 14
BAND = 4
SLOTS = 64

momentum_rate = 0.9
teacher_rate = 0.75
matrix_rate = 0.003
vector_rate = 0.03
matrix_decay = 0.05

F32 = jnp.float32
BF16 = jnp.bfloat16
TILE = 32
NN = (((1,), (0,)), ((), ()))
NT = (((1,), (1,)), ((), ()))
TN = (((0,), (0,)), ((), ()))
QKV, OUT, FC1, FC2 = range(4)


def dot(a, b, form=NN):
    return lax.dot_general(a, b, form, preferred_element_type=F32)


def is_live(position):
    block = position // SLOTS
    inner = position % SLOTS
    patch = (inner < BAND * GRID) & (BAND * block + inner // GRID < GRID)
    return patch | (inner == BAND * GRID) & (block == 0)


def used_rows(seq_len):
    last = max(s for s in range(seq_len) if is_live(s))
    return min(seq_len, -(-(last + 1) // TILE) * TILE)


def normal(x):
    centre = jnp.mean(x, -1, keepdims=True)
    c = x - centre
    rstd = lax.rsqrt(jnp.mean(c * c, -1, keepdims=True) + 1e-6)
    return c * rstd, rstd


def layer(dims, r, emit, unit_of):
    images, rows, width, ff = dims
    total = images * rows
    tile = rows // 2 if rows % 32 == 0 else TILE
    per_image = rows // tile
    pairs = width // 128

    def vec(k):
        return r.vec[k : k + 1, :]

    def wide_mask(i, at):
        return jnp.concatenate([r.mask[i, pl.ds(at, tile), :].astype(F32)] * (width // 128), 1)

    def start_of(i, at, m):
        return jnp.where(m > 0.5, vec(14), r.tok[i, pl.ds(at, tile), :].astype(F32))

    def row_tiles(body, lo=0, hi=images):
        @pl.loop(lo * per_image, hi * per_image)
        def _(t):
            i = t // per_image
            at = pl.multiple_of((t % per_image) * tile, tile)
            body(i, at, pl.ds(pl.multiple_of(t * tile, tile), tile))

    def add_sum(k, x):
        r.gsum[k * 8 : (k + 1) * 8, :] += x.reshape(-1, 8, width).sum(0)

    r.gsum[...] = jnp.zeros_like(r.gsum)
    lane_row = lax.broadcasted_iota(jnp.int32, (rows, 128), 0)
    r.live[...] = jnp.where(is_live(lane_row), 1.0, 0.0).astype(F32)
    for ref in (r.out, r.ingrad):
        ref[:, rows:, :] = jnp.zeros((images, ref.shape[1] - rows, width), BF16)
    key_row = lax.broadcasted_iota(jnp.int32, (rows, rows), 0)
    r.dead[...] = jnp.where(is_live(key_row), 0.0, -1e30).astype(F32)

    yield

    def first(i, at, ds):
        m = wide_mask(i, at)
        xhat, _ = normal(start_of(i, at, m))
        r.normed[ds, :] = (xhat * vec(0) + vec(1)).astype(BF16)

    row_tiles(first)
    yield

    for i in range(images):
        ds = pl.ds(i * rows, rows)
        x = r.normed[ds, :]
        for b in range(3):
            for n in range(width // 256):
                c = b * width + n * 256
                y = dot(x, r.w_qkv[:, c : c + 256])
                if b == 0:
                    y = y + r.vec[2:3, n * 256 : (n + 1) * 256]
                if b == 2:
                    y = y + r.vec[3:4, n * 256 : (n + 1) * 256]
                y = y.astype(BF16)
                if b == 0:
                    y = y * BF16(HEAD_DIM**-0.5)
                r.proj[ds, c : c + 256] = y
        yield

    first_head = lax.broadcasted_iota(jnp.int32, (rows, 128), 1) < HEAD_DIM

    def stacked(x):
        zero = jnp.zeros_like(x)
        return jnp.concatenate([jnp.where(first_head, x, zero), jnp.where(first_head, zero, x)], 0)

    def pair_of(i, p, b):
        return (pl.ds(i * rows, rows), pl.ds(pl.multiple_of(b * width + p * 128, 128), 128))

    def forward_pair(p):
        for i in range(images):
            q2, k2, v2 = (r.proj[pair_of(i, p, b)] for b in range(3))
            scores = dot(stacked(k2), q2, NT)
            v_t = v2.T
            parts = []
            for h in range(2):
                s = scores[h * rows : (h + 1) * rows] + r.dead[...]
                e = jnp.exp(s - jnp.max(s, 0, keepdims=True))
                pr = (e * (1.0 / jnp.sum(e, 0, keepdims=True))).astype(BF16)
                r.probs[i * pairs + p, h * rows : (h + 1) * rows, :] = pr
                parts.append(dot(v_t[h * HEAD_DIM : (h + 1) * HEAD_DIM], pr))
            out = jnp.concatenate(parts, 0).T
            r.att[pl.ds(i * rows, rows), pl.ds(pl.multiple_of(p * 128, 128), 128)] = out.astype(BF16)

    for p in range(pairs):
        forward_pair(p)
        yield

    @pl.loop(0, images)
    def _(i):
        ds = pl.ds(pl.multiple_of(i * rows, TILE), rows)
        r.mid[ds, :] = dot(r.att[ds, :], r.w_out[...])

    yield

    def second(i, at, ds):
        m = wide_mask(i, at)
        branch = r.mid[ds, :] + vec(4)
        middle = start_of(i, at, m) + vec(5) * branch
        r.branch[ds, :] = branch.astype(BF16)
        r.mid[ds, :] = middle
        xhat, _ = normal(middle)
        r.sec[ds, :] = (xhat * vec(6) + vec(7)).astype(BF16)

    def seeded(i, at, ds):
        m = wide_mask(i, at)
        seed = r.cot[i, pl.ds(at, tile), :].astype(F32) * m
        r.gm[ds, :] = (seed * vec(13)).astype(BF16)
        add_sum(12, seed * vec(13))
        r.mlp[ds, :] = jnp.zeros((tile, width), F32)
        r.gs[ds, :] = jnp.zeros((tile, width), F32)

    row_tiles(second)
    yield
    row_tiles(seeded)
    yield

    for t in range(ff // width):
        u = unit_of(t)
        base = pl.multiple_of(u * width, width)
        for n in range(width // 256):
            cols = pl.ds(pl.multiple_of(base + n * 256, 256), 256)
            bias = r.vec[pl.ds(8 + u, 1), n * 256 : (n + 1) * 256]
            tot = jnp.zeros((8, 256), F32)
            for i in range(images):
                ds = pl.ds(i * rows, rows)
                h = dot(r.sec[ds, :], r.w_fc1[:, cols]) + bias
                ga = dot(r.gm[ds, :], r.w_fc2[cols, :], NT)
                phi = 0.5 * (1.0 + lax.erf(h * 0.5**0.5))
                r.act[ds, n * 256 : (n + 1) * 256] = (h * phi).astype(BF16)
                gh = ga * (phi + h * jnp.exp(-0.5 * h * h) * (2.0 * math.pi) ** -0.5)
                r.gh[ds, n * 256 : (n + 1) * 256] = gh.astype(BF16)
                tot = tot + gh.reshape(-1, 8, 256).sum(0)
            r.gsum[pl.ds(pl.multiple_of((8 + u) * 8, 8), 8), n * 256 : (n + 1) * 256] += tot
            yield
        emit(FC1, t, dot(r.sec[...], r.gh[...], TN))
        yield
        emit(FC2, t, dot(r.act[...], r.gm[...], TN))
        yield
        for i in range(images):
            ds = pl.ds(i * rows, rows)
            r.mlp[ds, :] += dot(r.act[ds, :], r.w_fc2[pl.ds(base, width), :])
            r.gs[ds, :] += dot(r.gh[ds, :], r.w_fc1[:, pl.ds(base, width)], NT)
            yield

    def middle_back(i, at, ds):
        m = wide_mask(i, at)
        seed = r.cot[i, pl.ds(at, tile), :].astype(F32) * m
        mlp = r.mlp[ds, :] + vec(12)
        middle = r.mid[ds, :]
        live = jnp.concatenate([r.live[pl.ds(at, tile), :]] * (width // 128), 1)
        r.out[i, pl.ds(at, tile), :] = ((middle + vec(13) * mlp) * live).astype(BF16)
        add_sum(13, seed * mlp)
        xhat, rstd = normal(middle)
        g = r.gs[ds, :]
        add_sum(6, g * xhat)
        add_sum(7, g)
        gx = g * vec(6)
        gmid = seed + rstd * (
            gx - jnp.mean(gx, -1, keepdims=True) - xhat * jnp.mean(gx * xhat, -1, keepdims=True)
        )
        r.gs[ds, :] = gmid
        gb = gmid * vec(5)
        add_sum(4, gb)
        add_sum(5, gmid * r.branch[ds, :].astype(F32))
        r.act[ds, :] = gb.astype(BF16)

    row_tiles(middle_back)
    yield

    @pl.loop(0, images)
    def _(i):
        ds = pl.ds(pl.multiple_of(i * rows, TILE), rows)
        r.gatt[ds, :] = dot(r.act[ds, :], r.w_out[...], NT).astype(BF16)

    yield
    emit(OUT, 0, dot(r.att[...], r.act[...], TN))

    yield

    def back_pair(p):
        for i in range(images):
            q2, k2, v2 = (r.proj[pair_of(i, p, b)] for b in range(3))
            go = r.gatt[pl.ds(i * rows, rows), pl.ds(pl.multiple_of(p * 128, 128), 128)]
            gp = dot(stacked(v2), go, NT)
            k_t = k2.T
            pr = r.probs[i * pairs + p]
            parts, gsc = [], []
            for h in range(2):
                prf = pr[h * rows : (h + 1) * rows].astype(F32)
                t = prf * gp[h * rows : (h + 1) * rows]
                s = (t - prf * jnp.sum(t, 0, keepdims=True)).astype(BF16)
                gsc.append(s)
                parts.append(dot(k_t[h * HEAD_DIM : (h + 1) * HEAD_DIM], s))
            gv = dot(pr, go)
            gv = jnp.where(first_head, gv[:rows], gv[rows:]).astype(BF16)
            gk = dot(jnp.concatenate(gsc, 0), q2)
            gk = jnp.where(first_head, gk[:rows], gk[rows:]).astype(BF16)
            gq = (jnp.concatenate(parts, 0).T * HEAD_DIM**-0.5).astype(BF16)
            r.proj[pair_of(i, p, 0)] = gq
            r.proj[pair_of(i, p, 1)] = gk
            r.proj[pair_of(i, p, 2)] = gv
            at = pl.ds(pl.multiple_of(p * 128, 128), 128)
            r.gsum[16:24, at] += gq.astype(F32).reshape(-1, 8, 128).sum(0)
            r.gsum[24:32, at] += gv.astype(F32).reshape(-1, 8, 128).sum(0)

    groups = width // 256

    def emit_group(g):
        cols = [slice(b * width + g * 256, b * width + (g + 1) * 256) for b in range(3)]
        emit(QKV, g, dot(r.normed[...], jnp.concatenate([r.proj[:, c] for c in cols], 1), TN))

    for g in range(groups):
        for p in (2 * g, 2 * g + 1):
            back_pair(p)
            yield
        emit_group(g)
        yield

    def first_back(i, at, ds):
        m = wide_mask(i, at)
        xhat, rstd = normal(start_of(i, at, m))
        g = r.mlp[ds, :]
        add_sum(0, g * xhat)
        add_sum(1, g)
        gx = g * vec(0)
        gst = r.gs[ds, :] + rstd * (
            gx - jnp.mean(gx, -1, keepdims=True) - xhat * jnp.mean(gx * xhat, -1, keepdims=True)
        )
        add_sum(14, gst * m)
        r.ingrad[i, pl.ds(at, tile), :] = (gst * (1.0 - m)).astype(BF16)

    for i in range(images):
        ds = pl.ds(i * rows, rows)
        r.mlp[ds, :] = dot(r.proj[ds, :], r.w_qkv[...], NT)
        yield
        row_tiles(first_back, i, i + 1)
        yield
    r.gvec[...] = r.gsum[...].reshape(16, 8, width).sum(1)
    yield


class Refs:
    def __init__(self, *groups):
        for group in groups:
            self.__dict__.update(group._asdict())


class Weights(NamedTuple):
    w_qkv: object
    w_out: object
    w_fc1: object
    w_fc2: object


class Rows(NamedTuple):
    tok: object
    mask: object
    cot: object
    vec: object
    out: object
    ingrad: object
    gvec: object


class Work(NamedTuple):
    gsum: object
    dead: object
    live: object
    normed: object
    proj: object
    probs: object
    att: object
    branch: object
    mid: object
    sec: object
    gm: object
    mlp: object
    gs: object
    act: object
    gh: object
    gatt: object


def plain_kernel(dims, tok, mask, cot, qkv, out_w, fc1, fc2, vec, out, ingrad, *refs):
    grads, gvec, work = refs[:4], refs[4], refs[5:]
    rows = Rows(tok, mask, cot, vec, out, ingrad, gvec)
    r = Refs(Weights(qkv, out_w, fc1, fc2), rows, Work(*work))
    width = dims[2]

    def emit(kind, u, value):
        value = value.astype(BF16)
        if kind == FC1:
            grads[FC1][:, pl.ds(pl.multiple_of(u * width, width), width)] = value
        elif kind == FC2:
            grads[FC2][pl.ds(pl.multiple_of(u * width, width), width), :] = value
        elif kind == OUT:
            grads[OUT][...] = value
        else:
            for b in range(3):
                c = b * width + u * 256
                grads[QKV][:, c : c + 256] = value[:, b * 256 : (b + 1) * 256]

    for _ in layer(dims, r, emit, lambda t: t):
        pass


def scratch(dims):
    images, rows, width, ff = dims
    total = images * rows
    low = lambda *s: pltpu.VMEM(s, BF16)
    full = lambda *s: pltpu.VMEM(s, F32)
    return Work(
        gsum=full(128, width),
        dead=full(rows, rows),
        live=full(rows, 128),
        normed=low(total, width),
        proj=low(total, 3 * width),
        probs=low(images * (width // 128), 2 * rows, rows),
        att=low(total, width),
        branch=low(total, width),
        mid=full(total, width),
        sec=low(total, width),
        gm=low(total, width),
        mlp=full(total, width),
        gs=full(total, width),
        act=low(total, width),
        gh=low(total, width),
        gatt=low(total, width),
    )


def plain_layer(tok, mask, cot, w_qkv, w_out, w_fc1, w_fc2, vec):
    images, seq_len, width = tok.shape
    dims = (images, used_rows(seq_len), width, w_fc1.shape[1])
    shape = jax.ShapeDtypeStruct
    return pl.pallas_call(
        functools.partial(plain_kernel, dims),
        out_shape=(
            shape(tok.shape, BF16),
            shape(tok.shape, BF16),
            shape(w_qkv.shape, BF16),
            shape(w_out.shape, BF16),
            shape(w_fc1.shape, BF16),
            shape(w_fc2.shape, BF16),
            shape((16, width), F32),
        ),
        in_specs=[pl.BlockSpec(memory_space=pltpu.VMEM)] * 8,
        out_specs=[pl.BlockSpec(memory_space=pltpu.VMEM)] * 7,
        scratch_shapes=list(scratch(dims)),
        compiler_params=pltpu.CompilerParams(
            vmem_limit_bytes=63 << 20
        ),
        name="layer",
    )(tok, mask, cot, w_qkv, w_out, w_fc1, w_fc2, vec)


NZ = 4
PARTS = 12
MESH = pl.DeviceIdType.MESH


class Sems:
    sends = recvs = locals = 0

    def send(self, count=1):
        self.sends += count
        return self.sends - count

    def recv(self, count=1):
        self.recvs += count
        return self.recvs - count

    def both(self, count=1):
        return self.send(), self.recv(count)

    def local(self, count=1):
        self.locals += count
        return self.locals - count


def make_sems():
    s = Sems()
    s.tok, s.mask, s.cot, s.out, s.ingrad = (s.both() for _ in range(5))
    s.vec_z, s.vec_y = s.both(), s.both()
    s.sz, s.sy, s.sx, s.sc = (s.send(4) for _ in range(4))
    s.wz, s.wy, s.wx, s.wc = s.recv(16), s.recv(16), s.recv(32), s.recv(16)
    s.c, s.r1 = (s.send(5), s.recv(5)), (s.send(5), s.recv(PARTS + 1))
    s.r2, s.zr2 = s.both(4), s.both()
    s.za, s.zc, s.zd = s.both(8), s.recv(8), s.both(2)
    s.gx, s.gx_fc2 = s.both(7), s.send()
    s.gc = s.send(4), s.recv(4)
    s.vs, s.vy, s.vz, s.vb = (s.both() for _ in range(4))
    s.l_tok, s.l_cot, s.l_out, s.l_ingrad = (s.local() for _ in range(4))
    s.l_w, s.l_g = s.local(4), s.local(4)
    return s


SEMS = make_sems()


SCHEDULE = (
    (0, 0), (10,), (11,), (2, 0, 0), (27, 0, 2), (1, 0, 1), (6, 1), (27, 0, 3), (1, 0, 2), (5, 1),
    (6, 2), (2, 0, 1), (2, 1, 0), (9,), (0, 1), (27, 1, 2), (3, 0, 0, 1), (3, 0, 1, 0), (27, 1, 3),
    (1, 0, 3), (5, 2), (3, 0, 2, 0), (3, 0, 1, 1), (3, 1, 0, 1), (1, 1, 1), (2, 0, 2), (3, 0, 3, 0),
    (3, 1, 1, 0), (1, 1, 2), (3, 0, 2, 1), (3, 1, 2, 0), (1, 1, 3), (7, 0), (3, 1, 3, 0),
    (27, 2, 2), (2, 2, 0), (1, 2, 1), (2, 0, 3), (27, 2, 3), (3, 2, 0, 1), (7, 1), (2, 1, 1),
    (3, 2, 1, 0), (2, 1, 2), (3, 0, 3, 1), (1, 2, 2), (2, 1, 3), (4, 0, 0), (25, 0), (0, 2), (0, 3),
    (0, 4), (7, 2), (0, 5), (3, 1, 1, 1), (3, 1, 2, 1), (1, 2, 3), (5, 3), (6, 3), (0, 6),
    (2, 2, 1), (3, 2, 2, 0), (3, 1, 3, 1), (0, 7), (0, 8), (0, 9), (2, 2, 2), (0, 10), (27, 3, 2),
    (1, 3, 1), (4, 1, 0), (25, 1), (0, 11), (3, 2, 3, 0), (0, 12), (3, 2, 1, 1), (8,), (0, 13),
    (2, 2, 3), (3, 2, 2, 1), (27, 3, 3), (3, 3, 1, 0), (1, 3, 2), (3, 2, 3, 1), (2, 3, 0),
    (3, 3, 2, 0), (3, 3, 0, 1), (1, 3, 3), (4, 2, 0), (4, 3, 0), (25, 2), (25, 3), (0, 14), (0, 15),
    (2, 3, 1), (0, 16), (3, 3, 3, 0), (0, 17), (0, 18), (3, 3, 1, 1), (0, 19), (2, 3, 2), (12, 1),
    (0, 20), (0, 21), (12, 0), (4, 3, 1), (0, 22), (3, 3, 2, 1), (0, 23), (0, 24), (2, 3, 3),
    (0, 25), (0, 26), (0, 27), (12, 3), (0, 28), (13, 0), (0, 29), (12, 2), (13, 1), (4, 3, 2),
    (0, 30), (3, 3, 3, 1), (0, 31), (0, 32), (0, 33), (0, 34), (0, 35), (13, 3), (26, 3), (12, 5),
    (0, 36), (13, 2), (12, 4), (0, 37), (4, 3, 3), (0, 38), (14, 0), (0, 39), (26, 1), (0, 40),
    (0, 41), (0, 42), (0, 43), (12, 7), (13, 4), (13, 5), (0, 44), (0, 45), (12, 6), (0, 46),
    (18, 0), (14, 2), (26, 5), (0, 47), (0, 48), (18, 1), (0, 49), (0, 50), (13, 7), (12, 8),
    (0, 51), (18, 2), (0, 52), (14, 4), (0, 53), (12, 9), (26, 7), (13, 6), (0, 54), (0, 55),
    (0, 56), (15, 2, 0), (12, 10), (14, 6), (0, 57), (0, 58), (13, 8), (0, 59), (19, 0), (12, 11),
    (0, 60), (12, 12), (0, 61), (19, 1), (0, 62), (0, 63), (15, 3, 0), (0, 64), (20,), (19, 2),
    (16, 2, 0), (13, 9), (26, 8), (26, 9), (15, 1, 0), (13, 10), (15, 0, 0), (13, 11), (16, 3, 0),
    (26, 10), (21,), (13, 12), (22,), (15, 0, 2), (15, 0, 1), (16, 1, 0), (16, 0, 0), (15, 0, 3),
    (16, 0, 2), (23,), (16, 0, 1), (16, 0, 3), (24,),
)


class More(NamedTuple):
    vecs: object
    U: object
    RC: object
    R1: object
    R2: object
    ZA: object
    ZB: object
    ZC: object
    ZD: object
    ZR2: object
    XS: object
    XR: object
    gv0: object
    gv1: object
    gv2: object
    gv3: object
    gv4: object
    ss: object
    rs: object
    ls: object
    mk: object
    mr: object


def linked_kernel(dims, tokens, masks, cotangent, *refs):
    w_in, in_vec, o_out, o_ingrad, g_outs, gvec_out = (
        *(refs[:4], refs[4], refs[5]),
        *(refs[6], refs[7:11], refs[11]),
    )
    refs = refs[12:]
    w, rows, g_held = refs[:4], Rows(*refs[4:11]), refs[11:15]
    r = Refs(Weights(*w), rows, Work(*refs[15:31]), More(*refs[31:]))
    images, rows, width, ff = dims
    d, s = lax.axis_index("dp"), lax.axis_index("seq")
    z, y, x, c = d // 2, d % 2, s // 2, s % 2
    slots = tokens.shape[1]
    upper = z // 2
    mate, inner, outer = z + 1 - 2 * (z % 2), (z + 1) // 2 % 2 == 1, (z + 1) // 2 % 2 == 0
    far = (z, mate, 2 - upper, 3 - 3 * upper)
    to_c, to_x, to_y = (d, x * 2 + 1 - c), (d, (1 - x) * 2 + c), (z * 2 + 1 - y, s)

    def to_z(k):
        return (lax.rem(z + k, NZ) * 2 + y, s)

    def to_s(k):
        return (d, lax.rem(s + k, 4))

    def at_z(zz):
        return (zz * 2 + y, s)

    def copy(pair, src, dst, dev):
        return pltpu.make_async_remote_copy(
            src, dst, r.ss.at[pair[0]], r.rs.at[pair[1]], device_id=dev, device_id_type=MESH
        )

    def send(pair, src, dst, dev):
        copy(pair, src, dst, dev).start()

    def got(pair, dst):
        copy((0, pair[1]), dst, dst, to_c).wait_recv()

    def left(sem, src):
        copy((sem, 0), src, src, to_c).wait_send()

    def local(sem, src, dst):
        pltpu.make_async_copy(src, dst, r.ls.at[sem]).start()

    def settled(sem, dst):
        pltpu.make_async_copy(dst, dst, r.ls.at[sem]).wait()

    barrier = pltpu.get_barrier_semaphore()
    peers = [to_y] + [to_s(k) for k in (1, 2, 3)] + [to_z(k) for k in (1, 2, 3)]
    for dev in peers:
        pl.semaphore_signal(barrier, inc=1, device_id=dev, device_id_type=MESH)
    pl.semaphore_wait(barrier, len(peers))

    def band(t):
        return pl.ds(pl.multiple_of(t * slots, 64), slots)

    def scatter(pair, sem, src, dst, lo=0, hi=images):
        for k in (2, 1, 3):
            t = lax.rem(s + k, 4)
            rows_out = src.at[pl.ds(t * images + lo, hi - lo)]
            send(pair, rows_out, dst.at[lo:hi, band(s)], to_s(k))
        local(sem, src.at[pl.ds(s * images + lo, hi - lo)], dst.at[lo:hi, band(s)])

    def give_back(pair, sem, src, dst, i):
        at = pl.ds(s * images + i, 1)
        for k in (2, 1, 3):
            send(pair, src.at[i : i + 1, band(lax.rem(s + k, 4))], dst.at[at], to_s(k))
        local(sem, src.at[i : i + 1, band(s)], dst.at[at])

    def block(a, zz, yy):
        return (zz * 2 + yy) * w_in[a].shape[0]

    def cut(ref, a, base, kind, mine=True):
        n, m = w_in[a].shape
        half = n // 2
        if kind == 2:
            at = base + (c if mine else 1 - c) * half
            return ref.at[pl.ds(pl.multiple_of(at, 16), half)]
        at, xx = base + c * half, x if mine else 1 - x
        if a == FC2:
            q = half // 4
            if kind == 0:
                return ref.at[pl.ds(pl.multiple_of(at + x * q, 16), half - q)]
            return ref.at[pl.ds(pl.multiple_of(at + xx * (half - q), 16), q)]
        q = m // 4 if a == FC1 else m // 6
        rs = pl.ds(pl.multiple_of(at, 16), half)
        if kind == 0:
            return ref.at[rs, pl.ds(pl.multiple_of(x * q, 128), m - q)]
        return ref.at[rs, pl.ds(pl.multiple_of(xx * (m - q), 128), q)]

    def piece(a, zz, yy, kind, mine=True):
        return cut(w[a], a, block(a, zz, yy), kind, mine)

    def own_piece(a):
        return cut(w_in[a], a, 0, 0)

    def w_own(a):
        n = w_in[a].shape[0]
        at = pl.ds(pl.multiple_of(block(a, z, y), 16), n)
        local(SEMS.l_w + a, w_in[a], w[a].at[at])

    def w_y0(a):
        send((SEMS.sy + a, SEMS.wy + 4 * a), own_piece(a), piece(a, z, y, 0), to_y)

    def w_z(a):
        pair = (SEMS.sz + a, SEMS.wz + 4 * a + 1)
        send(pair, own_piece(a), piece(a, z, y, 0), at_z(mate))
        pair = (SEMS.sz + a, SEMS.wz + 4 * a + jnp.where(inner, 2, 3))
        send(pair, own_piece(a), piece(a, z, y, 0), at_z(far[2]))

    def w_share(a, k, other):
        p = piece(a, far[k], 1 - y if other else y, 1)
        send((SEMS.sx + a, SEMS.wx + 8 * a + 4 * other + k), p, p, to_x)

    def w_zr(a, k):
        p = piece(a, far[k], y, 0)
        if k == 1:
            got((0, SEMS.wz + 4 * a + k), p)
        else:
            pl.when(outer)(lambda: got((0, SEMS.wz + 4 * a + k), p))
        send((SEMS.sy + a, SEMS.wy + 4 * a + k), p, p, to_y)
        w_share(a, k, 0)

    def w_on(a, k):
        p = piece(a, far[k], y, 0)

        @pl.when(inner)
        def _():
            got((0, SEMS.wz + 4 * a + k), p)
            send((SEMS.sz + a, SEMS.wz + 4 * a + k), p, p, at_z(mate))

    def w_yr(a, k):
        got((0, SEMS.wy + 4 * a + k), piece(a, far[k], 1 - y, 0))
        w_share(a, k, 1)

    def w_xr(a, k, other):
        yy = 1 - y if other else y
        got((0, SEMS.wx + 8 * a + 4 * other + k), piece(a, far[k], yy, 1, False))
        p = piece(a, far[k], yy, 2)
        send((SEMS.sc + a, SEMS.wc + 4 * a + (k if a == FC2 else 0)), p, p, to_c)

    def w_cr(a, k):
        n = w_in[a].shape[0]
        n = (n if k else n // 2) if a == FC2 else 7 * n // 2
        got((0, SEMS.wc + 4 * a + k), w[a].at[0:n])

    def w_left(a):
        n, m = w_in[a].shape
        half = n // 2
        q = half // 4 if a == FC2 else m // 4 if a == FC1 else m // 6

        def share(count, far_end):
            if a == FC2:
                return w[a].at[0 : count * (q if far_end else half - q)]
            return w[a].at[0 : count * half, 0 : q if far_end else m - q]

        pl.when(outer)(lambda: left(SEMS.sz + a, share(2, False)))
        pl.when(inner)(lambda: left(SEMS.sz + a, share(4, False)))
        left(SEMS.sy + a, share(4, False))
        left(SEMS.sx + a, share(7, True))
        left(SEMS.sc + a, w[a].at[0 : 7 * half])

    def unit_of(t):
        return far[t]

    def part_of(kind, t):
        return (9 + t, 8, 2 * t + 1, 2 * t)[kind]

    def x_first(q):
        return q in (0, 2, 4)

    def halves(q):
        return (min(q, 11), *((0, 2) if q < 11 else (q - 11, q - 10)))

    step, half, third = width // 16, width // 2, width // 4

    def c_sem(part):
        return 4 if part == 12 else part % 4

    def emit(kind, t, value):
        q = part_of(kind, t)
        slot = q % 4
        value = value.astype(BF16)
        for cc in range(2):
            for yy in range(2):
                if kind == FC2:
                    pieces = [(yy * half + cc * third, 0, third)]
                else:
                    pieces = [(((zz * 2 + yy) * 2 + cc) * step, zz * step, step) for zz in range(4)]
                for src, dst, size in pieces:
                    for xx in range(2):
                        v = value[src : src + size, xx * half : (xx + 1) * half]
                        r.U[slot, cc, yy, xx, dst : dst + size, :] = v
        for part in (q,) if q < 11 else (11, 12):
            _, lo, hi = halves(part)
            src, dst = r.U.at[slot, 1 - c, :, lo:hi], r.RC.at[slot, :, lo:hi]
            send((SEMS.c[0] + c_sem(part), SEMS.c[1] + c_sem(part)), src, dst, to_c)

    def g_1(part):
        q, lo, hi = halves(part)
        slot = q % 4
        got((0, SEMS.c[1] + c_sem(part)), r.RC.at[slot, :, lo:hi])

        def add(side):
            if x_first(q):

                @pl.loop(0, 2)
                def _(k):
                    r.U[slot, c, k, side] = r.U[slot, c, k, side] + r.RC[slot, k, side]

            else:

                @pl.loop(lo, hi)
                def _(k):
                    r.U[slot, c, side, k] = r.U[slot, c, side, k] + r.RC[slot, side, k]

        pair = (SEMS.r1[0] + c_sem(part), SEMS.r1[1] + part)
        if x_first(q):
            add(1 - x)
            send(pair, r.U.at[slot, c, :, 1 - x], r.R1.at[q], to_x)
            add(x)
        else:
            add(1 - y)
            send(pair, r.U.at[slot, c, 1 - y, lo:hi], r.R1.at[q, lo:hi], to_y)
            add(y)

    def z_slot(q):
        return unit_of(q // 2) if q < 8 else q - 4

    def steps(at, count=1):
        return pl.ds(pl.multiple_of(at * step, 16), count * step)

    def g_2(part):
        q, lo, hi = halves(part)
        got((0, SEMS.r1[1] + part), r.R1.at[q, lo:hi])
        left(SEMS.c[0] + c_sem(part), r.RC.at[q % 4, :, lo:hi])

        @pl.loop(lo, hi)
        def _(k):
            if x_first(q):
                r.R1[q, k] = r.R1[q, k] + r.U[q % 4, c, k, x]
            else:
                r.R1[q, k] = r.R1[q, k] + r.U[q % 4, c, y, k]

        left(SEMS.r1[0] + c_sem(part), r.R1.at[q, lo:hi])
        if q in (0, 2, 4, 6):
            side, dev = (1 - y, to_y) if x_first(q) else (1 - x, to_x)
            send((SEMS.r2[0], SEMS.r2[1] + q // 2), r.R1.at[q, side], r.R2.at[q // 2], dev)
            return
        if part > 10:
            for k in (2, 1, 3):
                src = r.R1.at[q, lo, steps(lax.rem(z + k, NZ))]
                send((SEMS.zd[0], SEMS.zd[1] + lo), src, r.ZD.at[lo, k - 1], to_z(k))
            return
        j = z_slot(q)
        pair = (SEMS.za[0], SEMS.za[1] + j)

        @pl.when(outer)
        def _():
            src = r.R1.at[q, lo:hi, steps(1 - upper, 3)]
            send(pair, src, r.ZA.at[j, lo:hi], at_z(mate))

        @pl.when(inner)
        def _():
            send(pair, r.R1.at[q, lo:hi, steps(mate)], r.ZB.at[j, lo:hi], at_z(mate))

    def g_7(part):
        q, lo, hi = halves(part)
        j = z_slot(q)

        @pl.when(inner)
        def _():
            got((0, SEMS.za[1] + j), r.ZA.at[j, lo:hi])
            across = steps(1 - upper, 2)
            own = r.R1[q, lo:hi, steps(2 - 2 * upper, 2)]
            r.ZA[j, lo:hi, across] = r.ZA[j, lo:hi, across] + own
            for i in range(2):
                src = r.ZA.at[j, lo:hi, steps(1 - upper + i)]
                pair = (SEMS.za[0], SEMS.zc + j)
                send(pair, src, r.ZC.at[j, lo:hi], at_z(2 - 2 * upper + i))

    def g_3(q):
        t = q // 2
        got((0, SEMS.r2[1] + t), r.R2.at[t])
        r.R2[t] = r.R2[t] + r.R1[q, y if x_first(q) else x]
        if t:
            u = unit_of(t)
            k = lax.rem(u + NZ - z, NZ)
            send(SEMS.zr2, r.R2.at[t], r.ZR2.at[k - 1], at_z(u))

    def g_4(kind, i):
        if kind == FC2:
            got(SEMS.zr2, r.ZR2)
            total = r.R2[0].astype(F32)
            for k in range(3):
                total = total + r.ZR2[k].astype(F32)
            g = g_held[FC2]
            g[c, x, 0] = total.astype(BF16)
            send((SEMS.gx_fc2, SEMS.gx[1]), g.at[c, x], g.at[c, x], to_x)
            return
        for part in {FC1: (1, 3, 5, 7), OUT: (8,), QKV: (9 + i,)}[kind]:
            q, lo, hi = halves(part)
            j = z_slot(q)
            if part > 10:
                got((0, SEMS.zd[1] + lo), r.ZD.at[lo])
                total = r.R1[q, lo, steps(z)].astype(F32)
                for k in range(3):
                    total = total + r.ZD[lo, k].astype(F32)
                r.XS[j, lo] = total.astype(BF16)
                continue
            got((0, SEMS.zc + j), r.ZC.at[j, lo:hi])

            def put(near, at):
                total = r.R1[q, lo:hi, steps(z)].astype(F32) + near[j, lo:hi, at].astype(F32)
                r.XS[j, lo:hi] = (total + r.ZC[j, lo:hi].astype(F32)).astype(BF16)

            @pl.when(outer)
            def _():
                got((0, SEMS.za[1] + j), r.ZB.at[j, lo:hi])
                put(r.ZB, slice(None))

            @pl.when(inner)
            def _():
                put(r.ZA, steps(2 * upper))

        sem, at = x_span(kind, i)
        send((SEMS.gx[0], sem), r.XS.at[at], r.XR.at[at], to_x)

    def x_span(kind, i):
        if kind == FC1:
            return SEMS.gx[1] + 1, (slice(0, 4),)
        q, lo, hi = halves(8 if kind == OUT else 9 + i)
        return SEMS.gx[1] + (2 if kind == OUT else 3 + i), (q - 4, slice(lo, hi))

    def g_5(kind, i):
        g = g_held[kind]
        if kind == FC2:
            got(SEMS.gx, g.at[c, 1 - x])
        else:
            sem, at = x_span(kind, i)
            got((0, sem), r.XR.at[at])
            units = range(4) if kind == FC1 else (at[0],)
            for n, j in enumerate(units):
                sides = (0, 1) if kind == FC1 else range(at[1].start, at[1].stop)
                for xx in sides:
                    g[c, xx, min(i, 2) + n] = r.XS[j, xx] + r.XR[j, xx]
        if kind != QKV or i == 3:
            mine = g_outs[kind].at[c]
            send((SEMS.gc[0] + kind, SEMS.gc[1] + kind), g.at[c], mine, to_c)
            local(SEMS.l_g + kind, g.at[c], mine)

    def v_part(p):
        return slice(p // 2 * 8, p // 2 * 8 + 8), slice(p % 2 * half, (p % 2 + 1) * half)

    def v_1():
        for p in range(4):
            r.gv0[p] = r.gvec[v_part(p)]
        r.gv1[s] = r.gv0[s]
        for k in (2, 1, 3):
            send(SEMS.vs, r.gv0.at[lax.rem(s + k, 4)], r.gv1.at[s], to_s(k))

    def v_2():
        got(SEMS.vs, r.gv1.at[0:3])
        r.gv2[0] = r.gv1[0] + r.gv1[1] + r.gv1[2] + r.gv1[3]
        send(SEMS.vy, r.gv2.at[0], r.gv2.at[1], to_y)

    def v_3():
        got(SEMS.vy, r.gv2.at[1])
        r.gv3[z] = r.gv2[0] + r.gv2[1]
        for k in (2, 1, 3):
            send(SEMS.vz, r.gv3.at[z], r.gv3.at[z], to_z(k))

    def v_4():
        got(SEMS.vz, r.gv3.at[0:3])
        r.gv4[s] = (r.gv3[0] + r.gv3[1]) + (r.gv3[2] + r.gv3[3])
        for k in (2, 1, 3):
            send(SEMS.vb, r.gv4.at[s], r.gv4.at[s], to_s(k))

    def v_5():
        got(SEMS.vb, r.gv4.at[0:3])
        n = width // (2 * NZ)
        row = lax.broadcasted_iota(jnp.int32, (half, 128), 0)
        lane = lax.broadcasted_iota(jnp.int32, (half, 128), 1)
        for top in range(2):
            total = jnp.zeros((8, 128), F32)
            for side in range(2):
                pick = jnp.where((row + side * half == lane + d * n) & (lane < n), 1.0, 0.0)
                part = lax.dot(
                    r.gv4[2 * top + side],
                    pick.astype(F32),
                    precision=lax.Precision.HIGHEST,
                    preferred_element_type=F32,
                )
                total = total + part
            gvec_out[top * 8 : top * 8 + 8, :] = total

    def vectors_in():
        total = jnp.zeros((16, width), F32)
        n = width // (2 * NZ)
        lane = lax.broadcasted_iota(jnp.int32, (128, width), 0)
        col = lax.broadcasted_iota(jnp.int32, (128, width), 1)
        for k in range(2 * NZ):
            pick = jnp.where((col == lane + k * n) & (lane < n), 1.0, 0.0).astype(BF16)
            total = total + dot(r.vecs[k % 2, k // 2].astype(BF16), pick)
        r.vec[...] = total

    def vec_z():
        got(SEMS.vec_z, r.vecs.at[y, 0:3])
        send(SEMS.vec_y, r.vecs.at[y], r.vecs.at[y], to_y)

    def vec_y():
        got(SEMS.vec_y, r.vecs.at[1 - y])
        vectors_in()

    three = slice(0, 3 * slots)

    def tokens_in():
        got(SEMS.mask, r.mr.at[0:3])
        for b in range(4):
            column = r.mr[b].T[0:slots]
            for i in range(images):
                wide = jnp.broadcast_to(column[:, i : i + 1], (slots, 128)).astype(BF16)
                r.mask[i, b * slots : (b + 1) * slots, :] = wide
        got(SEMS.tok, r.tok.at[:, three])
        settled(SEMS.l_tok, r.tok.at[:, 0:slots])

    def cot_out(i):
        scatter(SEMS.cot, SEMS.l_cot, cotangent, r.cot, i, i + 1)

    def cot_in():
        got(SEMS.cot, r.cot.at[:, three])
        settled(SEMS.l_cot, r.cot.at[:, 0:slots])

    def out_back(i):
        give_back(SEMS.out, SEMS.l_out, r.out, o_out, i)

    def ingrad_back(i):
        give_back(SEMS.ingrad, SEMS.l_ingrad, r.ingrad, o_ingrad, i)

    def own_in(a):
        settled(SEMS.l_w + a, w[a].at[0 : w_in[a].shape[0]])

    own = r.vecs.at[y, z]
    own[...] = jnp.zeros((16, 128), F32)
    own[0 : in_vec.shape[0], 0 : in_vec.shape[1]] = in_vec[...].astype(F32)
    for k in (1, 2, 3):
        send(SEMS.vec_z, own, own, to_z(k))
    marks = jnp.where(masks[...] == 1, 1.0, 0.0).astype(F32)
    r.mk[...] = jnp.zeros(r.mk.shape, F32)
    for t in range(4):
        r.mk[t, 0:images, 0:slots] = marks[t * images : (t + 1) * images]
    r.mr[s] = r.mk[s]
    for k in (2, 1, 3):
        send(SEMS.mask, r.mk.at[lax.rem(s + k, 4)], r.mr.at[s], to_s(k))
    scatter(SEMS.tok, SEMS.l_tok, tokens, r.tok)
    w_y0(QKV)
    w_z(QKV)
    for a in (QKV, OUT, FC1, FC2):
        w_own(a)
    piece_done = layer(dims, r, emit, unit_of)

    def go(k):
        next(piece_done)

    table = (go, w_zr, w_yr, w_xr, w_cr, w_z, w_y0, cot_out, cot_in, tokens_in, vec_z, vec_y)
    table += (g_1, g_2, g_3, g_4, g_5, None, out_back, ingrad_back)
    table += (v_1, v_2, v_3, v_4, v_5, own_in, g_7, w_on)
    for op, *at in SCHEDULE:
        table[op](*at)
    for _ in piece_done:
        pass
    bands = (SEMS.out, SEMS.l_out, o_out), (SEMS.ingrad, SEMS.l_ingrad, o_ingrad)
    for pair, sem, dst in bands:
        got(pair, dst.at[0 : 3 * images])
        settled(sem, dst.at[0:images])
    sent = [(SEMS.tok, r.tok), (SEMS.cot, r.cot)]
    sent = [(pair, ref.at[:, three]) for pair, ref in sent] + [(SEMS.mask, r.mk.at[0:3])]
    sent += [(pair, dst.at[0 : 3 * images]) for pair, _, dst in bands]
    sent += [(SEMS.vec_z, r.vecs.at[0, 0:3]), (SEMS.vec_y, r.vecs.at[0])]
    sent += [(SEMS.r2, r.R2), (SEMS.za, r.ZA.at[0:7]), (SEMS.zd, r.ZD), (SEMS.zr2, r.ZR2), (SEMS.gx, r.XS)]
    sent += [((SEMS.gx_fc2,), g_held[FC2].at[c, x])]
    sent += [((SEMS.gc[0] + a,), g_held[a].at[c]) for a in range(4)]
    sent += [(SEMS.vs, r.gv0.at[0:3]), (SEMS.vy, r.gv2.at[0])]
    sent += [(SEMS.vz, r.gv3.at[0:3]), (SEMS.vb, r.gv4.at[0:3])]
    for pair, src in sent:
        left(pair[0], src)
    for a in range(4):
        w_left(a)
        settled(SEMS.l_g + a, g_outs[a].at[c])
        got((0, SEMS.gc[1] + a), g_outs[a].at[1 - c])


def linked_layer(tokens, masks, cotangent, weights):
    count, slots, width = tokens.shape
    images, seq_len = count // 4, slots * 4
    dims = (images, used_rows(seq_len), width, weights[2].shape[1])
    shape = jax.ShapeDtypeStruct
    low = lambda *s: pltpu.VMEM(s, BF16)
    full = lambda *s: pltpu.VMEM(s, F32)
    sems = lambda n: pltpu.SemaphoreType.DMA((n,))
    step, half, third = width // 16, width // 2, width // 4
    hbm = pl.BlockSpec(memory_space=pl.ANY)
    vmem = pl.BlockSpec(memory_space=pltpu.VMEM)
    sums = [(2, 2, 3, step, half), (2, 2, 1, step, half), (2, 2, 4, step, half)]
    sums += [(2, 2, 1, third, half)]
    held = [low(w.shape[0] * 2 * NZ, w.shape[1]) for w in weights[:4]]
    held += [low(images, seq_len, w) for w in (width, 128, width)]
    held += [full(16, width)] + [low(images, seq_len, width)] * 2 + [full(16, width)]
    held += [low(*v) for v in sums]
    more = More(
        vecs=full(2, NZ, 16, 128),
        U=low(4, 2, 2, 2, third, half),
        RC=low(4, 2, 2, third, half),
        R1=low(PARTS, 2, third, half),
        R2=low(4, third, half),
        ZA=low(8, 2, 3 * step, half),
        ZB=low(8, 2, step, half),
        ZC=low(8, 2, step, half),
        ZD=low(2, 3, step, half),
        ZR2=low(3, third, half),
        XS=low(8, 2, step, half),
        XR=low(8, 2, step, half),
        gv0=full(4, 8, half),
        gv1=full(4, 8, half),
        gv2=full(2, 8, half),
        gv3=full(4, 8, half),
        gv4=full(4, 8, half),
        ss=sems(SEMS.sends),
        rs=sems(SEMS.recvs),
        ls=sems(SEMS.locals),
        mk=full(4, 8, 128),
        mr=full(4, 8, 128),
    )
    return pl.pallas_call(
        functools.partial(linked_kernel, dims),
        out_shape=(
            shape(tokens.shape, BF16),
            shape(tokens.shape, BF16),
            *(shape(v, BF16) for v in sums),
            shape((16, 128), F32),
        ),
        in_specs=[hbm, vmem] + [hbm] * 5 + [vmem],
        out_specs=[hbm] * 6 + [vmem],
        scratch_shapes=held + list(scratch(dims)) + list(more),
        compiler_params=pltpu.CompilerParams(
            collective_id=0,
            has_side_effects=True,
            vmem_limit_bytes=63 << 20,
        ),
        name="layer",
    )(tokens, masks, cotangent, *weights[:4], weights[4].T)


def sgd_step(gradient, master, moment, teacher, step_rate, decay_rate):
    pulled = gradient + decay_rate * master
    moment_new = momentum_rate * moment + pulled
    weight_new = master - step_rate * (pulled + momentum_rate * moment_new)
    teacher_new = teacher_rate * teacher + (1.0 - teacher_rate) * weight_new
    return (weight_new, moment_new, teacher_new, weight_new.astype(BF16))


def on_device(tokens, masks, cotangent, *rest):
    weights, masters, moments, teachers = rest[:5], rest[5:10], rest[10:15], rest[15:20]
    images, slots, width = tokens.shape
    step = (weights, masters, moments, teachers)
    if (lax.axis_size("dp"), lax.axis_size("seq")) == (2 * NZ, 4):
        out, ingrad, *sums, gvec = linked_layer(tokens, masks, cotangent, weights)
        return finish(out, ingrad, sums, gvec, *step)
    wide = jnp.broadcast_to((masks == 1).astype(BF16)[..., None], (images, slots, 128))
    full = [lax.all_gather(w, "dp", axis=0, tiled=True) for w in weights]
    vec = jnp.zeros((16, width), F32).at[: full[4].shape[1]].set(full[4].astype(F32).T)
    tok, mask, cot = (
        lax.all_to_all(v, "seq", 0, 1, tiled=True) for v in (tokens, wide, cotangent)
    )
    out, ingrad, *grads, gvec = plain_layer(tok, mask, cot, *full[:4], vec)
    out, ingrad = (lax.all_to_all(v, "seq", 1, 0, tiled=True) for v in (out, ingrad))
    sums = [lax.psum_scatter(g, "dp", scatter_dimension=0, tiled=True) for g in grads]
    sums = [lax.psum(g, "seq") for g in sums]
    gvec = lax.psum(gvec, ("dp", "seq"))
    part = width // lax.axis_size("dp")
    own = lax.dynamic_slice(gvec, (0, lax.axis_index("dp") * part), (16, part))
    return finish(out, ingrad, sums, own, *step)


def whole(kind, ref):
    if len(ref.shape) == 2:
        return ref[...].astype(F32)
    units, half = ref.shape[2], ref.shape[4]
    if kind != QKV:
        pieces = [ref[0, xx, u] for u in range(units) for xx in range(2)]
    else:
        at, cut = range(units), half * 2 // 3
        pieces = [ref[0, 0, u, :, 0:cut] for u in at]
        for u in at:
            pieces += [ref[0, 0, u, :, cut:half], ref[0, 1, u, :, 0 : half - cut]]
        pieces += [ref[0, 1, u, :, half - cut : half] for u in at]
    return jnp.concatenate(pieces, 1).astype(F32)


def update_kernel(steps, *refs):
    ins, outs = refs[:22], refs[22:]
    for k in range(5):
        n, m = ins[5 + k].shape
        g = whole(k, ins[k])[:n, :m]
        got = sgd_step(g, *(ins[5 * j + k][...] for j in (1, 2, 3)), *steps[k])
        for ref, v in zip((outs[k], *(outs[5 * j + k] for j in (1, 2, 3, 4))), (g, *got)):
            ref[...] = v
    outs[25][...] = ins[20][...]
    outs[26][...] = ins[21][...].astype(F32)


def finish(out, ingrad, sums, own, weights, masters, moments, teachers):
    images, slots, width = out.shape
    part = width // lax.axis_size("dp")
    image_total = images * lax.axis_size("dp")
    big = (matrix_rate / math.sqrt(image_total), matrix_decay)
    small = (vector_rate / math.sqrt(image_total), 0.0)
    steps = (big, big, big, big, small)
    count = 2
    if part % (16 * count) or images % count:
        sums = [g.astype(F32) for g in (*sums, own[: weights[4].shape[1]].T)]
        old = zip(sums, masters, moments, teachers, steps)
        ups = [sgd_step(*v, *rates) for *v, rates in old]
        return (out, ingrad.astype(F32), *sums, *(u[j] for j in range(4) for u in ups))

    def spec(a):
        if a.ndim == 5:
            block = (1, 2, a.shape[2], a.shape[3] * 2 // count, a.shape[4])
            return pl.BlockSpec(block, lambda i: (i // (count // 2), 0, 0, i % (count // 2), 0))
        if a.ndim == 2 and a.shape[0] < part:
            return pl.BlockSpec(a.shape, lambda i: (0, 0))
        rest = (0,) * (a.ndim - 1)
        return pl.BlockSpec((a.shape[0] // count, *a.shape[1:]), lambda i: (i, *rest))

    flip = lambda group: (*group[:4], group[4].T)
    args = [*sums, own, *flip(masters), *flip(moments), *flip(teachers), out, ingrad]
    shape = jax.ShapeDtypeStruct
    outs = [shape(m.shape, F32) for _ in range(4) for m in flip(masters)]
    outs += [shape(m.shape, BF16) for m in flip(masters)]
    outs += [shape(out.shape, BF16), shape(out.shape, F32)]
    res = pl.pallas_call(
        functools.partial(update_kernel, steps),
        grid=(count,),
        out_shape=outs,
        in_specs=[spec(a) for a in args],
        out_specs=[spec(a) for a in outs],
        compiler_params=pltpu.CompilerParams(vmem_limit_bytes=60 << 20),
        name="update",
    )(*args)
    res = [v.T if k % 5 == 4 and k < 25 else v for k, v in enumerate(res)]
    return (res[25], res[26], *res[:25])


def solution(mesh):
    band = P("dp", "seq", None)
    rows = P("dp", None)
    return jax.shard_map(
        on_device,
        mesh=mesh,
        in_specs=(band, P("dp", "seq"), band) + (rows,) * 20,
        out_specs=(band, band) + (rows,) * 25,
        check_vma=False,
    )
```
